32 devices in a mesh: seq: 4 (over y, x), dp: 8 (over z, core).
Axes of the slice: x: 2, y: 2, z: 4, core: 2. Of those that a mesh axis runs over, the one named last changes fastest.
Arguments:
- tokens: bfloat16 [16, 1536, 2048], P('dp', 'seq'), may hold values from -6 to 6
- cotangent: bfloat16 [16, 1536, 2048], P('dp', 'seq'), may hold values from -6 to 6
- weight: bfloat16 [2048, 6144], P('dp'), may hold values from -0.125 to 0.125
- forget_peep: float32 [2048], replicated, may hold values from -3 to 3
- reset_peep: float32 [2048], replicated, may hold values from -4 to 4
- forget_bias: float32 [2048], replicated, may hold values from 0 to 8.5
- reset_bias: float32 [2048], replicated, may hold values from -4 to 4
- norm_gain: float32 [2048], replicated, may hold values from 0.5 to 1.5
- norm_bias: float32 [2048], replicated, may hold values from -3 to 3
- lengths: int32 [16], P('dp'), may hold values from 384 to 1536, as said below
Outputs:
- activations: float32 [16, 1536, 2048], P('dp', 'seq')
- input_grad: float32 [16, 1536, 2048], P('dp', 'seq')
- weight_grad: float32 [2048, 6144], P('dp', 'seq')
- forget_peep_grad: float32 [2048], replicated
- reset_peep_grad: float32 [2048], replicated
- forget_bias_grad: float32 [2048], replicated
- reset_bias_grad: float32 [2048], replicated
- norm_gain_grad: float32 [2048], replicated
- norm_bias_grad: float32 [2048], replicated
The draws below stay inside these ranges and needn't reach their ends.
Inputs may be any that keep to these rules, and one draw needn't show every extreme that they name: `lengths`: each micro-batch of 2 sequences holds one of full length 1536.
All inputs are finite; a program needn't handle non-finite values.
Results may differ from the reference program's by a relative error of at most 0.004.
Values may be sent and summed in bfloat16 or wider, within the bound.
No kernel may reach another device: no remote copies, remote signals or barrier semaphores. Data moves between devices by JAX's collectives and lax.ppermute only.
A program may use at most 256 MiB of HBM per device.

```python
import jax
import jax.numpy as jnp
from jax import lax

D = 2048
SEQS_DEV = 2
SEQ = 1536
SEQS = 16


def draw_forget_bias(key, part):
    key = jax.random.fold_in(key, 5)
    return jax.random.uniform(key, (D,), jnp.float32, 0.0, 8.0)


def draw_lengths(key, part):
    key = jax.random.fold_in(key, 11)
    first, second = jax.random.split(key)
    groups = SEQS // SEQS_DEV
    base = jax.random.randint(first, (groups, SEQS_DEV), SEQ // 4, SEQ + 1)
    chosen = jax.random.randint(second, (groups, 1), 0, SEQS_DEV)
    slots = jnp.arange(SEQS_DEV, dtype=jnp.int32)[None, :]
    filled = jnp.where(slots == chosen, SEQ, base)
    return filled.reshape(SEQS).astype(jnp.int32)


def steps_of(own_key, extent, pieces, low, largest):
    loudness = 1.0
    for position, parts in pieces:
        draws = jax.random.uniform(jax.random.fold_in(jax.random.fold_in(own_key, 6), position), (parts,), jnp.float32, low / len(pieces), largest / len(pieces))
        loudness = loudness * jnp.repeat(jnp.exp(draws), extent[position] // parts).reshape((-1,) + (1,) * (len(extent) - 1 - position))
    return loudness


def centred(own_key, extent, spread, most, cuts=(), kind=jnp.bfloat16):
    level = steps_of(own_key, extent, cuts, -0.22, 0.18) if cuts else 1.0
    array = jax.random.normal(own_key, extent, jnp.float32) * spread * level
    return jnp.minimum(jnp.maximum(array, -most), most).astype(kind)


def setup_inputs(seed: int = 0) -> dict:
    key_list = jax.random.split(jax.random.key(seed), 11)
    tokens = centred(key_list[0], (SEQS, SEQ, D), 1.0, 6.0, ((0, 8), (1, 4)))
    cotangent = centred(key_list[1], (SEQS, SEQ, D), 1.0, 6.0, ((0, 8), (1, 4)))
    weight = centred(key_list[2], (D, 3 * D), D ** -0.5, 0.125, ((0, 8),))
    forget_peep = centred(key_list[3], (D,), 0.5, 3.0, (), jnp.float32)
    reset_peep = centred(key_list[4], (D,), 1.0, 4.0, (), jnp.float32)
    forget_bias = draw_forget_bias(jax.random.fold_in(key_list[10], 71), 0)
    reset_bias = centred(key_list[6], (D,), 1.0, 4.0, (), jnp.float32)
    norm_gain = jnp.clip(1.0 + 0.1 * jax.random.normal(key_list[7], (D,), jnp.float32), 0.5, 1.5)
    norm_bias = centred(key_list[8], (D,), 0.5, 3.0, (), jnp.float32)
    lengths = draw_lengths(jax.random.fold_in(key_list[10], 71), 0)
    return {"tokens": tokens, "cotangent": cotangent, "weight": weight, "forget_peep": forget_peep, "reset_peep": reset_peep, "forget_bias": forget_bias, "reset_bias": reset_bias, "norm_gain": norm_gain, "norm_bias": norm_bias, "lengths": lengths}


@jax.custom_vjp
def low(v):
    return lax.optimization_barrier(v.astype(jnp.bfloat16)).astype(jnp.float32)

@jax.custom_vjp
def low_back(v):
    return v

def low_keep(v):
    return (low(v), None)

def low_pass(kept, grad):
    return (grad,)

def back_keep(v):
    return (v, None)

def back_low(kept, grad):
    return (low(grad),)
low.defvjp(low_keep, low_pass)
low_back.defvjp(back_keep, back_low)
EPS = 1e-05

def group_forward(inputs, live, weight, forget_peep, reset_peep, forget_bias, reset_bias, norm_gain, norm_bias):
    mean = lax.optimization_barrier(jnp.mean(inputs, axis=-1, keepdims=True))
    centered = inputs - mean
    var = lax.optimization_barrier(jnp.mean(centered * centered, axis=-1, keepdims=True))
    normed = centered * lax.rsqrt(var + EPS)
    unit = normed * norm_gain + norm_bias
    proj = jnp.einsum('std,de->ste', low(unit), weight, precision=lax.Precision.HIGHEST)
    proj = low_back(proj)
    cand, fpre, rpre = jnp.split(proj, 3, axis=-1)
    forget = jax.nn.sigmoid(fpre + forget_peep * unit + forget_bias)
    mask = live[..., None]
    decay = jnp.where(mask, forget, 1.0)
    inject = jnp.where(mask, (1.0 - forget) * cand, 0.0)

    def advance(carry, item):
        rate, term = item
        after = rate * carry + term
        return (after, (carry, after))
    start = jnp.zeros((inputs.shape[0], inputs.shape[2]), jnp.float32)
    unused, (before, state) = lax.scan(advance, start, (jnp.swapaxes(decay, 0, 1), jnp.swapaxes(inject, 0, 1)))
    before = jnp.swapaxes(before, 0, 1)
    state = jnp.swapaxes(state, 0, 1)
    reset = jax.nn.sigmoid(rpre + reset_peep * before + reset_bias)
    highway = reset * state + (1.0 - reset) * unit
    return inputs + jnp.where(mask, highway, 0.0)

def reference(tokens, cotangent, weight, forget_peep, reset_peep, forget_bias, reset_bias, norm_gain, norm_bias, lengths):
    groups = SEQS // SEQS_DEV
    inputs = tokens.astype(jnp.float32).reshape(groups, SEQS_DEV, SEQ, D)
    places = jnp.arange(SEQ, dtype=jnp.int32)
    live = (places[None, :] < lengths[:, None]).reshape(groups, SEQS_DEV, SEQ)
    counts = lax.optimization_barrier(jnp.sum(lengths.reshape(groups, SEQS_DEV), axis=1)).astype(jnp.float32)
    scale = SEQS_DEV * SEQ / counts
    grad_out = jnp.where(live[..., None], cotangent.astype(jnp.float32).reshape(groups, SEQS_DEV, SEQ, D), 0.0)
    grad_out = grad_out * scale[:, None, None, None]

    def whole(values, weight_f, fpeep, rpeep, fbias, rbias, gain, nbias):
        block = jax.checkpoint(lambda item_x, item_live: group_forward(item_x, item_live, weight_f, fpeep, rpeep, fbias, rbias, gain, nbias))
        return lax.map(lambda item: block(item[0], item[1]), (values, live))
    result, pull = jax.vjp(whole, inputs, weight.astype(jnp.float32), forget_peep, reset_peep, forget_bias, reset_bias, norm_gain, norm_bias)
    grads = pull(grad_out)
    return (result.reshape(SEQS, SEQ, D), grads[0].reshape(SEQS, SEQ, D), grads[1], grads[2], grads[3], grads[4], grads[5], grads[6], grads[7])
```

```python
import functools

import jax
import jax.numpy as jnp
from jax import lax
from jax.experimental import pallas as pl
from jax.experimental.pallas import tpu as pltpu
from jax.sharding import PartitionSpec as P

EPS = 1e-05
F32 = jnp.float32
BF = jnp.bfloat16
STEPS = 16
BLK = 128
GATES = 3
QUARTERS = 4


def params(mib, dims=1):
    return pltpu.CompilerParams(
        vmem_limit_bytes=mib * 1024 * 1024, dimension_semantics=("arbitrary",) * dims
    )


def cost(flops, bytes_accessed, transcendentals=0):
    return pl.CostEstimate(
        flops=int(flops), bytes_accessed=int(bytes_accessed), transcendentals=int(transcendentals)
    )


def sds(shape, dtype):
    return jax.ShapeDtypeStruct(shape, dtype)


def sigmoid(v):
    return jax.nn.sigmoid(v)


def split_kernel(ids, w, mine, theirs):
    c = ids[2]
    for s in range(4):
        a, mp = divmod(s, 2)
        for g in range(GATES):
            for mm in range(2):
                dst = s * 768 + g * 256 + mm * BLK
                base = g * 2048 + (2 * mp + mm) * 512 + a * BLK
                here = pl.multiple_of(base + c * 256, BLK)
                there = pl.multiple_of(base + (1 - c) * 256, BLK)
                mine[:, dst : dst + BLK] = w[:, pl.ds(here, BLK)]
                theirs[:, dst : dst + BLK] = w[:, pl.ds(there, BLK)]


def split_weight(ids, weight):
    rows, cols = weight.shape
    tile = rows // 2
    out = sds((rows, cols // 2), BF)
    spec = pl.BlockSpec((tile, cols // 2), lambda i, ids: (i, 0))
    return pl.pallas_call(
        split_kernel,
        grid_spec=pltpu.PrefetchScalarGridSpec(
            num_scalar_prefetch=1,
            grid=(2,),
            in_specs=[pl.BlockSpec((tile, cols), lambda i, ids: (i, 0))],
            out_specs=[spec, spec],
        ),
        out_shape=[out, out],
        compiler_params=params(24),
        cost_estimate=cost(0, rows * cols * 4),
        name="split_weight",
    )(ids, weight)


def norm_of(x):
    mean = jnp.mean(x, axis=-1, keepdims=True)
    centered = x - mean
    var = jnp.mean(centered * centered, axis=-1, keepdims=True)
    rstd = lax.rsqrt(var + EPS)
    return centered * rstd, rstd


def norm_kernel(ids, own, other, gain, bias, ub, ubt, u32, scr):
    c = ids[2]
    seqs, parts = own.shape[0], own.shape[1]
    for k, ref in enumerate((own, other)):
        for s in range(seqs):
            for h in range(parts):
                x = ref[s, h].astype(F32)
                normed, _ = norm_of(x)
                stream = (k * seqs + s) * parts + h
                unit = normed * gain[...] + bias[...]
                for j in range(scr.shape[0]):
                    scr[j, pl.ds(stream, STEPS, stride=16), :] = unit[:, j * BLK : (j + 1) * BLK]
    for j in range(scr.shape[0]):
        low = scr[j].astype(BF)
        ub[:, j * BLK : (j + 1) * BLK] = low
        ubt[j * BLK : (j + 1) * BLK, :] = low.T
    for a in range(2):
        for m in range(QUARTERS):
            dst = (a * QUARTERS + m) * BLK
            u32[:, dst : dst + BLK] = scr[m * 4 + a + 2 * c]


def norm_tokens(ids, own, other, gain, bias):
    seqs, parts, steps, width = own.shape
    rows = 2 * seqs * parts * steps
    tiles = steps // STEPS
    nat = pl.BlockSpec((seqs, parts, STEPS, width), lambda i, ids: (0, 0, i, 0))
    vec = pl.BlockSpec((1, width), lambda i, ids: (0, 0))
    return pl.pallas_call(
        norm_kernel,
        grid_spec=pltpu.PrefetchScalarGridSpec(
            num_scalar_prefetch=1,
            grid=(tiles,),
            in_specs=[nat, nat, vec, vec],
            out_specs=[
                pl.BlockSpec((256, width), lambda i, ids: (i, 0)),
                pl.BlockSpec((width, 256), lambda i, ids: (0, i)),
                pl.BlockSpec((256, width // 2), lambda i, ids: (i, 0)),
            ],
            scratch_shapes=[pltpu.VMEM((width // BLK, 256, BLK), F32)],
        ),
        out_shape=[
            sds((rows, width), BF),
            sds((width, rows), BF),
            sds((rows, width // 2), F32),
        ],
        compiler_params=params(32),
        cost_estimate=cost(rows * width * 10, rows * width * 10),
        name="norm_tokens",
    )(ids, own, other, gain, bias)


def live_rows(lim, tile):
    step = lax.broadcasted_iota(jnp.int32, lim.shape, 0) // 16 + tile * STEPS
    live = step < lim[...]
    return jnp.concatenate([live, live], axis=1)


def proj_kernel(
    s, nz, ids, ub, u32, mine, recv, rel, gx, gy, dx, dy, lim, vf, bfor,
    cand, decay, rpre, wout, plout, summ, prod, loc, sems,
):
    i = pl.program_id(0)
    tiles = pl.num_programs(0)
    width = wout.shape[0]
    zb = width // nz
    zb2, qb = zb // 2, zb // 4

    @pl.when(i == 0)
    def _():
        q, z, c = ids[0], ids[1], ids[2]
        copies = []

        def put(src, row, lo=0, hi=768):
            dst = wout.at[pl.ds(pl.multiple_of(row, qb), src.shape[0]), lo:hi]
            copy = pltpu.make_async_copy(src, dst, sems.at[len(copies)])
            copy.start()
            copies.append(copy)

        put(mine.at[:, s * 768 : (s + 1) * 768], z * zb + c * zb2)
        put(recv.at[:, s * 768 : (s + 1) * 768], z * zb + (1 - c) * zb2)
        for r in range(1, nz):
            base = lax.rem(z + r, nz) * zb
            lo, hi = (r - 1) * qb, r * qb
            put(rel.at[lo:hi, :], base + q * qb)
            put(gx.at[lo:hi, :], base + (q ^ 1) * qb)
            put(gy.at[lo:hi, :], base + (q ^ 2) * qb)
            put(dx.at[lo:hi, :], base + (q ^ 3) * qb, 0, 384)
            put(dy.at[lo:hi, :], base + (q ^ 3) * qb, 384, 768)
        for copy in copies:
            copy.wait()
        prod[...] = jnp.ones_like(prod)
        loc[...] = jnp.zeros_like(loc)

    zz = jnp.dot(ub[...], wout[...], preferred_element_type=F32)
    cd = zz[:, :256]
    gate = sigmoid(zz[:, 256:512] + vf[...] * u32[...] + bfor[...])
    dec = jnp.where(live_rows(lim, i), gate, 1.0)
    cand[...] = cd
    decay[...] = dec
    rpre[...] = zz[:, 512:]
    inj = (1.0 - dec) * cd
    pr, lc = prod[...], loc[...]
    for t in range(STEPS):
        d = dec[t * 16 : (t + 1) * 16]
        lc = d * lc + inj[t * 16 : (t + 1) * 16]
        pr = d * pr
    prod[...] = pr
    loc[...] = lc

    @pl.when(i == tiles - 1)
    def _():
        plout[0:16, :] = pr
        plout[16:32, :] = lc
        parts = 4
        for ks in range(4):
            tp = pr[ks * parts : ks * parts + 1]
            tl = lc[ks * parts : ks * parts + 1]
            for h in range(1, parts):
                n = ks * parts + h
                tl = pr[n : n + 1] * tl + lc[n : n + 1]
                tp = pr[n : n + 1] * tp
            summ[ks : ks + 1, :] = tp
            summ[4 + ks : 5 + ks, :] = tl


def project(s, nz, ids, ub, u32, mine, recv, pieces, lim, vf, bfor):
    rows, width = ub.shape
    tiles = rows // 256
    rel, gx, gy, dx, dy = pieces
    anyspec = pl.BlockSpec(memory_space=pl.ANY)
    rowblk = pl.BlockSpec((256, 256), lambda i, ids: (i, 0))
    chan = pl.BlockSpec((1, 256), lambda i, ids: (0, s))
    return pl.pallas_call(
        functools.partial(proj_kernel, s, nz),
        grid_spec=pltpu.PrefetchScalarGridSpec(
            num_scalar_prefetch=1,
            grid=(tiles,),
            in_specs=[
                pl.BlockSpec((256, width), lambda i, ids: (i, 0)),
                pl.BlockSpec((256, 256), lambda i, ids: (i, s)),
            ]
            + [anyspec] * 7
            + [pl.BlockSpec((256, 128), lambda i, ids: (0, 0)), chan, chan],
            out_specs=[
                rowblk,
                rowblk,
                rowblk,
                pl.BlockSpec((width, 768), lambda i, ids: (0, 0)),
                pl.BlockSpec((32, 256), lambda i, ids: (0, 0)),
                pl.BlockSpec((8, 256), lambda i, ids: (0, 0)),
            ],
            scratch_shapes=[
                pltpu.VMEM((16, 256), F32),
                pltpu.VMEM((16, 256), F32),
                pltpu.SemaphoreType.DMA((2 + 5 * (nz - 1),)),
            ],
        ),
        out_shape=[
            sds((rows, 256), F32),
            sds((rows, 256), F32),
            sds((rows, 256), F32),
            sds((width, 768), BF),
            sds((32, 256), F32),
            sds((8, 256), F32),
        ],
        compiler_params=params(32),
        cost_estimate=cost(2 * rows * width * 768, rows * width * 2 + width * 768 * 4 + rows * 4096),
        name=f"project_{s}",
    )(ids, ub, u32, mine, recv, rel, gx, gy, dx, dy, lim, vf, bfor)


def state_kernel(
    s, first, n_in, ids, cand, decay, rpre, u32, own0, own1, oth0, oth1, lim, scl, vr, br, plin,
    *rest,
):
    carries = rest[:n_in]
    rest = rest[n_in:]
    if not first:
        rest = rest[2:]
    (hown, hoth, dstate, src, bc, du0, dz3, lbs, summ, acc, st, pp, lb, ac, scr) = rest
    i = pl.program_id(0)
    tiles = pl.num_programs(0)
    parts = 4

    @pl.when(i == 0)
    def _():
        carry = carries[-1][4:8, :]
        for ref in carries[-2::-1]:
            carry = ref[4:8, :] + ref[0:4, :] * carry
        for ks in range(4):
            cc = carry[ks : ks + 1]
            for h in range(parts):
                n = ks * parts + h
                st[n : n + 1, :] = cc
                cc = plin[n : n + 1, :] * cc + plin[16 + n : 17 + n, :]
        pp[...] = jnp.ones_like(pp)
        lb[...] = jnp.zeros_like(lb)
        ac[...] = jnp.zeros_like(ac)

    for k, halves in enumerate(((own0, own1), (oth0, oth1))):
        for b, ref in enumerate(halves):
            for sq in range(ref.shape[0]):
                for h in range(parts):
                    stream = (k * ref.shape[0] + sq) * parts + h
                    scr[b, pl.ds(stream, STEPS, stride=16), :] = ref[sq, h].astype(F32)
    live = live_rows(lim, i)
    sc = scl[...]
    gy = jnp.where(live, jnp.concatenate([scr[0] * sc, scr[1] * sc], axis=1), 0.0)
    dec = decay[...]
    cd = cand[...]
    inj = (1.0 - dec) * cd
    cur = st[...]
    befores, states = [], []
    for t in range(STEPS):
        befores.append(cur)
        cur = dec[t * 16 : (t + 1) * 16] * cur + inj[t * 16 : (t + 1) * 16]
        states.append(cur)
    st[...] = cur
    before = jnp.concatenate(befores, axis=0)
    state = jnp.concatenate(states, axis=0)
    u = u32[...]
    r = sigmoid(rpre[...] + vr[...] * before + br[...])
    hv = jnp.where(live, r * state + (1.0 - r) * u, 0.0)
    for t in range(STEPS):
        for b in range(2):
            part = hv[t * 16 : (t + 1) * 16, b * BLK : (b + 1) * BLK]
            hown[0, b, t * 8 : (t + 1) * 8, :] = part[:8]
            hoth[0, b, t * 8 : (t + 1) * 8, :] = part[8:]
    ds = gy * r
    dx = gy - ds
    drl = dx * r * (state - u)
    sr = dec * ds + vr[...] * drl
    dstate[...] = ds
    src[...] = sr
    bc[...] = before - cd
    du0[...] = dx
    dz3[...] = drl.astype(BF)
    p, l = pp[...], lb[...]
    for t in range(STEPS):
        l = l + p * sr[t * 16 : (t + 1) * 16]
        p = p * dec[t * 16 : (t + 1) * 16]
    pp[...] = p
    lb[...] = l
    ac[0:8, :] += jnp.sum((drl * before).reshape(32, 8, 256), axis=0)
    ac[8:16, :] += jnp.sum(drl.reshape(32, 8, 256), axis=0)

    @pl.when(i == tiles - 1)
    def _():
        acc[...] = ac[...]
        lbs[...] = l
        for ks in range(4):
            n = ks * parts + parts - 1
            tl, tp = l[n : n + 1], p[n : n + 1]
            for h in range(parts - 2, -1, -1):
                n = ks * parts + h
                tl = l[n : n + 1] + p[n : n + 1] * tl
                tp = p[n : n + 1] * tp
            summ[ks : ks + 1, :] = tp
            summ[4 + ks : 5 + ks, :] = tl


def states(s, ids, cand, decay, rpre, u32, cot_own, cot_oth, lim, scl, vr, br, plin, carries, held):
    rows = cand.shape[0]
    tiles = rows // 256
    a, mp = divmod(s, 2)
    seqs, parts = cot_own.shape[0], cot_own.shape[1]
    first = held is None
    rowblk = pl.BlockSpec((256, 256), lambda i, ids: (i, 0))
    fix = lambda shape: pl.BlockSpec(shape, lambda i, ids: (0,) * len(shape))
    chan = pl.BlockSpec((1, 256), lambda i, ids: (0, s))

    def nat_own(m):
        return pl.BlockSpec(
            (seqs, parts, STEPS, BLK), lambda i, ids: (0, 0, i, m * 4 + 2 * ids[2] + a)
        )

    def nat_oth(m):
        return pl.BlockSpec((seqs, parts, STEPS, BLK), lambda i, ids: (0, 0, i, m * 2 + a))

    hspec = pl.BlockSpec((1, 2, 128, BLK), lambda i, ids: (s, 0, i, 0))
    in_specs = (
        [rowblk, rowblk, rowblk, pl.BlockSpec((256, 256), lambda i, ids: (i, s))]
        + [nat_own(2 * mp), nat_own(2 * mp + 1), nat_oth(2 * mp), nat_oth(2 * mp + 1)]
        + [fix((256, 128)), fix((256, 128)), chan, chan, fix((32, 256))]
        + [fix((8, 256))] * len(carries)
    )
    args = [ids, cand, decay, rpre, u32, cot_own, cot_own, cot_oth, cot_oth, lim, scl, vr, br, plin]
    args += list(carries)
    aliases = {}
    if not first:
        in_specs = in_specs + [pl.BlockSpec(memory_space=pl.ANY)] * 2
        aliases = {len(args): 0, len(args) + 1: 1}
        args += list(held)
    return pl.pallas_call(
        functools.partial(state_kernel, s, first, len(carries)),
        grid_spec=pltpu.PrefetchScalarGridSpec(
            num_scalar_prefetch=1,
            grid=(tiles,),
            in_specs=in_specs,
            out_specs=[
                hspec,
                hspec,
                rowblk,
                rowblk,
                rowblk,
                rowblk,
                rowblk,
                fix((16, 256)),
                fix((8, 256)),
                fix((16, 256)),
            ],
            scratch_shapes=[pltpu.VMEM((16, 256), F32)] * 4 + [pltpu.VMEM((2, 256, BLK), F32)],
        ),
        out_shape=[
            sds((4, 2, rows // 2, BLK), F32),
            sds((4, 2, rows // 2, BLK), F32),
            sds((rows, 256), F32),
            sds((rows, 256), F32),
            sds((rows, 256), F32),
            sds((rows, 256), F32),
            sds((rows, 256), BF),
            sds((16, 256), F32),
            sds((8, 256), F32),
            sds((16, 256), F32),
        ],
        input_output_aliases=aliases,
        compiler_params=params(32),
        cost_estimate=cost(rows * 256 * 60, rows * 256 * 40, rows * 256 * 2),
        name=f"states_{s}",
    )(*args)


def adjoint_kernel(n_in, ids, decay, bc, dstate, src, du0, u32, vf, plin, lbs, *rest):
    carries = rest[:n_in]
    dz12, du, acc, adj, ac = rest[n_in:]
    i = pl.program_id(0)
    tiles = pl.num_programs(0)
    parts = 4

    @pl.when(i == 0)
    def _():
        after = carries[-1][4:8, :]
        for ref in carries[-2::-1]:
            after = ref[4:8, :] + ref[0:4, :] * after
        for ks in range(4):
            cc = after[ks : ks + 1]
            for h in range(parts - 1, -1, -1):
                n = ks * parts + h
                adj[n : n + 1, :] = cc
                cc = lbs[n : n + 1, :] + plin[n : n + 1, :] * cc
        ac[...] = jnp.zeros_like(ac)

    dec = decay[...]
    ds = dstate[...]
    sr = src[...]
    cur = adj[...]
    totals = [None] * STEPS
    for t in range(STEPS - 1, -1, -1):
        totals[t] = ds[t * 16 : (t + 1) * 16] + cur
        cur = dec[t * 16 : (t + 1) * 16] * cur + sr[t * 16 : (t + 1) * 16]
    adj[...] = cur
    total = jnp.concatenate(totals, axis=0)
    dcand = total * (1.0 - dec)
    dfl = dcand * bc[...] * dec
    dz12[:, :256] = dcand.astype(BF)
    dz12[:, 256:] = dfl.astype(BF)
    du[...] = du0[...] + dfl * vf[...]
    ac[0:8, :] += jnp.sum((dfl * u32[...]).reshape(32, 8, 256), axis=0)
    ac[8:16, :] += jnp.sum(dfl.reshape(32, 8, 256), axis=0)

    @pl.when(i == tiles - 1)
    def _():
        acc[...] = ac[...]


def adjoints(s, ids, decay, bc, dstate, src, du0, u32, vf, plin, lbs, carries):
    rows = decay.shape[0]
    tiles = rows // 256
    last = tiles - 1
    rowblk = pl.BlockSpec((256, 256), lambda i, ids: (last - i, 0))
    fix = lambda shape: pl.BlockSpec(shape, lambda i, ids: (0,) * len(shape))
    return pl.pallas_call(
        functools.partial(adjoint_kernel, len(carries)),
        grid_spec=pltpu.PrefetchScalarGridSpec(
            num_scalar_prefetch=1,
            grid=(tiles,),
            in_specs=[rowblk] * 5
            + [
                pl.BlockSpec((256, 256), lambda i, ids: (last - i, s)),
                pl.BlockSpec((1, 256), lambda i, ids: (0, s)),
                fix((32, 256)),
                fix((16, 256)),
            ]
            + [fix((8, 256))] * len(carries),
            out_specs=[
                pl.BlockSpec((256, 512), lambda i, ids: (last - i, 0)),
                rowblk,
                fix((16, 256)),
            ],
            scratch_shapes=[pltpu.VMEM((16, 256), F32)] * 2,
        ),
        out_shape=[sds((rows, 512), BF), sds((rows, 256), F32), sds((16, 256), F32)],
        compiler_params=params(32),
        cost_estimate=cost(rows * 256 * 20, rows * 256 * 32),
        name=f"adjoints_{s}",
    )(ids, decay, bc, dstate, src, du0, u32, vf, plin, lbs, *carries)


def wgrad_kernel(ids, ubt, za0, zb0, za1, zb1, out):
    q = ids[0]
    lhs = ubt[...]
    for mp, (za, zb) in enumerate(((za0, zb0), (za1, zb1))):
        left = jnp.dot(lhs, za[...], preferred_element_type=F32)
        right = jnp.dot(lhs, zb[...], preferred_element_type=F32)
        for g in range(GATES):
            for mm in range(2):
                n = g * QUARTERS + 2 * mp + mm
                val = left[:, g * 256 + mm * BLK : g * 256 + (mm + 1) * BLK] if g < 2 else right[
                    :, mm * BLK : (mm + 1) * BLK
                ]
                out[(n // 3) ^ q, n % 3] = val.astype(BF)


def weight_grad_part(flip, nz, ids, ubt, za0, zb0, za1, zb1):
    width, rows = ubt.shape
    half = width // nz // 2
    full = lambda v: pl.BlockSpec(v.shape, lambda i, ids: (0, 0))

    def pick(i, ids):
        rh = 1 - ids[2] if flip else ids[2]
        return (2 * i + rh, 0)

    return pl.pallas_call(
        wgrad_kernel,
        grid_spec=pltpu.PrefetchScalarGridSpec(
            num_scalar_prefetch=1,
            grid=(nz,),
            in_specs=[pl.BlockSpec((half, rows), pick), full(za0), full(zb0), full(za1), full(zb1)],
            out_specs=pl.BlockSpec((4, 3, half, BLK), lambda i, ids: (0, 0, i, 0)),
        ),
        out_shape=sds((4, 3, nz * half, BLK), BF),
        compiler_params=params(32),
        cost_estimate=cost(2 * rows * width // 2 * 1536, rows * width + rows * 3072 + width * 1536),
        name="weight_grad_part",
    )(ids, ubt, za0, zb0, za1, zb1)


def unit_grad_kernel(first, ids, za0, zb0, za1, zb1, w0, w1, *rest):
    dims = (((1,), (1,)), ((), ()))
    if first:
        own, oth = rest
    else:
        pown, poth, e0, e1, e2, e3, own, oth, scr = rest
    total = None
    for za, zb, w in ((za0, zb0, w0), (za1, zb1, w1)):
        part = lax.dot_general(za[...], w[:, :512], dims, preferred_element_type=F32)
        total = part if total is None else total + part
        total = total + lax.dot_general(zb[...], w[:, 512:], dims, preferred_element_type=F32)
    if first:
        for t in range(STEPS):
            own[t * 8 : (t + 1) * 8, :] = total[t * 16 : t * 16 + 8]
            oth[t * 8 : (t + 1) * 8, :] = total[t * 16 + 8 : t * 16 + 16]
        return
    scr[...] = total
    c = ids[2]
    for s, ref in enumerate((e0, e1, e2, e3)):
        a, mp = divmod(s, 2)
        for mm in range(2):
            lane = pl.multiple_of((2 * mp + mm) * 512 + a * BLK + c * 256, BLK)
            scr[:, pl.ds(lane, BLK)] += ref[:, mm * BLK : (mm + 1) * BLK]
    for t in range(STEPS):
        own[t * 8 : (t + 1) * 8, :] = scr[t * 16 : t * 16 + 8] + pown[t * 8 : (t + 1) * 8, :]
        oth[t * 8 : (t + 1) * 8, :] = scr[t * 16 + 8 : t * 16 + 16] + poth[t * 8 : (t + 1) * 8, :]


def unit_grads(ids, dz, ws, partial, elem):
    rows = dz[0][0].shape[0]
    width = ws[0].shape[0]
    tiles = rows // 256
    first = partial is None
    blk = lambda n: pl.BlockSpec((256, n), lambda i, ids: (i, 0))
    wspec = pl.BlockSpec((width, 768), lambda i, ids: (0, 0))
    out = pl.BlockSpec((128, width), lambda i, ids: (i, 0))
    in_specs = [blk(512), blk(256), blk(512), blk(256), wspec, wspec]
    args = [ids, dz[0][0], dz[0][1], dz[1][0], dz[1][1], ws[0], ws[1]]
    scratch = []
    if not first:
        in_specs += [out, out] + [blk(256)] * 4
        args += list(partial) + list(elem)
        scratch = [pltpu.VMEM((256, width), F32)]
    return pl.pallas_call(
        functools.partial(unit_grad_kernel, first),
        grid_spec=pltpu.PrefetchScalarGridSpec(
            num_scalar_prefetch=1,
            grid=(tiles,),
            in_specs=in_specs,
            out_specs=[out, out],
            scratch_shapes=scratch,
        ),
        out_shape=[sds((rows // 2, width), F32)] * 2,
        compiler_params=params(40),
        cost_estimate=cost(2 * rows * width * 1536, rows * 3072 + width * 3072 + rows * width * 8),
        name="unit_grads",
    )(*args)


def activation_kernel(ids, tok, hown, hrcv, out):
    c = ids[2]
    for s in range(4):
        a, mp = divmod(s, 2)
        for mm in range(2):
            base = (2 * mp + mm) * 512 + a * BLK
            for ref, core in ((hown, c), (hrcv, 1 - c)):
                lane = pl.ds(pl.multiple_of(base + core * 256, BLK), BLK)
                for st in range(8):
                    sq, h = divmod(st, 4)
                    val = ref[s, mm, pl.ds(st, STEPS, stride=8), :]
                    out[sq, h, :, lane] = tok[sq, h, :, lane].astype(F32) + val


def activations_of(ids, tok, hown, hrcv):
    seqs, parts, steps, width = tok.shape
    tiles = steps // STEPS
    nat = pl.BlockSpec((seqs, parts, STEPS, width), lambda i, ids: (0, 0, i, 0))
    hspec = pl.BlockSpec((4, 2, 128, BLK), lambda i, ids: (0, 0, i, 0))
    return pl.pallas_call(
        activation_kernel,
        grid_spec=pltpu.PrefetchScalarGridSpec(
            num_scalar_prefetch=1, grid=(tiles,), in_specs=[nat, hspec, hspec], out_specs=nat
        ),
        out_shape=sds(tok.shape, F32),
        compiler_params=params(24),
        cost_estimate=cost(seqs * parts * steps * width, seqs * parts * steps * width * 10),
        name="activations_of",
    )(ids, tok, hown, hrcv)


def input_grad_kernel(ids, duo, dur, tok, cot, lim, scl, gain, *rest):
    accs = rest[:8]
    out, sums, ga, ba, scr = rest[8:]
    i = pl.program_id(0)
    tiles = pl.num_programs(0)

    @pl.when(i == 0)
    def _():
        ga[...] = jnp.zeros_like(ga)
        ba[...] = jnp.zeros_like(ba)

    for j in range(scr.shape[0]):
        scr[j] = duo[:, j * BLK : (j + 1) * BLK] + dur[:, j * BLK : (j + 1) * BLK]
    step = lax.broadcasted_iota(jnp.int32, (STEPS, 1), 0) + i * STEPS
    for st in range(8):
        sq, h = divmod(st, 4)
        du = jnp.concatenate(
            [scr[j, pl.ds(st, STEPS, stride=8), :] for j in range(scr.shape[0])], axis=1
        )
        normed, rstd = norm_of(tok[sq, h].astype(F32))
        dn = du * gain[...]
        gn = du * normed
        m1 = jnp.mean(dn, axis=-1, keepdims=True)
        m2 = jnp.mean(dn * normed, axis=-1, keepdims=True)
        gy = jnp.where(step < lim[st], cot[sq, h].astype(F32) * scl[0], 0.0)
        out[sq, h] = rstd * (dn - m1 - normed * m2) + gy
        ga[...] += gn[0:8] + gn[8:16]
        ba[...] += du[0:8] + du[8:16]

    @pl.when(i == tiles - 1)
    def _():
        sums[...] = jnp.zeros_like(sums)
        sums[4:5, :] = jnp.sum(ga[...], axis=0, keepdims=True)
        sums[5:6, :] = jnp.sum(ba[...], axis=0, keepdims=True)
        c = ids[2]
        for s in range(4):
            a, mp = divmod(s, 2)
            accb, accc = accs[s], accs[4 + s]
            rows = (accc[0:8, :], accb[0:8, :], accc[8:16, :], accb[8:16, :])
            for j, val in enumerate(rows):
                val = jnp.sum(val, axis=0, keepdims=True)
                for mm in range(2):
                    lane = pl.multiple_of((2 * mp + mm) * 512 + a * BLK + c * 256, BLK)
                    sums[j : j + 1, pl.ds(lane, BLK)] = val[:, mm * BLK : (mm + 1) * BLK]


def input_grads(ids, duo, dur, tok, cot, lim8, scale, gain, accb, accc):
    seqs, parts, steps, width = tok.shape
    tiles = steps // STEPS
    nat = pl.BlockSpec((seqs, parts, STEPS, width), lambda i, ids: (0, 0, i, 0))
    fix = lambda shape: pl.BlockSpec(shape, lambda i, ids: (0,) * len(shape))
    smem = pl.BlockSpec(memory_space=pltpu.SMEM)
    dub = pl.BlockSpec((128, width), lambda i, ids: (i, 0))
    n = seqs * parts * steps * width
    return pl.pallas_call(
        input_grad_kernel,
        grid_spec=pltpu.PrefetchScalarGridSpec(
            num_scalar_prefetch=1,
            grid=(tiles,),
            in_specs=[dub, dub, nat, nat, smem, smem, fix((1, width))] + [fix((16, 256))] * 8,
            out_specs=[nat, fix((8, width))],
            scratch_shapes=[
                pltpu.VMEM((8, width), F32),
                pltpu.VMEM((8, width), F32),
                pltpu.VMEM((width // BLK, 128, BLK), F32),
            ],
        ),
        out_shape=[sds(tok.shape, F32), sds((8, width), F32)],
        compiler_params=params(32),
        cost_estimate=cost(n * 20, n * 16),
        name="input_grads",
    )(ids, duo, dur, tok, cot, lim8, scale, gain, *accb, *accc)


def assemble_kernel(ids, k0, k1, x0, x1, out):
    c = ids[2]
    for refs, core in (((k0, k1), c), ((x0, x1), 1 - c)):
        for a, ref in enumerate(refs):
            for j in range(3):
                lane = pl.multiple_of(j * 512 + a * BLK + core * 256, BLK)
                out[:, pl.ds(lane, BLK)] = ref[j]


def assemble(ids, kept, swapped):
    rows = kept[0].shape[1]
    return pl.pallas_call(
        assemble_kernel,
        grid_spec=pltpu.PrefetchScalarGridSpec(
            num_scalar_prefetch=1,
            grid=(1,),
            in_specs=[pl.BlockSpec((3, rows, BLK), lambda i, ids: (0, 0, 0))] * 4,
            out_specs=pl.BlockSpec((rows, 1536), lambda i, ids: (0, 0)),
        ),
        out_shape=sds((rows, 1536), F32),
        compiler_params=params(16),
        cost_estimate=cost(0, rows * 1536 * 8),
        name="assemble",
    )(ids, *kept, *swapped)


def local(
    nseq,
    ndp,
    tokens,
    cotangent,
    weight,
    forget_peep,
    reset_peep,
    forget_bias,
    reset_bias,
    norm_gain,
    norm_bias,
    lengths,
):
    axes = ("seq", "dp")
    nz = ndp // 2
    seqs, span, width = tokens.shape
    parts = 8 // seqs
    sub = span // parts
    q = lax.axis_index("seq").astype(jnp.int32)
    dp = lax.axis_index("dp").astype(jnp.int32)
    z, c = dp // 2, dp % 2
    ids = jnp.stack([q, z, c])

    def table(move):
        pairs = []
        for qq in range(nseq):
            for zz in range(nz):
                for cc in range(2):
                    to = move(qq, zz, cc)
                    if to is not None:
                        pairs.append(
                            (qq * ndp + zz * 2 + cc, to[0] * ndp + to[1] * 2 + to[2])
                        )
        return pairs

    def send(value, move):
        return lax.ppermute(value, axes, table(move))

    def to_core(qq, zz, cc):
        return (qq, zz, 1 - cc)

    def to_x(qq, zz, cc):
        return (qq ^ 1, zz, cc)

    def to_y(qq, zz, cc):
        return (qq ^ 2, zz, cc)

    def shift_z(k):
        return lambda qq, zz, cc: (qq, (zz + k) % nz, cc)

    def shift_q(k):
        return lambda qq, zz, cc: (qq + k, zz, cc) if 0 <= qq + k < nseq else None

    mine, theirs = split_weight(ids, weight)
    recv = send(theirs, to_core)
    tok4 = tokens.reshape(seqs, parts, sub, width)
    cot4 = cotangent.reshape(seqs, parts, sub, width)
    tok_oth = send(tokens, to_core).reshape(seqs, parts, sub, width)
    cot_cols = jnp.concatenate(
        [lax.dynamic_slice_in_dim(cotangent, m * 512 + (1 - c) * 256, 256, 2) for m in range(4)],
        axis=2,
    )
    cot_oth = send(cot_cols, to_core).reshape(seqs, parts, sub, width // 2)
    len_oth = send(lengths, to_core)

    lens = jnp.stack([lengths, len_oth])
    counts = jnp.sum(lens, axis=1).astype(F32)
    scale = (seqs * span * nseq) / counts
    lim16 = (
        lens[:, :, None] - q * span - sub * jnp.arange(parts, dtype=jnp.int32)[None, None, :]
    ).reshape(16)
    lim = jnp.broadcast_to(lim16[None, :, None], (STEPS, 16, BLK)).reshape(256, BLK)
    scl = jnp.broadcast_to(scale[None, :, None, None], (STEPS, 2, 8, BLK)).reshape(256, BLK)

    def by_core(vec):
        v = lax.dynamic_slice_in_dim(vec.reshape(4, 4, BLK), 2 * c, 2, 1)
        return v.transpose(1, 0, 2).reshape(1, width // 2)

    vf, vr, bfor, brst = (by_core(v) for v in (forget_peep, reset_peep, forget_bias, reset_bias))
    gain, bias = norm_gain.reshape(1, width), norm_bias.reshape(1, width)

    qb = weight.shape[0] // 2
    source = jnp.where(q // 2 == c, mine, recv)
    quarter = lax.dynamic_slice_in_dim(source, (q % 2) * qb, qb, 0)
    pieces = []
    for s in range(4):
        piece = quarter[:, s * 768 : (s + 1) * 768]
        if nz <= 4:
            rel = jnp.concatenate([send(piece, shift_z(-k)) for k in range(1, nz)], axis=0)
        else:
            groups = [[cc + 2 * zz for zz in range(nz)] for cc in range(2)]
            got = lax.all_gather(piece, "dp", axis=0, tiled=True, axis_index_groups=groups)
            rel = lax.dynamic_slice_in_dim(
                jnp.concatenate([got, got], axis=0), (z + 1) * qb, (nz - 1) * qb, 0
            )
        gx = send(rel, to_x)
        gy = send(rel, to_y)
        dx = send(gy[:, :384], to_x)
        dy = send(gx[:, 384:], to_y)
        pieces.append((rel, gx, gy, dx, dy))

    ub, ubt, u32 = norm_tokens(ids, tok4, tok_oth, gain, bias)

    held = None
    ws, elem, accb, accc = [], [], [], []
    kept, swapped = [], []
    partial = None
    for a in range(2):
        fwd = []
        for s in (2 * a, 2 * a + 1):
            fwd.append(project(s, nz, ids, ub, u32, mine, recv, pieces[s], lim, vf, bfor))
            ws.append(fwd[-1][3])
        both = jnp.stack([f[5] for f in fwd])
        got = [send(both, shift_q(k)) for k in range(1, nseq)]
        mid = []
        for n, s in enumerate((2 * a, 2 * a + 1)):
            cand, decay, rpre, _, plin, _ = fwd[n]
            mid.append(
                states(
                    s, ids, cand, decay, rpre, u32, cot4, cot_oth, lim, scl, vr, brst, plin,
                    [g[n] for g in got], held,
                )
            )
            held = mid[-1][:2]
            accb.append(mid[-1][9])
        both = jnp.stack([m[8] for m in mid])
        got = [send(both, shift_q(-k)) for k in range(1, nseq)]
        dz = []
        for n, s in enumerate((2 * a, 2 * a + 1)):
            _, _, dstate, src, bc, du0, dz3, lbs, _, _ = mid[n]
            dz12, du, acc = adjoints(
                s, ids, fwd[n][1], bc, dstate, src, du0, u32, vf, fwd[n][4], lbs,
                [g[n] for g in got],
            )
            elem.append(du)
            accc.append(acc)
            dz.append((dz12, dz3))
        for flip in (True, False):
            out = weight_grad_part(
                flip, nz, ids, ubt, dz[0][0], dz[0][1], dz[1][0], dz[1][1]
            )
            half = out.shape[2] // 2
            ra = send(out[3, :, :half], to_x)
            rb = send(out[3, :, half:], to_y)
            s1 = jnp.concatenate(
                [out[1, :, :half], (out[1, :, half:].astype(F32) + rb.astype(F32)).astype(BF)], 1
            )
            s2 = jnp.concatenate(
                [(out[2, :, :half].astype(F32) + ra.astype(F32)).astype(BF), out[2, :, half:]], 1
            )
            r1 = send(s1, to_x)
            r2 = send(s2, to_y)
            tot = out[0].astype(F32) + r1.astype(F32) + r2.astype(F32)
            rows = tot.shape[1] // nz
            if nz <= 4:
                low = tot.astype(BF)
                acc = lax.dynamic_slice_in_dim(tot, z * rows, rows, 1)
                for k in range(1, nz):
                    part = lax.dynamic_slice_in_dim(low, ((z + k) % nz) * rows, rows, 1)
                    acc = acc + send(part, shift_z(k)).astype(F32)
            else:
                groups = [[cc + 2 * zz for zz in range(nz)] for cc in range(2)]
                acc = lax.psum_scatter(
                    tot, "dp", scatter_dimension=1, axis_index_groups=groups, tiled=True
                )
            if flip:
                swapped.append(send(acc, to_core))
            else:
                kept.append(acc)
        partial = unit_grads(ids, dz, ws[2 * a :], partial, elem if a else None)

    hrcv = send(held[1], to_core)
    activations = activations_of(ids, tok4, held[0], hrcv)
    dur = send(partial[1], to_core)
    input_grad, sums = input_grads(
        ids, partial[0], dur, tok4, cot4, lim16[:8], scale[:1], gain, accb, accc
    )
    bit = 1
    while bit < nseq:
        sums = sums + send(sums, lambda qq, zz, cc, b=bit: (qq ^ b, zz, cc))
        bit *= 2
    bit = 1
    while bit < nz:
        sums = sums + send(sums, lambda qq, zz, cc, b=bit: (qq, zz ^ b, cc))
        bit *= 2
    sums = sums + send(sums, to_core)
    weight_grad = assemble(ids, kept, swapped)
    shape = tokens.shape
    return (
        activations.reshape(shape),
        input_grad.reshape(shape),
        weight_grad,
        sums[0],
        sums[1],
        sums[2],
        sums[3],
        sums[4],
        sums[5],
    )


def solution(mesh):
    whole = P("dp", "seq", None)
    in_specs = (whole, whole, P("dp", None)) + (P(),) * 6 + (P("dp"),)
    out_specs = (whole, whole, P("dp", "seq")) + (P(),) * 6
    step = functools.partial(local, mesh.shape["seq"], mesh.shape["dp"])
    return jax.shard_map(step, mesh=mesh, in_specs=in_specs, out_specs=out_specs, check_vma=False)
```

```python
import functools

import jax
import jax.numpy as jnp
from jax import lax
from jax.experimental import pallas as pl
from jax.experimental.pallas import tpu as pltpu
from jax.sharding import PartitionSpec as P

EPS = 1e-05
F32 = jnp.float32
BF = jnp.bfloat16
STEPS = 16
BLK = 128
GATES = 3
QUARTERS = 4
PARTS = 4


def params(mib, dims=1):
    return pltpu.CompilerParams(
        vmem_limit_bytes=mib * 1024 * 1024, dimension_semantics=("arbitrary",) * dims
    )


def cost(flops, bytes_accessed, transcendentals=0):
    return pl.CostEstimate(
        flops=int(flops), bytes_accessed=int(bytes_accessed), transcendentals=int(transcendentals)
    )


def sds(shape, dtype):
    return jax.ShapeDtypeStruct(shape, dtype)


def far(shape, dtype):
    return pltpu.HBM(shape, dtype)


def near(shape, dtype):
    return pltpu.VMEM(shape, dtype)


def far_in(*values):
    return [pltpu.with_memory_space_constraint(v, pltpu.HBM) for v in values]


def near_in(*values):
    return [pltpu.with_memory_space_constraint(v, pltpu.VMEM) for v in values]


ANY = pl.BlockSpec(memory_space=pl.ANY)
NEAR = pl.BlockSpec(memory_space=pltpu.VMEM)
SMEM = pl.BlockSpec(memory_space=pltpu.SMEM)


def ordered(kernel, deps):
    n = len(deps)

    def body(ids, *refs):
        return kernel(ids, *refs[n:])

    return body, list(deps), [ANY] * n


def call(kernel, name, grid, ids, deps, args, in_specs, out_specs, out_shape, mib, est, scratch=()):
    body, deps, dep_specs = ordered(kernel, deps)
    return pl.pallas_call(
        body,
        grid_spec=pltpu.PrefetchScalarGridSpec(
            num_scalar_prefetch=1,
            grid=grid,
            in_specs=dep_specs + in_specs,
            out_specs=out_specs,
            scratch_shapes=list(scratch),
        ),
        out_shape=out_shape,
        compiler_params=params(mib, len(grid)),
        cost_estimate=est,
        name=name,
    )(ids, *deps, *args)


def call_flat(kernel, name, ids, deps, args, in_specs, out_shape, mib, est, scratch=(), out_specs=None, aliases=None):
    body, deps, dep_specs = ordered(kernel, deps)
    many = isinstance(out_shape, (list, tuple))
    if out_specs is None:
        out_specs = [NEAR] * len(out_shape) if many else NEAR
    shift = 1 + len(deps)
    return pl.pallas_call(
        body,
        in_specs=[SMEM] + dep_specs + in_specs,
        out_specs=out_specs,
        out_shape=out_shape,
        scratch_shapes=list(scratch),
        input_output_aliases={k + shift: v for k, v in (aliases or {}).items()},
        compiler_params=pltpu.CompilerParams(vmem_limit_bytes=mib * 1024 * 1024),
        cost_estimate=est,
        name=name,
    )(ids, *deps, *args)


def split_kernel(ids, w, mine, theirs):
    c = ids[2]
    for s in range(4):
        a, mp = divmod(s, 2)
        for g in range(GATES):
            for mm in range(2):
                dst = s * 768 + g * 256 + mm * BLK
                base = g * 2048 + (2 * mp + mm) * 512 + a * BLK
                here = pl.multiple_of(base + c * 256, BLK)
                there = pl.multiple_of(base + (1 - c) * 256, BLK)
                mine[:, dst : dst + BLK] = w[:, pl.ds(here, BLK)]
                theirs[:, dst : dst + BLK] = w[:, pl.ds(there, BLK)]


def split_weight(ids, weight):
    rows, cols = weight.shape
    tile = rows // 2
    spec = pl.BlockSpec((tile, cols // 2), lambda i, ids: (i, 0))
    return call(
        split_kernel, "split_weight", (2,), ids, (), far_in(weight),
        [pl.BlockSpec((tile, cols), lambda i, ids: (i, 0))], [spec, spec],
        [sds((rows, cols // 2), BF)] * 2, 16, cost(0, rows * cols * 4),
    )


def quarter_kernel(ids, mine, recv, out, p0, p1):
    q, c = ids[0], ids[2]
    half = out.shape[0]
    at = pl.ds(pl.multiple_of(lax.rem(q, 2) * half, half), half)
    first = (lax.div(q, 2) == c).astype(jnp.int32) == 1
    val = jnp.where(first, mine[at, :], recv[at, :])
    out[...] = val[:, 1536:]
    p0[...] = val[:, :768]
    p1[...] = val[:, 768:1536]


def quarter_of(ids, deps, mine, recv):
    rows, cols = mine.shape
    half = rows // 2
    return call_flat(
        quarter_kernel, "quarter_of", ids, deps, [mine, recv], [NEAR, NEAR],
        [sds((half, 1536), BF), sds((half, 768), BF), sds((half, 768), BF)], 16,
        cost(0, rows * cols * 4),
    )


def copy_kernel(ids, src, dst):
    dst[...] = src[...]


def hand_on(ids, deps, value):
    return call_flat(
        copy_kernel, "hand_on", ids, deps, [value], [NEAR], sds(value.shape, value.dtype), 16,
        cost(0, value.size * 4),
    )


def plane_kernel(ids, *refs):
    rel = refs[-1]
    row = 0
    for ref in refs[:-1]:
        rel[row : row + ref.shape[0], :] = ref[...]
        row += ref.shape[0]


def plane_pieces(s, ids, deps, parts):
    rows = sum(p.shape[0] for p in parts)
    return call_flat(
        plane_kernel, f"plane_pieces_{s}", ids, deps, list(parts), [NEAR] * len(parts),
        sds((rows, 768), BF), 16, cost(0, rows * 768 * 4),
    )


def cross_kernel(ids, gx, gy, tox, toy):
    tox[...] = gy[:, :384]
    toy[...] = gx[:, 384:]


def cross_pieces(s, ids, deps, gx, gy):
    rows = gx.shape[0]
    return call_flat(
        cross_kernel, f"cross_pieces_{s}", ids, deps, [gx, gy], [NEAR, NEAR],
        [sds((rows, 384), BF)] * 2, 16, cost(0, rows * 768 * 4),
    )


def norm_of(x):
    mean = jnp.mean(x, axis=-1, keepdims=True)
    centered = x - mean
    var = jnp.mean(centered * centered, axis=-1, keepdims=True)
    rstd = lax.rsqrt(var + EPS)
    return centered * rstd, rstd


def norm_kernel(ids, own, other, gain, bias, ub, ubt, ulo, scr):
    c = ids[2]
    seqs = own.shape[0]
    for k, ref in enumerate((own, other)):
        for st in range(8):
            sq, h = divmod(st, PARTS)
            normed, _ = norm_of(ref[sq, h].astype(F32))
            unit = normed * gain[...] + bias[...]
            for j in range(scr.shape[0]):
                scr[j, pl.ds(k * 128 + st, STEPS, stride=8), :] = unit[:, j * BLK : (j + 1) * BLK]
    for j in range(scr.shape[0]):
        low = scr[j].astype(BF)
        ub[0, :, :, j * BLK : (j + 1) * BLK] = low.reshape(2, 128, BLK)
        ubt[j * BLK : (j + 1) * BLK, :] = low.T
    for a in range(2):
        for m in range(QUARTERS):
            unit = scr[m * 4 + a + 2 * c]
            rest = (unit - unit.astype(BF).astype(F32)).astype(BF)
            dst = (a * QUARTERS + m) * BLK
            ulo[0, :, :, dst : dst + BLK] = rest.reshape(2, 128, BLK)


def tile_block(cols):
    return pl.BlockSpec((1, 2, 128, cols), lambda i, ids: (i, 0, 0, 0))


def norm_tokens(ids, deps, own, other, gain, bias):
    seqs, parts, steps, width = own.shape
    rows = seqs * parts * steps
    tiles = steps // STEPS
    nat = pl.BlockSpec((seqs, parts, STEPS, width), lambda i, ids: (0, 0, i, 0))
    vec = pl.BlockSpec((1, width), lambda i, ids: (0, 0))
    return call(
        norm_kernel, "norm_tokens", (tiles,), ids, deps, [*far_in(own, other), gain, bias],
        [nat, nat, vec, vec],
        [
            tile_block(width),
            pl.BlockSpec((width, 256), lambda i, ids: (0, i)),
            tile_block(width // 2),
        ],
        [
            far((tiles, 2, 128, width), BF),
            far((width, 2 * rows), BF),
            far((tiles, 2, 128, width // 2), BF),
        ],
        20, cost(rows * width * 20, rows * width * 14),
        scratch=[pltpu.VMEM((width // BLK, 256, BLK), F32)],
    )


def flat(ref):
    value = ref[...]
    return value.reshape(256, value.shape[-1])


def core_lane(a, m, c):
    return pl.multiple_of(m * 512 + a * BLK + c * 256, BLK)


def pairs():
    for tp in range(STEPS // 2):
        for k in range(2):
            yield k, tp * 16, k * 128 + tp * 16


def live_pair(lim, row, tile):
    live = lim[row : row + 16, :] > tile * STEPS
    return jnp.concatenate([live, live], axis=1)


def fold_streams(pr, lc, ahead):
    out = []
    order = range(PARTS) if ahead else range(PARTS - 1, -1, -1)
    for sq in range(2):
        tp = tl = None
        for h in order:
            n = sq * PARTS + h
            p, l = pr[n : n + 1], lc[n : n + 1]
            tp, tl = (p, l) if tp is None else ((p * tp, p * tl + l) if ahead else (p * tp, l + p * tl))
        out.append((tp, tl))
    return out


def proj_kernel(s, nz, joined, ids, ub, ulo, *rest):
    n_w = 1 if joined else 7
    weights, rest = rest[:n_w], rest[n_w:]
    lim, vf, bfor = rest[:3]
    rest = rest[3:]
    before = rest[0] if s % 2 else None
    cand, decay, rpre, plout, summ = rest[s % 2 : s % 2 + 5]
    rest = rest[s % 2 + 5 :]
    if joined:
        zbuf, prod, loc, wbuf, sems = rest
    else:
        wall, zbuf, prod, loc, wbuf, sems = rest
    tiles = cand.shape[0]
    width = wbuf.shape[0]
    q, z, c = ids[0], ids[1], ids[2]
    a, mp = divmod(s, 2)
    cols = slice(mp * 768, mp * 768 + 768)
    copies = []

    def put(src, row, rows, lo=0, hi=768):
        dst = wbuf.at[pl.ds(row, rows), lo:hi]
        copy = pltpu.make_async_copy(src, dst, sems.at[len(copies)])
        copy.start()
        copies.append(copy)

    if joined:
        put(weights[0].at[:, cols], 0, width)
    else:
        mine, recv, rel, gx, gy, dx, dy = weights
        zb = width // nz
        zb2, qb = zb // 2, zb // 4
        mult = lambda v: pl.multiple_of(v, qb)
        put(mine.at[:, s * 768 : (s + 1) * 768], mult(z * zb + c * zb2), zb2)
        put(recv.at[:, s * 768 : (s + 1) * 768], mult(z * zb + (1 - c) * zb2), zb2)
        for r in range(1, nz):
            base = lax.rem(z + r, nz) * zb
            lo, hi = (r - 1) * qb, r * qb
            put(rel.at[lo:hi, :], mult(base + q * qb), qb)
            put(gx.at[lo:hi, :], mult(base + (q ^ 1) * qb), qb)
            put(gy.at[lo:hi, :], mult(base + (q ^ 2) * qb), qb)
            put(dx.at[lo:hi, :], mult(base + (q ^ 3) * qb), qb, 0, 384)
            put(dy.at[lo:hi, :], mult(base + (q ^ 3) * qb), qb, 384, 768)
    for copy in copies:
        copy.wait()
    if not joined:
        keep = pltpu.make_async_copy(wbuf, wall, sems.at[len(copies)])
        keep.start()
    prod[...] = jnp.ones_like(prod)
    loc[...] = jnp.zeros_like(loc)

    def tile(ubr, ulor):
        i = pl.program_id(0)
        zbuf[:, :768] = jnp.dot(flat(ubr), wbuf[...], preferred_element_type=F32)
        low = flat(ulor).astype(F32)
        for mm in range(2):
            high = ubr[:, :, :, pl.ds(core_lane(a, 2 * mp + mm, c), BLK)].reshape(256, BLK)
            zbuf[:, 768 + mm * BLK : 768 + (mm + 1) * BLK] = (
                high.astype(F32) + low[:, mm * BLK : (mm + 1) * BLK]
            )
        pr = [prod[0:8, :], prod[8:16, :]]
        lc = [loc[0:8, :], loc[8:16, :]]
        for k, r0, row in pairs():
            cd = zbuf[row : row + 16, :256]
            logit = zbuf[row : row + 16, 256:512] + vf[...] * zbuf[row : row + 16, 768:] + bfor[...]
            dec = jnp.where(live_pair(lim, row, i), jax.nn.sigmoid(logit), 1.0)
            inj = (1.0 - dec) * cd
            cand[i, k, r0 : r0 + 16, :] = cd
            decay[i, k, r0 : r0 + 16, :] = dec
            rpre[i, k, r0 : r0 + 16, :] = zbuf[row : row + 16, 512:768]
            for t in range(2):
                d = dec[t * 8 : t * 8 + 8]
                lc[k] = d * lc[k] + inj[t * 8 : t * 8 + 8]
                pr[k] = d * pr[k]
        for k in range(2):
            prod[k * 8 : k * 8 + 8, :] = pr[k]
            loc[k * 8 : k * 8 + 8, :] = lc[k]

    pltpu.emit_pipeline(
        tile,
        grid=(tiles,),
        in_specs=[
            pl.BlockSpec((1, 2, 128, width), lambda i: (i, 0, 0, 0)),
            pl.BlockSpec((1, 2, 128, 256), lambda i: (i, 0, 0, s)),
        ],
    )(ub, ulo)
    if s % 2:
        summ[0] = before[0]
    plout[0:16, :] = prod[...]
    plout[16:32, :] = loc[...]
    for k in range(2):
        pr, lc = prod[k * 8 : k * 8 + 8, :], loc[k * 8 : k * 8 + 8, :]
        for sq, (tp, tl) in enumerate(fold_streams(pr, lc, True)):
            ks = k * 2 + sq
            summ[s % 2, ks : ks + 1, :] = tp
            summ[s % 2, 4 + ks : 5 + ks, :] = tl
    if not joined:
        keep.wait()


def project(s, nz, ids, deps, ub, ulo, weights, lim, vf, bfor, before):
    tiles, _, _, width = ub.shape
    joined = len(weights) == 1
    shape = (tiles, 2, 128, 256)
    rows = tiles * 256
    chan = slice(s * 256, s * 256 + 256)
    args = far_in(ub, ulo, *weights) + [lim, vf[:, chan], bfor[:, chan]]
    in_specs = [ANY] * (2 + len(weights)) + [NEAR] * 3
    if s % 2:
        args.append(before)
        in_specs.append(NEAR)
    out_shape = [near(shape, F32)] * 3 + [sds((32, 256), F32), sds((2, 8, 256), F32)]
    out_specs = [NEAR] * 5
    if not joined:
        out_shape.append(far((width, 768), BF))
        out_specs.append(ANY)
    return call_flat(
        functools.partial(proj_kernel, s, nz, joined), f"project_{s}", ids, deps, args, in_specs,
        out_shape, 16, cost(2 * rows * width * 768, rows * width * 2 + width * 768 * 4),
        scratch=[
            pltpu.VMEM((256, 1024), F32),
            pltpu.VMEM((16, 256), F32),
            pltpu.VMEM((16, 256), F32),
            pltpu.VMEM((width, 768), BF),
            pltpu.SemaphoreType.DMA((3 + 5 * (nz - 1),)),
        ],
        out_specs=out_specs,
    )


def halves(v):
    return v[:8], v[8:]


def enter(got, n, ahead, q, count):
    value = jnp.zeros((4, 256), F32)
    for j in range(count) if ahead else range(count - 1, -1, -1):
        used = (j < q) if ahead else (j > q)
        longer = got[j, n, 4:8, :] + got[j, n, 0:4, :] * value
        value = jnp.where(used, longer, value)
    return value


def state_kernel(a, count, held, ids, *refs):
    fwd = (refs[0:4], refs[4:8])
    ub, cot_own, cot_oth, lim, scl, vr, br, got = refs[8:16]
    rest = refs[16 + (2 if held else 0) :]
    hown, hoth = rest[:2]
    out = (rest[2:6], rest[6:10])
    dzr, uu, lbs, summ, acc, st, pp, lb, ac, scr = rest[10:]
    tiles = dzr.shape[0]
    q, c = ids[0], ids[2]
    for n in range(2):
        cand, decay, rpre, plin = fwd[n]
        bc, src, dstate, du0 = out[n]
        lanes = slice(n * 256, n * 256 + 256)
        carry = enter(got, n, True, q, count)
        for ks in range(4):
            cc = carry[ks : ks + 1]
            for h in range(PARTS):
                m = ks * PARTS + h
                st[m : m + 1, :] = cc
                cc = plin[m : m + 1, :] * cc + plin[16 + m : 17 + m, :]
        pp[...] = jnp.ones_like(pp)
        lb[...] = jnp.zeros_like(lb)
        ac[...] = jnp.zeros_like(ac)

        def tile(u0, u1, own0, own1, oth0, oth1, ho, ht):
            i = pl.program_id(0)
            for k, pair in enumerate(((own0, own1), (oth0, oth1))):
                for b, ref in enumerate(pair):
                    for m in range(8):
                        sq, h = divmod(m, PARTS)
                        scr[b, pl.ds(k * 128 + m, STEPS, stride=8), :] = ref[sq, h].astype(F32)
            cur = [st[0:8, :], st[8:16, :]]
            p = [pp[0:8, :], pp[8:16, :]]
            l = [lb[0:8, :], lb[8:16, :]]
            peep = [jnp.zeros((8, 256), F32)] * 2
            bias = [jnp.zeros((8, 256), F32)] * 2
            wr, wb = vr[:, lanes], br[:, lanes]
            for k, r0, row in pairs():
                at = slice(r0, r0 + 16)
                dec = decay[i, k, at, :]
                cd = cand[i, k, at, :]
                inj = (1.0 - dec) * cd
                befores, states = [], []
                for d, v in zip(halves(dec), halves(inj)):
                    befores.append(cur[k])
                    cur[k] = d * cur[k] + v
                    states.append(cur[k])
                before = jnp.concatenate(befores, axis=0)
                state = jnp.concatenate(states, axis=0)
                low = jnp.concatenate([u0[0, k, at, :], u1[0, k, at, :]], axis=1)
                uu[i, k, at, lanes] = low
                u = low.astype(F32)
                live = lim[row : row + 16, :] > i * STEPS
                sc = jnp.where(live, scl[row : row + 16, :], 0.0)
                gy = jnp.concatenate(
                    [scr[0, row : row + 16, :] * sc, scr[1, row : row + 16, :] * sc], axis=1
                )
                r = jax.nn.sigmoid(rpre[i, k, at, :] + wr * before + wb)
                gap = state - u
                hv = jnp.where(jnp.concatenate([live, live], axis=1), u + r * gap, 0.0).astype(BF)
                href = ht if k else ho
                href[0, 0, at, :] = hv[:, :BLK]
                href[0, 1, at, :] = hv[:, BLK:]
                ds = gy * r
                drl = ds * (1.0 - r) * gap
                sr = dec * ds + wr * drl
                dstate[i, k, at, :] = ds
                src[i, k, at, :] = sr
                bc[i, k, at, :] = before - cd
                du0[i, k, at, :] = gy - ds
                dzr[i, k, at, lanes] = drl.astype(BF)
                for d, v in zip(halves(dec), halves(sr)):
                    l[k] = l[k] + p[k] * v
                    p[k] = p[k] * d
                for e, w in zip(halves(drl), befores):
                    peep[k] = peep[k] + e * w
                    bias[k] = bias[k] + e
            for k in range(2):
                st[k * 8 : k * 8 + 8, :] = cur[k]
                pp[k * 8 : k * 8 + 8, :] = p[k]
                lb[k * 8 : k * 8 + 8, :] = l[k]
            ac[0:8, :] += peep[0] + peep[1]
            ac[8:16, :] += bias[0] + bias[1]

        nat = cot_own.shape[:2]

        def unit(mm):
            return pl.BlockSpec(
                (1, 2, 128, BLK), lambda i: (i, 0, 0, (2 * n + mm) * 4 + 2 * c + a)
            )

        def nat_own(mm):
            return pl.BlockSpec(
                (*nat, STEPS, BLK), lambda i: (0, 0, i, (2 * n + mm) * 4 + 2 * c + a)
            )

        def nat_oth(mm):
            return pl.BlockSpec((*nat, STEPS, BLK), lambda i: (0, 0, i, (2 * n + mm) * 2 + a))

        hspec = pl.BlockSpec((1, 2, 128, BLK), lambda i: (2 * a + n, 0, i, 0))
        pltpu.emit_pipeline(
            tile,
            grid=(tiles,),
            in_specs=[unit(0), unit(1), nat_own(0), nat_own(1), nat_oth(0), nat_oth(1)],
            out_specs=[hspec, hspec],
        )(ub, ub, cot_own, cot_own, cot_oth, cot_oth, hown, hoth)
        acc[n] = ac[...]
        lbs[n] = lb[...]
        for k in range(2):
            p, l = pp[k * 8 : k * 8 + 8, :], lb[k * 8 : k * 8 + 8, :]
            for sq, (tp, tl) in enumerate(fold_streams(p, l, False)):
                ks = k * 2 + sq
                summ[n, ks : ks + 1, :] = tp
                summ[n, 4 + ks : 5 + ks, :] = tl


def states(a, count, ids, deps, fwd, ub, cot_own, cot_oth, lim, scl, vr, br, got, held):
    tiles = ub.shape[0]
    rows = tiles * 128
    one = (tiles, 2, 128, 256)
    two = (tiles, 2, 128, 512)
    chan = slice(a * 512, a * 512 + 512)
    args, in_specs = [], []
    for f in fwd:
        args += near_in(*f[:3]) + [f[3]]
        in_specs += [NEAR] * 4
    args += far_in(ub, cot_own, cot_oth) + [lim, scl, vr[:, chan], br[:, chan], got]
    in_specs += [ANY] * 3 + [NEAR] * 5
    aliases = {}
    if held:
        aliases = {len(args): 0, len(args) + 1: 1}
        args += far_in(*held)
        in_specs += [ANY] * 2
    small = sds((2, 16, 256), F32)
    return call_flat(
        functools.partial(state_kernel, a, count, bool(held)), f"states_{a}", ids, deps, args,
        in_specs,
        [far((4, 2, rows, BLK), BF)] * 2
        + [near(one, F32)] * 8
        + [near(two, BF)] * 2
        + [small, sds((2, 8, 256), F32), small],
        16, cost(rows * 1024 * 60, rows * 1024 * 10, rows * 1024 * 2),
        scratch=[pltpu.VMEM((16, 256), F32)] * 4 + [pltpu.VMEM((2, 256, BLK), F32)],
        out_specs=[ANY] * 2 + [NEAR] * 13,
        aliases=aliases,
    )


def adjoint_kernel(count, ids, *refs):
    ins = (refs[0:6], refs[6:12])
    uu, vf, lbs, got, du, dzc, dzf, acc, adj = refs[12:]
    tiles = du.shape[0]
    q = ids[0]
    for n in range(2):
        decay, bc, src, dstate, du0, plin = ins[n]
        lanes = slice(n * 256, n * 256 + 256)
        wf = vf[:, lanes]
        after = enter(got, n, False, q, count)
        for ks in range(4):
            cc = after[ks : ks + 1]
            for h in range(PARTS - 1, -1, -1):
                m = ks * PARTS + h
                adj[m : m + 1, :] = cc
                cc = lbs[n, m : m + 1, :] + plin[m : m + 1, :] * cc

        def tile(step, state):
            i = tiles - 1 - step
            cur, peep, bias = [state[0], state[1]], state[2], state[3]
            for k, r0, _ in reversed(list(pairs())):
                at = slice(r0, r0 + 16)
                dec = decay[i, k, at, :]
                ds = dstate[i, k, at, :]
                sr = src[i, k, at, :]
                late = ds[8:] + cur[k]
                cur[k] = dec[8:] * cur[k] + sr[8:]
                early = ds[:8] + cur[k]
                cur[k] = dec[:8] * cur[k] + sr[:8]
                dcand = jnp.concatenate([early, late], axis=0) * (1.0 - dec)
                dfl = dcand * bc[i, k, at, :] * dec
                dzc[i, k, at, lanes] = dcand.astype(BF)
                dzf[i, k, at, lanes] = dfl.astype(BF)
                du[i, k, at, lanes] = du0[i, k, at, :] + dfl * wf
                w = dfl * uu[i, k, at, lanes].astype(F32)
                peep = peep + (w[:8] + w[8:])
                bias = bias + (dfl[:8] + dfl[8:])
            return cur[0], cur[1], peep, bias

        zero = jnp.zeros((8, 256), F32)
        end = lax.fori_loop(0, tiles, tile, (adj[0:8, :], adj[8:16, :], zero, zero))
        acc[n, 0:8, :] = end[2]
        acc[n, 8:16, :] = end[3]


def adjoints(a, count, ids, deps, fwd, mid, uu, vf, lbs, got):
    tiles = uu.shape[0]
    rows = tiles * 128
    shape = (tiles, 2, 128, 512)
    args = []
    for f, m in zip(fwd, mid):
        args += near_in(f[1], *m) + [f[3]]
    args += near_in(uu) + [vf[:, a * 512 : a * 512 + 512], lbs, got]
    return call_flat(
        functools.partial(adjoint_kernel, count), f"adjoints_{a}", ids, deps, args,
        [NEAR] * len(args),
        [near(shape, F32), near(shape, BF), near(shape, BF), sds((2, 16, 256), F32)],
        16, cost(rows * 1024 * 20, rows * 1024 * 4), scratch=[pltpu.VMEM((16, 256), F32)],
    )


def wgrad_kernel(which, nz, ids, ubt, dzc, dzf, dzr, own, xp, yp, da, db, scr):
    q, c = ids[0], ids[2]
    rh = 1 - c if which == "other" else c
    half = scr.shape[0]
    rows = ubt.shape[1]

    def tile(lhs):
        i = pl.program_id(0)
        for g, dz in enumerate((dzc, dzf, dzr)):
            rhs = dz[...].reshape(rows, 512)
            scr[:, g * 512 : (g + 1) * 512] = jnp.dot(
                lhs[...], rhs, preferred_element_type=F32
            ).astype(BF)

        def block(r, j):
            return scr[:, pl.ds(pl.multiple_of(((q ^ r) * 3 + j) * BLK, BLK), BLK)]

        at = pl.ds(pl.multiple_of(i * half, half), half)
        for j in range(3):
            own[j, at, :] = block(0, j)
            xp[j, at, :] = block(1, j)
            yp[j, at, :] = block(2, j)

        @pl.when(i < nz // 2)
        def _():
            for j in range(3):
                da[j, at, :] = block(3, j)

        @pl.when(i >= nz // 2)
        def _():
            back = pl.ds(pl.multiple_of((i - nz // 2) * half, half), half)
            for j in range(3):
                db[j, back, :] = block(3, j)

    pltpu.emit_pipeline(
        tile, grid=(nz,), in_specs=[pl.BlockSpec((half, rows), lambda i: (2 * i + rh, 0))]
    )(ubt)


def weight_grad_part(which, nz, ids, deps, ubt, dz):
    width, rows = ubt.shape
    half = width // nz // 2
    return call_flat(
        functools.partial(wgrad_kernel, which, nz), "weight_grad_part", ids, deps,
        [*far_in(ubt), *near_in(*dz)], [ANY] + [NEAR] * 3,
        [sds((3, nz * half, BLK), BF)] * 3 + [sds((3, nz * half // 2, BLK), BF)] * 2,
        16, cost(2 * rows * nz * half * 1536, rows * width + width * 1536),
        scratch=[pltpu.VMEM((half, 1536), BF)],
    )


def relay_kernel(ids, xp, yp, ra, rb, s1, s2):
    half = ra.shape[1]
    s1[:, :half, :] = xp[:, :half, :]
    s1[:, half:, :] = (xp[:, half:, :].astype(F32) + rb[...].astype(F32)).astype(BF)
    s2[:, :half, :] = (yp[:, :half, :].astype(F32) + ra[...].astype(F32)).astype(BF)
    s2[:, half:, :] = yp[:, half:, :]


def relay_sums(ids, deps, xp, yp, ra, rb):
    rows = xp.shape[1]
    return call_flat(
        relay_kernel, "relay_sums", ids, deps, [xp, yp, ra, rb], [NEAR] * 4,
        [sds(xp.shape, BF)] * 2, 16, cost(rows * 768, rows * 384 * 10),
    )


def plane_sum_kernel(nz, ids, own, r1, r2, *outs):
    rows = outs[0].shape[1]
    for k, out in enumerate(outs):
        start = lax.rem(ids[1] + k, nz) * rows
        at = pl.ds(pl.multiple_of(start, rows), rows)
        tot = own[:, at, :].astype(F32) + r1[:, at, :].astype(F32) + r2[:, at, :].astype(F32)
        out[...] = tot.astype(out.dtype)


def plane_sums(nz, ids, deps, own, r1, r2):
    rows = own.shape[1] // nz
    return call_flat(
        functools.partial(plane_sum_kernel, nz), "plane_sums", ids, deps, [own, r1, r2], [NEAR] * 3,
        [sds((3, rows, BLK), F32)] + [sds((3, rows, BLK), BF)] * (nz - 1), 16,
        cost(rows * 768 * nz, rows * 384 * 8 * nz),
    )


def total_kernel(ids, *refs):
    total = refs[0][...].astype(F32)
    for ref in refs[1:-1]:
        total = total + ref[...].astype(F32)
    refs[-1][...] = total


def total_of(ids, deps, parts):
    return call_flat(
        total_kernel, "total_of", ids, deps, list(parts), [NEAR] * len(parts),
        sds(parts[0].shape, F32), 16, cost(parts[0].size * 4, parts[0].size * 14),
    )


DIMS = (((1,), (1,)), ((), ()))
TILE_N = 512


def unit_kernel(k, ids, c0, f0, r0, c1, f1, r1, e0, e1, w0, w1, w2, out, lhs, acc):
    c = ids[2]
    rows = acc.shape[0]
    for a, refs in enumerate(((c0, f0, r0), (c1, f1, r1))):
        for mp in range(2):
            for g, ref in enumerate(refs):
                dst = a * 1536 + mp * 768 + g * 256
                val = ref[:, k, :, mp * 256 : (mp + 1) * 256]
                lhs[:, dst : dst + 256] = val.reshape(rows, 256)

    def tile(wa, wb, wc):
        m = pl.program_id(0)
        acc[:, :TILE_N] = lax.dot_general(
            lhs[:, :768], wa[...], DIMS, preferred_element_type=F32
        ) + lax.dot_general(lhs[:, 768:1536], wb[...], DIMS, preferred_element_type=F32)
        acc[:, :TILE_N] += lax.dot_general(lhs[:, 1536:], wc[...], DIMS, preferred_element_type=F32)
        for a, ref in enumerate((e0, e1)):
            val = ref[:, k, :, pl.ds(pl.multiple_of(m * BLK, BLK), BLK)]
            acc[:, pl.ds(core_lane(a, 0, c), BLK)] += val.reshape(rows, BLK)
        out[:, pl.ds(pl.multiple_of(m * TILE_N, TILE_N), TILE_N)] = acc[...].astype(out.dtype)

    blk = lambda w: pl.BlockSpec((TILE_N, w.shape[1]), lambda i: (i, 0))
    pltpu.emit_pipeline(
        tile, grid=(w0.shape[0] // TILE_N,), in_specs=[blk(w0), blk(w1), blk(w2)]
    )(w0, w1, w2)


def unit_grads(k, ids, deps, dz0, dz1, e0, e1, ws):
    tiles = e0.shape[0]
    rows, width = tiles * 128, ws[0].shape[0]
    return call_flat(
        functools.partial(unit_kernel, k), f"unit_grads_{k}", ids, deps,
        [*near_in(*dz0, *dz1, e0, e1), *far_in(*ws)], [NEAR] * 8 + [ANY] * 3,
        near((rows, width), BF if k else F32), 24,
        cost(2 * rows * width * 3072, width * 3072 * 2),
        scratch=[pltpu.VMEM((rows, 3072), BF), pltpu.VMEM((rows, TILE_N), F32)],
    )


def norm_grad_kernel(ids, du_own, recv, tok, cot, lim, scl, gain, *rest):
    accb, accc = rest[:2], rest[2:4]
    out, sums, ga, ba, scr = rest[4:]
    c = ids[2]
    ga[...] = jnp.zeros_like(ga)
    ba[...] = jnp.zeros_like(ba)

    def tile(tokr, cotr, outr):
        i = pl.program_id(0)
        rows = pl.ds(pl.multiple_of(i * 128, 128), 128)
        for j in range(scr.shape[0]):
            lanes = slice(j * BLK, (j + 1) * BLK)
            scr[j] = du_own[rows, lanes] + recv[rows, lanes].astype(F32)
        step = lax.broadcasted_iota(jnp.int32, (STEPS, 1), 0) + i * STEPS
        gsum = jnp.zeros(ga.shape, F32)
        bsum = jnp.zeros(ba.shape, F32)
        for st in range(8):
            sq, h = divmod(st, PARTS)
            x16 = tokr[sq, h].astype(F32)
            c16 = cotr[sq, h].astype(F32)
            for part in range(2):
                cut = slice(part * 8, part * 8 + 8)
                du = jnp.concatenate(
                    [scr[j, pl.ds(st + part * 64, 8, stride=8), :] for j in range(scr.shape[0])],
                    axis=1,
                )
                normed, rstd = norm_of(x16[cut])
                dn = du * gain[...]
                m1 = jnp.mean(dn, axis=-1, keepdims=True)
                m2 = jnp.mean(dn * normed, axis=-1, keepdims=True)
                gy = jnp.where(step[cut] < lim[st], c16[cut] * scl[0], 0.0)
                outr[sq, h, cut, :] = rstd * (dn - m1 - normed * m2) + gy
                gsum = gsum + du * normed
                bsum = bsum + du
        ga[...] += gsum
        ba[...] += bsum

    seqs, parts, steps, width = tok.shape
    nat = pl.BlockSpec((seqs, parts, STEPS, width), lambda i: (0, 0, i, 0))
    pltpu.emit_pipeline(
        tile, grid=(steps // STEPS,), in_specs=[nat, nat], out_specs=[nat]
    )(tok, cot, out)
    sums[...] = jnp.zeros_like(sums)
    sums[4:5, :] = jnp.sum(ga[...], axis=0, keepdims=True)
    sums[5:6, :] = jnp.sum(ba[...], axis=0, keepdims=True)
    for s in range(4):
        a, mp = divmod(s, 2)
        rows = (
            accc[a][mp, 0:8, :],
            accb[a][mp, 0:8, :],
            accc[a][mp, 8:16, :],
            accb[a][mp, 8:16, :],
        )
        for j, val in enumerate(rows):
            val = jnp.sum(val, axis=0, keepdims=True)
            for mm in range(2):
                lane = pl.ds(core_lane(a, 2 * mp + mm, c), BLK)
                sums[j : j + 1, lane] = val[:, mm * BLK : (mm + 1) * BLK]


def norm_grads(ids, deps, du_own, recv, tok, cot, lim8, scale, gain, accb, accc):
    rows, width = du_own.shape
    n = rows * width
    return call_flat(
        norm_grad_kernel, "norm_grads", ids, deps,
        [*near_in(du_own, recv), *far_in(tok, cot), lim8, scale, gain, *accb, *accc],
        [NEAR] * 2 + [ANY] * 2 + [SMEM] * 2 + [NEAR] * 5,
        [far(tok.shape, F32), sds((8, width), F32)], 20, cost(n * 20, n * 8),
        scratch=[
            pltpu.VMEM((8, width), F32),
            pltpu.VMEM((8, width), F32),
            pltpu.VMEM((width // BLK, 128, BLK), F32),
        ],
        out_specs=[ANY, NEAR],
    )


def activation_kernel(ids, tok, hown, hrcv, out, scr):
    c = ids[2]
    for s in range(4):
        a, mp = divmod(s, 2)
        for mm in range(2):
            for n, (ref, core) in enumerate(((hown, c), (hrcv, 1 - c))):
                scr[n] = ref[s, mm].astype(F32)
                lane = pl.ds(core_lane(a, 2 * mp + mm, core), BLK)
                for st in range(8):
                    sq, h = divmod(st, PARTS)
                    val = scr[n, pl.ds(st, STEPS, stride=8), :]
                    out[sq, h, :, lane] = tok[sq, h, :, lane].astype(F32) + val


def activations_of(ids, deps, tok, hown, hrcv):
    seqs, parts, steps, width = tok.shape
    tiles = steps // STEPS
    nat = pl.BlockSpec((seqs, parts, STEPS, width), lambda i, ids: (0, 0, i, 0))
    hspec = pl.BlockSpec((4, 2, 128, BLK), lambda i, ids: (0, 0, i, 0))
    n = seqs * parts * steps * width
    return call(
        activation_kernel, "activations_of", (tiles,), ids, deps, far_in(tok, hown, hrcv),
        [nat, hspec, hspec], nat, far(tok.shape, F32), 16, cost(n, n * 8),
        scratch=[pltpu.VMEM((2, 128, BLK), F32)],
    )


def assemble_kernel(counts, ids, *refs):
    out = refs[-1]
    c = ids[2]
    start = 0
    for b, n in enumerate(counts):
        group = refs[start : start + n]
        start += n
        a, core = b % 2, c if b < 2 else 1 - c
        for j in range(3):
            total = group[0][j]
            for ref in group[1:]:
                total = total + ref[j].astype(F32)
            lane = pl.multiple_of(j * 512 + a * BLK + core * 256, BLK)
            out[:, pl.ds(lane, BLK)] = total


def assemble(ids, deps, groups):
    rows = groups[0][0].shape[1]
    counts = [len(g) for g in groups]
    args = [ref for group in groups for ref in group]
    return call_flat(
        functools.partial(assemble_kernel, counts), "assemble", ids, deps, args,
        [NEAR] * len(args), sds((rows, 1536), F32), 16, cost(0, rows * 1536 * 8),
    )


def local(
    nseq,
    ndp,
    tokens,
    cotangent,
    weight,
    forget_peep,
    reset_peep,
    forget_bias,
    reset_bias,
    norm_gain,
    norm_bias,
    lengths,
):
    axes = ("seq", "dp")
    nz = ndp // 2
    seqs, span, width = tokens.shape
    sub = span // PARTS
    q = lax.axis_index("seq").astype(jnp.int32)
    dp = lax.axis_index("dp").astype(jnp.int32)
    z, c = dp // 2, dp % 2
    ids = jnp.stack([q, z, c])

    def table(move):
        pairs = []
        for qq in range(nseq):
            for zz in range(nz):
                for cc in range(2):
                    to = move(qq, zz, cc)
                    if to is not None:
                        pairs.append((qq * ndp + zz * 2 + cc, to[0] * ndp + to[1] * 2 + to[2]))
        return pairs

    def send(value, move):
        return lax.ppermute(value, axes, table(move))

    def to_core(qq, zz, cc):
        return (qq, zz, 1 - cc)

    def to_x(qq, zz, cc):
        return (qq ^ 1, zz, cc)

    def to_y(qq, zz, cc):
        return (qq ^ 2, zz, cc)

    def shift_z(k):
        return lambda qq, zz, cc: (qq, (zz + k) % nz, cc)

    def shift_zc(k):
        return lambda qq, zz, cc: (qq, (zz + k) % nz, 1 - cc)

    def shift_q(k):
        return lambda qq, zz, cc: (qq + k, zz, cc) if 0 <= qq + k < nseq else None

    mine, theirs = split_weight(ids, weight)
    recv = send(theirs, to_core)
    nat = (seqs, PARTS, sub, width)
    tok4 = tokens.reshape(nat)
    cot4 = cotangent.reshape(nat)
    tok_oth = send(tokens, to_core).reshape(nat)
    cot_cols = jnp.concatenate(
        [lax.dynamic_slice_in_dim(cotangent, m * 512 + (1 - c) * 256, 256, 2) for m in range(4)],
        axis=2,
    )
    cot_oth = send(cot_cols, to_core).reshape(seqs, PARTS, sub, width // 2)
    len_oth = send(lengths, to_core)

    lens = jnp.stack([lengths, len_oth])
    counts = jnp.sum(lens, axis=1).astype(F32)
    scale = (seqs * span * nseq) / counts
    lim16 = (
        lens[:, :, None] - q * span - sub * jnp.arange(PARTS, dtype=jnp.int32)[None, None, :]
    ).reshape(2, 8)
    spread_rows = lambda v: jnp.broadcast_to(v, (2, STEPS, 8, BLK)).reshape(256, BLK)
    step_in_tile = jnp.arange(STEPS, dtype=jnp.int32)[None, :, None, None]
    lim = spread_rows(lim16[:, None, :, None] - step_in_tile)
    scl = spread_rows(scale[:, None, None, None])

    def by_core(vec):
        v = lax.dynamic_slice_in_dim(vec.reshape(4, 4, BLK), 2 * c, 2, 1)
        return v.transpose(1, 0, 2).reshape(1, width // 2)

    vf, vr, bfor, brst = (by_core(v) for v in (forget_peep, reset_peep, forget_bias, reset_bias))
    gain, bias = norm_gain.reshape(1, width), norm_bias.reshape(1, width)

    tail = [mine]

    def run(kernel, *head, rest=(), token=-1, after=()):
        out = kernel(*head, ids, (tail[0], *after), *rest)
        tail[0] = out[token] if isinstance(out, (list, tuple)) else out
        return out

    groups = [[cc + 2 * zz for zz in range(nz)] for cc in range(2)]

    def along_z(piece):
        if nz <= 4:
            return [send(piece, shift_z(-k)) for k in range(1, nz)]
        got = lax.all_gather(piece, "dp", axis=0, tiled=True, axis_index_groups=groups)
        n = got.shape[0] // nz
        twice = jnp.concatenate([got, got], axis=0)
        return [lax.dynamic_slice_in_dim(twice, (z + 1) * n, n * (nz - 1), 0)]

    def gather_1(s, zs):
        rel = run(plane_pieces, s, rest=(zs,))
        return rel, send(rel, to_x), send(rel, to_y)

    def gather_2(s, got):
        rel, gx, gy = got
        tox, toy = run(cross_pieces, s, rest=(gx, gy))
        return rel, gx, gy, send(tox, to_x), send(toy, to_y)

    def spread(both):
        return lax.all_gather(both, "seq")

    def run_project(s, weights, before=None, after=()):
        rest = (ub, ulo, weights, lim, vf, bfor, before)
        return run(project, s, nz, rest=rest, token=4, after=after)

    def run_states(a, fwd, got, held, after=()):
        rest = (fwd, ub, cot4, cot_oth, lim, scl, vr, brst, got, held)
        out = run(states, a, nseq, rest=rest, after=after)
        return {
            "h": out[:2], "mid": (out[2:6], out[6:10]), "dzr": out[10], "u": out[11],
            "lbs": out[12], "summ": out[13], "acc": out[14],
        }

    def run_adjoints(a, fwd, m, got, after=()):
        rest = (fwd, m["mid"], m["u"], vf, m["lbs"], got)
        du, dzc, dzf, acc = run(adjoints, a, nseq, rest=rest, after=after)
        return {"du": du, "dz": (dzc, dzf, m["dzr"]), "acc": acc}

    def sum_1(which, dz, after=()):
        own, xp, yp, da, db = run(weight_grad_part, which, nz, rest=(ubt, dz), after=after)
        return own, xp, yp, send(da, to_x), send(db, to_y)

    def sum_2(got):
        own, xp, yp, ra, rb = got
        s1, s2 = run(relay_sums, rest=(xp, yp, ra, rb))
        return own, send(s1, to_x), send(s2, to_y)

    def sum_3(got, cross):
        if nz > 4:
            own, r1, r2 = got
            total = own.astype(F32) + r1.astype(F32) + r2.astype(F32)
            total = lax.psum_scatter(
                total, "dp", scatter_dimension=1, axis_index_groups=groups, tiled=True
            )
            return [send(total, to_core) if cross else total]
        parts = list(run(plane_sums, nz, rest=got))
        if cross:
            return [send(parts[k], shift_zc(k)) for k in range(nz)]
        return parts[:1] + [send(parts[k], shift_z(k)) for k in range(1, nz)]

    def sum_4(got):
        return [run(total_of, rest=(got,))]

    last, p0, p1 = run(quarter_of, rest=(mine, recv))
    z0 = along_z(p0)
    z1 = along_z(p1)
    ub, ubt, ulo = run(norm_tokens, rest=(tok4, tok_oth, gain, bias), after=(cot_oth,))
    g0 = gather_1(0, z0)
    every = [
        [qq * ndp + zz * 2 + cc for zz in range(nz) for qq in range(nseq)] for cc in range(2)
    ]
    last = run(hand_on, rest=(last,))
    w_hi = lax.all_gather(last, axes, axis=0, tiled=True, axis_index_groups=every)
    g0 = gather_2(0, g0)
    g1 = gather_1(1, z1)
    f0 = run_project(0, (mine, recv, *g0))
    g1 = gather_2(1, g1)
    f1 = run_project(1, (mine, recv, *g1), f0[4])
    m0 = run_states(0, (f0, f1), spread(f1[4]), ())
    d0 = run_adjoints(0, (f0, f1), m0, spread(m0["summ"]))
    s0 = sum_1("other", d0["dz"])
    f2 = run_project(2, (w_hi,))
    s0 = sum_2(s0)
    f3 = run_project(3, (w_hi,), f2[4])
    got = spread(f3[4])
    s1 = sum_1("own", d0["dz"], after=(got,))
    m1 = run_states(1, (f2, f3), got, m0["h"])
    got = spread(m1["summ"])
    d1 = run_adjoints(1, (f2, f3), m1, got)
    s1 = sum_2(s1)
    s0 = sum_3(s0, True)
    s2 = sum_1("other", d1["dz"])
    s3 = sum_1("own", d1["dz"])
    s0 = sum_4(s0)
    s1 = sum_3(s1, False)
    s2 = sum_2(s2)
    parts = (d0["dz"], d1["dz"], d0["du"], d1["du"], (f0[5], f1[5], w_hi))
    dur = send(run(unit_grads, 1, rest=parts), to_core)
    s3 = sum_2(s3)
    s1 = sum_4(s1)
    s2 = sum_3(s2, True)
    own = run(unit_grads, 0, rest=parts)
    s3 = sum_3(s3, False)
    input_grad, sums = run(
        norm_grads,
        rest=(
            own, dur, tok4, cot4, lim16[0], scale[:1], gain, (m0["acc"], m1["acc"]),
            (d0["acc"], d1["acc"]),
        ),
    )
    hrcv = send(m1["h"][1], to_core)
    bit = 1
    while bit < nseq:
        sums = sums + send(sums, lambda qq, zz, cc, b=bit: (qq ^ b, zz, cc))
        bit *= 2
    bit = 1
    while bit < nz:
        sums = sums + send(sums, lambda qq, zz, cc, b=bit: (qq, zz ^ b, cc))
        bit *= 2
    sums = sums + send(sums, to_core)
    activations = run(activations_of, rest=(tok4, m1["h"][0], hrcv))
    weight_grad = run(assemble, rest=((s1, s3, s0, s2),))
    shape = tokens.shape
    return (
        activations.reshape(shape),
        input_grad.reshape(shape),
        weight_grad,
        sums[0],
        sums[1],
        sums[2],
        sums[3],
        sums[4],
        sums[5],
    )


def solution(mesh):
    whole = P("dp", "seq", None)
    in_specs = (whole, whole, P("dp", None)) + (P(),) * 6 + (P("dp"),)
    out_specs = (whole, whole, P("dp", "seq")) + (P(),) * 6
    step = functools.partial(local, mesh.shape["seq"], mesh.shape["dp"])
    return jax.shard_map(step, mesh=mesh, in_specs=in_specs, out_specs=out_specs, check_vma=False)
```

```python
import functools

import jax
import jax.numpy as jnp
from jax import lax
from jax.experimental import pallas as pl
from jax.experimental.pallas import tpu as pltpu
from jax.sharding import PartitionSpec as P

EPS = 1e-05
F32 = jnp.float32
BF = jnp.bfloat16
STEPS = 16
BLK = 128
GATES = 3
QUARTERS = 4
PARTS = 4


def params(mib, dims=1):
    return pltpu.CompilerParams(
        vmem_limit_bytes=mib * 1024 * 1024, dimension_semantics=("arbitrary",) * dims
    )


def cost(flops, bytes_accessed, transcendentals=0):
    return pl.CostEstimate(
        flops=int(flops), bytes_accessed=int(bytes_accessed), transcendentals=int(transcendentals)
    )


def sds(shape, dtype):
    return jax.ShapeDtypeStruct(shape, dtype)


def far(shape, dtype):
    return pltpu.HBM(shape, dtype)


def near(shape, dtype):
    return pltpu.VMEM(shape, dtype)


def far_in(*values):
    return [pltpu.with_memory_space_constraint(v, pltpu.HBM) for v in values]


def near_in(*values):
    return [pltpu.with_memory_space_constraint(v, pltpu.VMEM) for v in values]


ANY = pl.BlockSpec(memory_space=pl.ANY)
NEAR = pl.BlockSpec(memory_space=pltpu.VMEM)
SMEM = pl.BlockSpec(memory_space=pltpu.SMEM)


def ordered(kernel, deps):
    n = len(deps)

    def body(ids, *refs):
        return kernel(ids, *refs[n:])

    return body, list(deps), [ANY] * n


def call(kernel, name, grid, ids, deps, args, in_specs, out_specs, out_shape, mib, est, scratch=()):
    body, deps, dep_specs = ordered(kernel, deps)
    return pl.pallas_call(
        body,
        grid_spec=pltpu.PrefetchScalarGridSpec(
            num_scalar_prefetch=1,
            grid=grid,
            in_specs=dep_specs + in_specs,
            out_specs=out_specs,
            scratch_shapes=list(scratch),
        ),
        out_shape=out_shape,
        compiler_params=params(mib, len(grid)),
        cost_estimate=est,
        name=name,
    )(ids, *deps, *args)


def call_flat(kernel, name, ids, deps, args, in_specs, out_shape, mib, est, scratch=(), out_specs=None, aliases=None):
    body, deps, dep_specs = ordered(kernel, deps)
    many = isinstance(out_shape, (list, tuple))
    if out_specs is None:
        out_specs = [NEAR] * len(out_shape) if many else NEAR
    shift = 1 + len(deps)
    return pl.pallas_call(
        body,
        in_specs=[SMEM] + dep_specs + in_specs,
        out_specs=out_specs,
        out_shape=out_shape,
        scratch_shapes=list(scratch),
        input_output_aliases={k + shift: v for k, v in (aliases or {}).items()},
        compiler_params=pltpu.CompilerParams(vmem_limit_bytes=mib * 1024 * 1024),
        cost_estimate=est,
        name=name,
    )(ids, *deps, *args)


def split_kernel(ids, w, mine, theirs):
    c = ids[2]
    for s in range(4):
        a, mp = divmod(s, 2)
        for g in range(GATES):
            for mm in range(2):
                dst = s * 768 + g * 256 + mm * BLK
                base = g * 2048 + (2 * mp + mm) * 512 + a * BLK
                here = pl.multiple_of(base + c * 256, BLK)
                there = pl.multiple_of(base + (1 - c) * 256, BLK)
                mine[:, dst : dst + BLK] = w[:, pl.ds(here, BLK)]
                theirs[:, dst : dst + BLK] = w[:, pl.ds(there, BLK)]


def split_weight(ids, weight):
    rows, cols = weight.shape
    tile = rows // 2
    spec = pl.BlockSpec((tile, cols // 2), lambda i, ids: (i, 0))
    return call(
        split_kernel, "split_weight", (2,), ids, (), far_in(weight),
        [pl.BlockSpec((tile, cols), lambda i, ids: (i, 0))], [spec, spec],
        [sds((rows, cols // 2), BF)] * 2, 16, cost(0, rows * cols * 4),
    )


def quarter_kernel(ids, mine, recv, out, p0):
    q, c = ids[0], ids[2]
    half = out.shape[0]
    at = pl.ds(pl.multiple_of(lax.rem(q, 2) * half, half), half)
    first = (lax.div(q, 2) == c).astype(jnp.int32) == 1
    val = jnp.where(first, mine[at, :], recv[at, :])
    out[...] = val[:, 1536:]
    p0[...] = val[:, :1536]


def quarter_of(ids, deps, mine, recv):
    rows, cols = mine.shape
    half = rows // 2
    return call_flat(
        quarter_kernel, "quarter_of", ids, deps, [mine, recv], [NEAR, NEAR],
        [sds((half, 1536), BF)] * 2, 8,
        cost(0, rows * cols * 4),
    )


def copy_kernel(ids, src, dst):
    dst[...] = src[...]


def hand_on(ids, deps, value):
    return call_flat(
        copy_kernel, "hand_on", ids, deps, [value], [NEAR], sds(value.shape, value.dtype), 16,
        cost(0, value.size * 4),
    )


def gate_kernel(ids, *refs):
    pass


def gate(ids, deps, values, hold=None):
    shape = {None: sds, "far": far, "near": near}[hold]
    held = {None: lambda *v: list(v), "far": far_in, "near": near_in}[hold]
    return call_flat(
        gate_kernel, "gate", ids, deps, held(*values), [ANY] * len(values),
        [shape(v.shape, v.dtype) for v in values], 4, cost(0, 1), out_specs=[ANY] * len(values),
        aliases={n: n for n in range(len(values))},
    )


def add_kernel(ids, *refs):
    total = refs[0][...]
    for ref in refs[1:-1]:
        total = total + ref[...]
    refs[-1][...] = total


def add_up(ids, deps, *values):
    a = values[0]
    return call_flat(
        add_kernel, "add_up", ids, deps, list(values), [NEAR] * len(values), sds(a.shape, a.dtype),
        4, cost(a.size, a.size * 4 * len(values)),
    )


def plane_kernel(s, ids, *refs):
    rel = refs[-1]
    row = 0
    for ref in refs[:-1]:
        rel[row : row + ref.shape[0], :] = ref[:, s * 768 : (s + 1) * 768]
        row += ref.shape[0]


def plane_pieces(s, ids, deps, parts):
    rows = sum(p.shape[0] for p in parts)
    return call_flat(
        functools.partial(plane_kernel, s), f"plane_pieces_{s}", ids, deps, list(parts),
        [NEAR] * len(parts), sds((rows, 768), BF), 8, cost(0, rows * 768 * 4),
    )


def cross_kernel(ids, gx, gy, tox, toy):
    tox[...] = gy[:, :384]
    toy[...] = gx[:, 384:]


def cross_pieces(s, ids, deps, gx, gy):
    rows = gx.shape[0]
    return call_flat(
        cross_kernel, f"cross_pieces_{s}", ids, deps, [gx, gy], [NEAR, NEAR],
        [sds((rows, 384), BF)] * 2, 16, cost(0, rows * 768 * 4),
    )


def norm_of(x):
    mean = jnp.mean(x, axis=-1, keepdims=True)
    centered = x - mean
    var = jnp.mean(centered * centered, axis=-1, keepdims=True)
    rstd = lax.rsqrt(var + EPS)
    return centered * rstd, rstd


def norm_kernel(ids, own, other, gain, bias, ub, ubt, ulo, scr):
    c = ids[2]
    seqs = own.shape[0]
    for k, ref in enumerate((own, other)):
        for st in range(8):
            sq, h = divmod(st, PARTS)
            normed, _ = norm_of(ref[sq, h].astype(F32))
            unit = normed * gain[...] + bias[...]
            for j in range(scr.shape[0]):
                scr[j, pl.ds(k * 128 + st, STEPS, stride=8), :] = unit[:, j * BLK : (j + 1) * BLK]
    for j in range(scr.shape[0]):
        low = scr[j].astype(BF)
        ub[0, :, :, j * BLK : (j + 1) * BLK] = low.reshape(2, 128, BLK)
        ubt[j * BLK : (j + 1) * BLK, :] = low.T
    for a in range(2):
        for m in range(QUARTERS):
            unit = scr[m * 4 + a + 2 * c]
            rest = (unit - unit.astype(BF).astype(F32)).astype(BF)
            dst = (a * QUARTERS + m) * BLK
            ulo[0, :, :, dst : dst + BLK] = rest.reshape(2, 128, BLK)


def tile_block(cols):
    return pl.BlockSpec((1, 2, 128, cols), lambda i, ids: (i, 0, 0, 0))


def norm_tokens(ids, deps, own, other, gain, bias):
    seqs, parts, steps, width = own.shape
    rows = seqs * parts * steps
    tiles = steps // STEPS
    nat = pl.BlockSpec((seqs, parts, STEPS, width), lambda i, ids: (0, 0, i, 0))
    vec = pl.BlockSpec((1, width), lambda i, ids: (0, 0))
    return call(
        norm_kernel, "norm_tokens", (tiles,), ids, deps, [*far_in(own, other), gain, bias],
        [nat, nat, vec, vec],
        [
            tile_block(width),
            pl.BlockSpec((width, 256), lambda i, ids: (0, i)),
            tile_block(width // 2),
        ],
        [
            far((tiles, 2, 128, width), BF),
            far((width, 2 * rows), BF),
            far((tiles, 2, 128, width // 2), BF),
        ],
        20, cost(rows * width * 20, rows * width * 14),
        scratch=[pltpu.VMEM((width // BLK, 256, BLK), F32)],
    )


def flat(ref):
    value = ref[...]
    return value.reshape(256, value.shape[-1])


def core_lane(a, m, c):
    return pl.multiple_of(m * 512 + a * BLK + c * 256, BLK)


def pairs():
    for tp in range(STEPS // 2):
        for k in range(2):
            yield k, tp * 16, k * 128 + tp * 16


def live_pair(lim, row, tile):
    live = lim[row : row + 16, :] > tile * STEPS
    return jnp.concatenate([live, live], axis=1)


def fold_streams(pr, lc, ahead):
    out = []
    order = range(PARTS) if ahead else range(PARTS - 1, -1, -1)
    for sq in range(2):
        tp = tl = None
        for h in order:
            n = sq * PARTS + h
            p, l = pr[n : n + 1], lc[n : n + 1]
            tp, tl = (p, l) if tp is None else ((p * tp, p * tl + l) if ahead else (p * tp, l + p * tl))
        out.append((tp, tl))
    return out


def proj_kernel(s, nz, joined, ids, ub, ulo, *rest):
    n_w = 1 if joined else 7
    weights, rest = rest[:n_w], rest[n_w:]
    lim, vf, bfor = rest[:3]
    rest = rest[3:]
    before = rest[0] if s % 2 else None
    cand, decay, rpre, plout, summ = rest[s % 2 : s % 2 + 5]
    rest = rest[s % 2 + 5 :]
    if joined:
        zbuf, prod, loc, wbuf, sems = rest
    else:
        wall, zbuf, prod, loc, wbuf, sems = rest
    tiles = cand.shape[0]
    width = wbuf.shape[0]
    q, z, c = ids[0], ids[1], ids[2]
    a, mp = divmod(s, 2)
    cols = slice(mp * 768, mp * 768 + 768)
    copies = []

    def put(src, row, rows, lo=0, hi=768):
        dst = wbuf.at[pl.ds(row, rows), lo:hi]
        copy = pltpu.make_async_copy(src, dst, sems.at[len(copies)])
        copy.start()
        copies.append(copy)

    if joined:
        put(weights[0].at[:, cols], 0, width)
    else:
        mine, recv, rel, gx, gy, dx, dy = weights
        zb = width // nz
        zb2, qb = zb // 2, zb // 4
        mult = lambda v: pl.multiple_of(v, qb)
        put(mine.at[:, s * 768 : (s + 1) * 768], mult(z * zb + c * zb2), zb2)
        put(recv.at[:, s * 768 : (s + 1) * 768], mult(z * zb + (1 - c) * zb2), zb2)
        for r in range(1, nz):
            base = lax.rem(z + r, nz) * zb
            lo, hi = (r - 1) * qb, r * qb
            put(rel.at[lo:hi, :], mult(base + q * qb), qb)
            put(gx.at[lo:hi, :], mult(base + (q ^ 1) * qb), qb)
            put(gy.at[lo:hi, :], mult(base + (q ^ 2) * qb), qb)
            put(dx.at[lo:hi, :], mult(base + (q ^ 3) * qb), qb, 0, 384)
            put(dy.at[lo:hi, :], mult(base + (q ^ 3) * qb), qb, 384, 768)
    for copy in copies:
        copy.wait()
    if not joined:
        keep = pltpu.make_async_copy(wbuf, wall, sems.at[len(copies)])
        keep.start()
    prod[...] = jnp.ones_like(prod)
    loc[...] = jnp.zeros_like(loc)

    def tile(ubr, ulor):
        i = pl.program_id(0)
        zbuf[:, :768] = jnp.dot(flat(ubr), wbuf[...], preferred_element_type=F32)
        low = flat(ulor).astype(F32)
        for mm in range(2):
            high = ubr[:, :, :, pl.ds(core_lane(a, 2 * mp + mm, c), BLK)].reshape(256, BLK)
            zbuf[:, 768 + mm * BLK : 768 + (mm + 1) * BLK] = (
                high.astype(F32) + low[:, mm * BLK : (mm + 1) * BLK]
            )
        pr = [prod[0:8, :], prod[8:16, :]]
        lc = [loc[0:8, :], loc[8:16, :]]
        for k, r0, row in pairs():
            cd = zbuf[row : row + 16, :256]
            logit = zbuf[row : row + 16, 256:512] + vf[...] * zbuf[row : row + 16, 768:] + bfor[...]
            dec = jnp.where(live_pair(lim, row, i), jax.nn.sigmoid(logit), 1.0)
            inj = (1.0 - dec) * cd
            cand[i, k, r0 : r0 + 16, :] = cd
            decay[i, k, r0 : r0 + 16, :] = dec
            rpre[i, k, r0 : r0 + 16, :] = zbuf[row : row + 16, 512:768]
            for t in range(2):
                d = dec[t * 8 : t * 8 + 8]
                lc[k] = d * lc[k] + inj[t * 8 : t * 8 + 8]
                pr[k] = d * pr[k]
        for k in range(2):
            prod[k * 8 : k * 8 + 8, :] = pr[k]
            loc[k * 8 : k * 8 + 8, :] = lc[k]

    pltpu.emit_pipeline(
        tile,
        grid=(tiles,),
        in_specs=[
            pl.BlockSpec((1, 2, 128, width), lambda i: (i, 0, 0, 0)),
            pl.BlockSpec((1, 2, 128, 256), lambda i: (i, 0, 0, s)),
        ],
    )(ub, ulo)
    if s % 2:
        summ[0] = before[0]
    plout[0:16, :] = prod[...]
    plout[16:32, :] = loc[...]
    for k in range(2):
        pr, lc = prod[k * 8 : k * 8 + 8, :], loc[k * 8 : k * 8 + 8, :]
        for sq, (tp, tl) in enumerate(fold_streams(pr, lc, True)):
            ks = k * 2 + sq
            summ[s % 2, ks : ks + 1, :] = tp
            summ[s % 2, 4 + ks : 5 + ks, :] = tl
    if not joined:
        keep.wait()


def project(s, nz, ids, deps, ub, ulo, weights, lim, vf, bfor, before):
    tiles, _, _, width = ub.shape
    joined = len(weights) == 1
    shape = (tiles, 2, 128, 256)
    rows = tiles * 256
    chan = slice(s * 256, s * 256 + 256)
    args = far_in(ub, ulo, *weights) + [lim, vf[:, chan], bfor[:, chan]]
    in_specs = [ANY] * (2 + len(weights)) + [NEAR] * 3
    if s % 2:
        args.append(before)
        in_specs.append(NEAR)
    out_shape = [near(shape, F32)] * 3 + [near((32, 256), F32), near((2, 8, 256), F32)]
    out_specs = [NEAR] * 5
    if not joined:
        out_shape.append(far((width, 768), BF))
        out_specs.append(ANY)
    return call_flat(
        functools.partial(proj_kernel, s, nz, joined), f"project_{s}", ids, deps, args, in_specs,
        out_shape, 12, cost(2 * rows * width * 768, rows * width * 2 + width * 768 * 4),
        scratch=[
            pltpu.VMEM((256, 1024), F32),
            pltpu.VMEM((16, 256), F32),
            pltpu.VMEM((16, 256), F32),
            pltpu.VMEM((width, 768), BF),
            pltpu.SemaphoreType.DMA((3 + 5 * (nz - 1),)),
        ],
        out_specs=out_specs,
    )


def halves(v):
    return v[:8], v[8:]


def enter(got, n, ahead, q, count):
    value = jnp.zeros((4, 256), F32)
    for j in range(count) if ahead else range(count - 1, -1, -1):
        used = (j < q) if ahead else (j > q)
        longer = got[j, n, 4:8, :] + got[j, n, 0:4, :] * value
        value = jnp.where(used, longer, value)
    return value


def state_kernel(a, count, held, ids, *refs):
    fwd = (refs[0:4], refs[4:8])
    ub, ulo, cot_own, cot_oth, lim, scl, vr, br, got = refs[8:17]
    rest = refs[17 + (2 if held else 0) :]
    hown, hoth = rest[:2]
    out = (rest[2:5], rest[5:8])
    dzr, uu, lbs, summ, acc, st, pp, lb, ac, scr = rest[8:]
    tiles = dzr.shape[0]
    q, c = ids[0], ids[2]
    for n in range(2):
        cand, decay, rpre, plin = fwd[n]
        bc, dstate, du0 = out[n]
        lanes = slice(n * 256, n * 256 + 256)
        carry = enter(got, n, True, q, count)
        for ks in range(4):
            cc = carry[ks : ks + 1]
            for h in range(PARTS):
                m = ks * PARTS + h
                st[m : m + 1, :] = cc
                cc = plin[m : m + 1, :] * cc + plin[16 + m : 17 + m, :]
        pp[...] = jnp.ones_like(pp)
        lb[...] = jnp.zeros_like(lb)
        ac[...] = jnp.zeros_like(ac)

        def tile(u0, u1, ul, own0, own1, oth0, oth1, ho, ht):
            i = pl.program_id(0)
            for k, pair in enumerate(((own0, own1), (oth0, oth1))):
                for b, ref in enumerate(pair):
                    for m in range(8):
                        sq, h = divmod(m, PARTS)
                        scr[b, pl.ds(k * 128 + m, STEPS, stride=8), :] = ref[sq, h].astype(F32)
            cur = [st[0:8, :], st[8:16, :]]
            p = [pp[0:8, :], pp[8:16, :]]
            l = [lb[0:8, :], lb[8:16, :]]
            peep = [jnp.zeros((8, 256), F32)] * 2
            bias = [jnp.zeros((8, 256), F32)] * 2
            wr, wb = vr[:, lanes], br[:, lanes]
            for k, r0, row in pairs():
                at = slice(r0, r0 + 16)
                dec = decay[i, k, at, :]
                cd = cand[i, k, at, :]
                inj = (1.0 - dec) * cd
                befores, states = [], []
                for d, v in zip(halves(dec), halves(inj)):
                    befores.append(cur[k])
                    cur[k] = d * cur[k] + v
                    states.append(cur[k])
                before = jnp.concatenate(befores, axis=0)
                state = jnp.concatenate(states, axis=0)
                low = jnp.concatenate([u0[0, k, at, :], u1[0, k, at, :]], axis=1)
                uu[i, k, at, lanes] = low
                u = low.astype(F32) + ul[0, k, at, :].astype(F32)
                live = lim[row : row + 16, :] > i * STEPS
                sc = jnp.where(live, scl[row : row + 16, :], 0.0)
                gy = jnp.concatenate(
                    [scr[0, row : row + 16, :] * sc, scr[1, row : row + 16, :] * sc], axis=1
                )
                r = jax.nn.sigmoid(rpre[i, k, at, :] + wr * before + wb)
                gap = state - u
                hv = jnp.where(jnp.concatenate([live, live], axis=1), u + r * gap, 0.0).astype(BF)
                href = ht if k else ho
                href[0, 0, at, :] = hv[:, :BLK]
                href[0, 1, at, :] = hv[:, BLK:]
                ds = gy * r
                drl = ds * (1.0 - r) * gap
                sr = dec * ds + wr * drl
                dstate[i, k, at, :] = ds
                bc[i, k, at, :] = before - cd
                du0[i, k, at, :] = (gy - ds).astype(BF)
                dzr[i, k, at, lanes] = drl.astype(BF)
                for d, v in zip(halves(dec), halves(sr)):
                    l[k] = l[k] + p[k] * v
                    p[k] = p[k] * d
                for e, w in zip(halves(drl), befores):
                    peep[k] = peep[k] + e * w
                    bias[k] = bias[k] + e
            for k in range(2):
                st[k * 8 : k * 8 + 8, :] = cur[k]
                pp[k * 8 : k * 8 + 8, :] = p[k]
                lb[k * 8 : k * 8 + 8, :] = l[k]
            ac[0:8, :] += peep[0] + peep[1]
            ac[8:16, :] += bias[0] + bias[1]

        nat = cot_own.shape[:2]

        def unit(mm):
            return pl.BlockSpec(
                (1, 2, 128, BLK), lambda i: (i, 0, 0, (2 * n + mm) * 4 + 2 * c + a)
            )

        def tail():
            return pl.BlockSpec((1, 2, 128, 256), lambda i: (i, 0, 0, 2 * a + n))

        def nat_own(mm):
            return pl.BlockSpec(
                (*nat, STEPS, BLK), lambda i: (0, 0, i, (2 * n + mm) * 4 + 2 * c + a)
            )

        def nat_oth(mm):
            return pl.BlockSpec((*nat, STEPS, BLK), lambda i: (0, 0, i, (2 * n + mm) * 2 + a))

        hspec = pl.BlockSpec((1, 2, 128, BLK), lambda i: (2 * a + n, 0, i, 0))
        pltpu.emit_pipeline(
            tile,
            grid=(tiles,),
            in_specs=[unit(0), unit(1), tail(), nat_own(0), nat_own(1), nat_oth(0), nat_oth(1)],
            out_specs=[hspec, hspec],
        )(ub, ub, ulo, cot_own, cot_own, cot_oth, cot_oth, hown, hoth)
        acc[n] = ac[...]
        lbs[n] = lb[...]
        for k in range(2):
            p, l = pp[k * 8 : k * 8 + 8, :], lb[k * 8 : k * 8 + 8, :]
            for sq, (tp, tl) in enumerate(fold_streams(p, l, False)):
                ks = k * 2 + sq
                summ[n, ks : ks + 1, :] = tp
                summ[n, 4 + ks : 5 + ks, :] = tl


def states(a, count, ids, deps, fwd, ub, ulo, cot_own, cot_oth, lim, scl, vr, br, got, held):
    tiles = ub.shape[0]
    rows = tiles * 128
    one = (tiles, 2, 128, 256)
    two = (tiles, 2, 128, 512)
    chan = slice(a * 512, a * 512 + 512)
    args, in_specs = [], []
    for f in fwd:
        args += near_in(*f[:3]) + [f[3]]
        in_specs += [NEAR] * 4
    args += far_in(ub, ulo, cot_own, cot_oth) + [lim, scl, vr[:, chan], br[:, chan], got]
    in_specs += [ANY] * 4 + [NEAR] * 5
    aliases = {}
    if held:
        aliases = {len(args): 0, len(args) + 1: 1}
        args += far_in(*held)
        in_specs += [ANY] * 2
    small = near((2, 16, 256), F32)
    return call_flat(
        functools.partial(state_kernel, a, count, bool(held)), f"states_{a}", ids, deps, args,
        in_specs,
        [far((4, 2, rows, BLK), BF)] * 2
        + [near(one, F32), near(one, F32), near(one, BF)] * 2
        + [near(two, BF)] * 2
        + [small, near((2, 8, 256), F32), small],
        10, cost(rows * 1024 * 60, rows * 1024 * 10, rows * 1024 * 2),
        scratch=[pltpu.VMEM((16, 256), F32)] * 4 + [pltpu.VMEM((2, 256, BLK), F32)],
        out_specs=[ANY] * 2 + [NEAR] * 11,
        aliases=aliases,
    )


def adjoint_kernel(count, ids, *refs):
    ins = (refs[0:5], refs[5:10])
    dzr, uu, vf, vr, lbs, got, du, dzc, dzf, acc, adj = refs[10:]
    tiles = du.shape[0]
    q = ids[0]
    for n in range(2):
        decay, bc, dstate, du0, plin = ins[n]
        lanes = slice(n * 256, n * 256 + 256)
        wf, wr = vf[:, lanes], vr[:, lanes]
        after = enter(got, n, False, q, count)
        for ks in range(4):
            cc = after[ks : ks + 1]
            for h in range(PARTS - 1, -1, -1):
                m = ks * PARTS + h
                adj[m : m + 1, :] = cc
                cc = lbs[n, m : m + 1, :] + plin[m : m + 1, :] * cc

        def tile(step, state):
            i = tiles - 1 - step
            cur, peep, bias = [state[0], state[1]], state[2], state[3]
            for k, r0, _ in reversed(list(pairs())):
                at = slice(r0, r0 + 16)
                dec = decay[i, k, at, :]
                ds = dstate[i, k, at, :]
                sr = dec * ds + wr * dzr[i, k, at, lanes].astype(F32)
                late = ds[8:] + cur[k]
                cur[k] = dec[8:] * cur[k] + sr[8:]
                early = ds[:8] + cur[k]
                cur[k] = dec[:8] * cur[k] + sr[:8]
                dcand = jnp.concatenate([early, late], axis=0) * (1.0 - dec)
                dfl = dcand * bc[i, k, at, :] * dec
                dzc[i, k, at, lanes] = dcand.astype(BF)
                dzf[i, k, at, lanes] = dfl.astype(BF)
                du[i, k, at, lanes] = (du0[i, k, at, :].astype(F32) + dfl * wf).astype(BF)
                w = dfl * uu[i, k, at, lanes].astype(F32)
                peep = peep + (w[:8] + w[8:])
                bias = bias + (dfl[:8] + dfl[8:])
            return cur[0], cur[1], peep, bias

        zero = jnp.zeros((8, 256), F32)
        end = lax.fori_loop(0, tiles, tile, (adj[0:8, :], adj[8:16, :], zero, zero))
        acc[n, 0:8, :] = end[2]
        acc[n, 8:16, :] = end[3]


def adjoints(a, count, ids, deps, fwd, mid, dzr, uu, vf, vr, lbs, got):
    tiles = uu.shape[0]
    rows = tiles * 128
    shape = (tiles, 2, 128, 512)
    args = []
    for f, m in zip(fwd, mid):
        args += near_in(f[1], *m) + [f[3]]
    chan = slice(a * 512, a * 512 + 512)
    args += near_in(dzr, uu) + [vf[:, chan], vr[:, chan], lbs, got]
    return call_flat(
        functools.partial(adjoint_kernel, count), f"adjoints_{a}", ids, deps, args,
        [NEAR] * len(args),
        [near(shape, BF)] * 3 + [near((2, 16, 256), F32)],
        6, cost(rows * 1024 * 20, rows * 1024 * 4), scratch=[pltpu.VMEM((16, 256), F32)],
    )


def wgrad_kernel(which, nz, n_kept, ids, ubt, dzc, dzf, dzr, *rest):
    kept, rest = rest[: max(n_kept - 3, 0)], rest[max(n_kept - 3, 0) :]
    own, xp, yp, da, db = rest[:5]
    scr, sems = rest[5 + n_kept :]
    copies = [
        pltpu.make_async_copy(src, dst, sems.at[n])
        for n, (src, dst) in enumerate(zip((dzc, dzf, dzr, *kept), rest[5 : 5 + n_kept]))
    ]
    for copy in copies:
        copy.start()
    q, c = ids[0], ids[2]
    rh = 1 - c if which == "other" else c
    half = scr.shape[0]
    rows = ubt.shape[1]

    def tile(lhs):
        i = pl.program_id(0)
        for g, dz in enumerate((dzc, dzf, dzr)):
            rhs = dz[...].reshape(rows, 512)
            scr[:, g * 512 : (g + 1) * 512] = jnp.dot(
                lhs[...], rhs, preferred_element_type=F32
            ).astype(BF)

        def block(r, j):
            return scr[:, pl.ds(pl.multiple_of(((q ^ r) * 3 + j) * BLK, BLK), BLK)]

        at = pl.ds(pl.multiple_of(i * half, half), half)
        for j in range(3):
            own[j, at, :] = block(0, j)
            xp[j, at, :] = block(1, j)
            yp[j, at, :] = block(2, j)

        @pl.when(i < nz // 2)
        def _():
            for j in range(3):
                da[j, at, :] = block(3, j)

        @pl.when(i >= nz // 2)
        def _():
            back = pl.ds(pl.multiple_of((i - nz // 2) * half, half), half)
            for j in range(3):
                db[j, back, :] = block(3, j)

    pltpu.emit_pipeline(
        tile, grid=(nz,), in_specs=[pl.BlockSpec((half, rows), lambda i: (2 * i + rh, 0))]
    )(ubt)
    for copy in copies:
        copy.wait()


def weight_grad_part(which, nz, ids, deps, ubt, dz, keep=()):
    width, rows = ubt.shape
    half = width // nz // 2
    kept = (*dz, *keep) if keep else ()
    return call_flat(
        functools.partial(wgrad_kernel, which, nz, len(kept)), "weight_grad_part", ids, deps,
        [*far_in(ubt), *near_in(*dz, *keep)], [ANY] + [NEAR] * (3 + len(keep)),
        [sds((3, nz * half, BLK), BF)] * 3
        + [sds((3, nz * half // 2, BLK), BF)] * 2
        + [far(v.shape, v.dtype) for v in kept],
        10, cost(2 * rows * nz * half * 1536, rows * width + width * 1536),
        scratch=[pltpu.VMEM((half, 1536), BF), pltpu.SemaphoreType.DMA((4,))],
        out_specs=[NEAR] * 5 + [ANY] * len(kept),
    )


def relay_kernel(ids, xp, yp, ra, rb, s1, s2):
    half = ra.shape[1]
    s1[:, :half, :] = xp[:, :half, :]
    s1[:, half:, :] = (xp[:, half:, :].astype(F32) + rb[...].astype(F32)).astype(BF)
    s2[:, :half, :] = (yp[:, :half, :].astype(F32) + ra[...].astype(F32)).astype(BF)
    s2[:, half:, :] = yp[:, half:, :]


def relay_sums(ids, deps, xp, yp, ra, rb):
    rows = xp.shape[1]
    return call_flat(
        relay_kernel, "relay_sums", ids, deps, [xp, yp, ra, rb], [NEAR] * 4,
        [sds(xp.shape, BF)] * 2, 16, cost(rows * 768, rows * 384 * 10),
    )


def plane_sum_kernel(nz, ids, own, r1, r2, *outs):
    rows = outs[0].shape[1]
    for k, out in enumerate(outs):
        start = lax.rem(ids[1] + k, nz) * rows
        at = pl.ds(pl.multiple_of(start, rows), rows)
        tot = own[:, at, :].astype(F32) + r1[:, at, :].astype(F32) + r2[:, at, :].astype(F32)
        out[...] = tot.astype(out.dtype)


def plane_sums(nz, ids, deps, own, r1, r2):
    rows = own.shape[1] // nz
    return call_flat(
        functools.partial(plane_sum_kernel, nz), "plane_sums", ids, deps, [own, r1, r2], [NEAR] * 3,
        [sds((3, rows, BLK), F32)] + [sds((3, rows, BLK), BF)] * (nz - 1), 16,
        cost(rows * 768 * nz, rows * 384 * 8 * nz),
    )


def fold_kernel(sets, d, ids, *refs):
    n = sum(len(g) for g in sets) if sets else 2
    srcs, outs = refs[:n], refs[n:]
    if sets:
        groups, at = [], 0
        for g in sets:
            groups.append(srcs[at : at + len(g)])
            at += len(g)
    else:
        groups = [[ref.at[g] for ref in srcs] for g in range(srcs[0].shape[0])]
    half = groups[0][0].shape[1] // 2
    bit = lax.rem(lax.div(ids[1], d), 2) if d else 0
    for g, parts in enumerate(groups):
        spots = ((outs[0], bit), (outs[1], 1 - bit)) if d else ((outs[g], None),)
        for out, where in spots:
            rows = slice(None) if where is None else pl.ds(pl.multiple_of(where * half, half), half)
            total = parts[0][:, rows, :].astype(F32)
            for part in parts[1:]:
                total = total + part[:, rows, :].astype(F32)
            if d:
                out[g] = total.astype(out.dtype)
            else:
                out[...] = total


def fold_z(d, ids, deps, sets):
    stacked = not isinstance(sets[0], (list, tuple))
    args = list(sets) if stacked else [v for g in sets for v in g]
    count = sets[0].shape[0] if stacked else len(sets)
    _, rows, _ = args[0].shape[-3:]
    if d:
        shape = (count, 3, rows // 2, BLK)
        out_shape = [sds(shape, F32), sds(shape, BF)]
    else:
        out_shape = [sds((3, rows, BLK), F32)] * count
    return call_flat(
        functools.partial(fold_kernel, None if stacked else [tuple(g) for g in sets], d), "fold_z",
        ids, deps, args, [NEAR] * len(args), out_shape, 8,
        cost(rows * 768 * count, rows * 384 * 10 * count),
    )


DIMS = (((1,), (1,)), ((), ()))
TILE_N = 512


def unit_kernel(k, ids, *refs):
    first, second, ws = refs[0:4], refs[4:8], refs[8:11]
    far_out, out, lhs, e0, wbuf, sems, wsems, osems = refs[12 if k == 0 else 11 :]
    c = ids[2]
    rows = out.shape[0]
    tiles = ws[0].shape[0] // TILE_N

    def fetch(m):
        slot, lane, copies = m % 2, 0, []
        for n, w in enumerate(ws):
            cols = w.shape[1]
            dst = wbuf.at[slot, :, lane : lane + cols]
            src = w.at[m * TILE_N : (m + 1) * TILE_N, :]
            copies.append(pltpu.make_async_copy(src, dst, wsems.at[slot, n]))
            lane += cols
        return copies

    copies = [(first[3].at[:, k], e0)]
    for mp in range(2):
        for g, ref in enumerate(first[:3]):
            dst = mp * 768 + g * 256
            src = ref.at[:, k, :, mp * 256 : (mp + 1) * 256]
            copies.append((src, lhs.at[:, :, dst : dst + 256]))
    copies = [pltpu.make_async_copy(a, b, sems.at[n]) for n, (a, b) in enumerate(copies)]
    for copy in copies + fetch(0):
        copy.start()
    for mp in range(2):
        for g, ref in enumerate(second[:3]):
            dst = 1536 + mp * 768 + g * 256
            lhs[:, :, dst : dst + 256] = ref[:, k, :, mp * 256 : (mp + 1) * 256]
    for copy in copies:
        copy.wait()
    moved = []
    for m in range(tiles):
        if m + 1 < tiles:
            for copy in fetch(m + 1):
                copy.start()
        for copy in fetch(m):
            copy.wait()
        lo = m * TILE_N
        left = lhs[...].reshape(rows, 3072)
        acc = lax.dot_general(left, wbuf[m % 2], DIMS, preferred_element_type=F32)
        out[:, lo : lo + TILE_N] = acc.astype(out.dtype)
        cols = slice(m * BLK, (m + 1) * BLK)
        for a, val in enumerate((e0[:, :, cols], second[3][:, k, :, cols])):
            lane = pl.ds(pl.multiple_of(lo + a * BLK + c * 256, BLK), BLK)
            total = out[:, lane].astype(F32) + val.reshape(rows, BLK).astype(F32)
            out[:, lane] = total.astype(out.dtype)
        slot = 1 - c if k else c
        done = pltpu.make_async_copy(
            out.at[:, lo : lo + TILE_N], far_out.at[slot, :, lo : lo + TILE_N], osems.at[m]
        )
        done.start()
        moved.append(done)
    for done in moved:
        done.wait()


def unit_grads(k, ids, deps, first, second, ws, held):
    tiles = first[0].shape[0]
    rows, width = tiles * 128, ws[0].shape[0]
    args = [*far_in(*first), *near_in(*second), *far_in(*ws)]
    return call_flat(
        functools.partial(unit_kernel, k), f"unit_grads_{k}", ids, deps, args + far_in(*held),
        [ANY] * 4 + [NEAR] * 4 + [ANY] * (3 + len(held)),
        far((2, rows, width), BF), 24, cost(2 * rows * width * 3072, width * 3072 * 2),
        scratch=[
            pltpu.VMEM((rows, width), BF),
            pltpu.VMEM((tiles, 128, 3072), BF),
            pltpu.VMEM((tiles, 128, 512), BF),
            pltpu.VMEM((2, TILE_N, 3072), BF),
            pltpu.SemaphoreType.DMA((7,)),
            pltpu.SemaphoreType.DMA((2, 3)),
            pltpu.SemaphoreType.DMA((width // TILE_N,)),
        ],
        out_specs=ANY, aliases={len(args): 0} if held else {},
    )


def norm_grad_kernel(ids, du2, tok, cot, lim, scl, gain, *rest):
    accb, accc = rest[:2], rest[2:4]
    out, sums, ga, ba, scr = rest[4:]
    c = ids[2]
    ga[...] = jnp.zeros_like(ga)
    ba[...] = jnp.zeros_like(ba)

    def tile(dur, tokr, cotr, outr):
        i = pl.program_id(0)
        for j in range(scr.shape[0]):
            lanes = slice(j * BLK, (j + 1) * BLK)
            scr[j] = dur[0, :, lanes].astype(F32) + dur[1, :, lanes].astype(F32)
        step = lax.broadcasted_iota(jnp.int32, (STEPS, 1), 0) + i * STEPS
        gsum = jnp.zeros(ga.shape, F32)
        bsum = jnp.zeros(ba.shape, F32)
        for st in range(8):
            sq, h = divmod(st, PARTS)
            x16 = tokr[sq, h].astype(F32)
            c16 = cotr[sq, h].astype(F32)
            for part in range(2):
                cut = slice(part * 8, part * 8 + 8)
                du = jnp.concatenate(
                    [scr[j, pl.ds(st + part * 64, 8, stride=8), :] for j in range(scr.shape[0])],
                    axis=1,
                )
                normed, rstd = norm_of(x16[cut])
                dn = du * gain[...]
                m1 = jnp.mean(dn, axis=-1, keepdims=True)
                m2 = jnp.mean(dn * normed, axis=-1, keepdims=True)
                gy = jnp.where(step[cut] < lim[st], c16[cut] * scl[0], 0.0)
                outr[sq, h, cut, :] = rstd * (dn - m1 - normed * m2) + gy
                gsum = gsum + du * normed
                bsum = bsum + du
        ga[...] += gsum
        ba[...] += bsum

    seqs, parts, steps, width = tok.shape
    nat = pl.BlockSpec((seqs, parts, STEPS, width), lambda i: (0, 0, i, 0))
    pltpu.emit_pipeline(
        tile,
        grid=(steps // STEPS,),
        in_specs=[pl.BlockSpec((2, 128, width), lambda i: (0, i, 0)), nat, nat],
        out_specs=[nat],
    )(du2, tok, cot, out)
    sums[...] = jnp.zeros_like(sums)
    sums[4:5, :] = jnp.sum(ga[...], axis=0, keepdims=True)
    sums[5:6, :] = jnp.sum(ba[...], axis=0, keepdims=True)
    for s in range(4):
        a, mp = divmod(s, 2)
        rows = (
            accc[a][mp, 0:8, :],
            accb[a][mp, 0:8, :],
            accc[a][mp, 8:16, :],
            accb[a][mp, 8:16, :],
        )
        for j, val in enumerate(rows):
            val = jnp.sum(val, axis=0, keepdims=True)
            for mm in range(2):
                lane = pl.ds(core_lane(a, 2 * mp + mm, c), BLK)
                sums[j : j + 1, lane] = val[:, mm * BLK : (mm + 1) * BLK]


def norm_grads(ids, deps, du2, tok, cot, lim8, scale, gain, accb, accc):
    _, rows, width = du2.shape
    n = rows * width
    return call_flat(
        norm_grad_kernel, "norm_grads", ids, deps,
        [*far_in(du2, tok, cot), lim8, scale, gain, *accb, *accc],
        [ANY] * 3 + [SMEM] * 2 + [NEAR] * 5,
        [far(tok.shape, F32), sds((8, width), F32)], 14, cost(n * 20, n * 8),
        scratch=[
            pltpu.VMEM((8, width), F32),
            pltpu.VMEM((8, width), F32),
            pltpu.VMEM((width // BLK, 128, BLK), F32),
        ],
        out_specs=[ANY, NEAR],
    )


def activation_kernel(ids, tok, hown, hrcv, out, scr):
    c = ids[2]
    for s in range(4):
        a, mp = divmod(s, 2)
        for mm in range(2):
            for n, (ref, core) in enumerate(((hown, c), (hrcv, 1 - c))):
                scr[n] = ref[s, mm].astype(F32)
                lane = pl.ds(core_lane(a, 2 * mp + mm, core), BLK)
                for st in range(8):
                    sq, h = divmod(st, PARTS)
                    val = scr[n, pl.ds(st, STEPS, stride=8), :]
                    out[sq, h, :, lane] = tok[sq, h, :, lane].astype(F32) + val


def activations_of(ids, deps, tok, hown, hrcv):
    seqs, parts, steps, width = tok.shape
    tiles = steps // STEPS
    nat = pl.BlockSpec((seqs, parts, STEPS, width), lambda i, ids: (0, 0, i, 0))
    hspec = pl.BlockSpec((4, 2, 128, BLK), lambda i, ids: (0, 0, i, 0))
    n = seqs * parts * steps * width
    return call(
        activation_kernel, "activations_of", (tiles,), ids, deps, far_in(tok, hown, hrcv),
        [nat, hspec, hspec], nat, far(tok.shape, F32), 16, cost(n, n * 8),
        scratch=[pltpu.VMEM((2, 128, BLK), F32)],
    )


def assemble_kernel(counts, ids, *refs):
    out = refs[-1]
    c = ids[2]
    start = 0
    for b, n in enumerate(counts):
        group = refs[start : start + n]
        start += n
        a, core = b % 2, c if b < 2 else 1 - c
        for j in range(3):
            total = group[0][j]
            for ref in group[1:]:
                total = total + ref[j].astype(F32)
            lane = pl.multiple_of(j * 512 + a * BLK + core * 256, BLK)
            out[:, pl.ds(lane, BLK)] = total


def assemble(ids, deps, groups):
    rows = groups[0][0].shape[1]
    counts = [len(g) for g in groups]
    args = [ref for group in groups for ref in group]
    return call_flat(
        functools.partial(assemble_kernel, counts), "assemble", ids, deps, args,
        [NEAR] * len(args), sds((rows, 1536), F32), 16, cost(0, rows * 1536 * 8),
    )


def local(
    nseq,
    ndp,
    tokens,
    cotangent,
    weight,
    forget_peep,
    reset_peep,
    forget_bias,
    reset_bias,
    norm_gain,
    norm_bias,
    lengths,
):
    axes = ("seq", "dp")
    nz = ndp // 2
    seqs, span, width = tokens.shape
    sub = span // PARTS
    q = lax.axis_index("seq").astype(jnp.int32)
    dp = lax.axis_index("dp").astype(jnp.int32)
    z, c = dp // 2, dp % 2
    ids = jnp.stack([q, z, c])

    def table(move):
        pairs = []
        for qq in range(nseq):
            for zz in range(nz):
                for cc in range(2):
                    to = move(qq, zz, cc)
                    if to is not None:
                        pairs.append((qq * ndp + zz * 2 + cc, to[0] * ndp + to[1] * 2 + to[2]))
        return pairs

    def send(value, move):
        return lax.ppermute(value, axes, table(move))

    def to_core(qq, zz, cc):
        return (qq, zz, 1 - cc)

    def to_x(qq, zz, cc):
        return (qq ^ 1, zz, cc)

    def to_y(qq, zz, cc):
        return (qq ^ 2, zz, cc)

    def shift_z(k):
        return lambda qq, zz, cc: (qq, (zz + k) % nz, cc)

    def shift_zc(k):
        return lambda qq, zz, cc: (qq, (zz + k) % nz, 1 - cc)

    def shift_q(k):
        return lambda qq, zz, cc: (qq + k, zz, cc) if 0 <= qq + k < nseq else None

    mine, theirs = split_weight(ids, weight)
    recv = send(theirs, to_core)
    nat = (seqs, PARTS, sub, width)
    tok4 = tokens.reshape(nat)
    cot4 = cotangent.reshape(nat)
    tok_oth = send(tokens, to_core).reshape(nat)
    cot_cols = jnp.concatenate(
        [lax.dynamic_slice_in_dim(cotangent, m * 512 + (1 - c) * 256, 256, 2) for m in range(4)],
        axis=2,
    )
    cot_oth = send(cot_cols, to_core).reshape(seqs, PARTS, sub, width // 2)
    len_oth = send(lengths, to_core)

    lens = jnp.stack([lengths, len_oth])
    counts = jnp.sum(lens, axis=1).astype(F32)
    scale = (seqs * span * nseq) / counts
    lim16 = (
        lens[:, :, None] - q * span - sub * jnp.arange(PARTS, dtype=jnp.int32)[None, None, :]
    ).reshape(2, 8)
    spread_rows = lambda v: jnp.broadcast_to(v, (2, STEPS, 8, BLK)).reshape(256, BLK)
    step_in_tile = jnp.arange(STEPS, dtype=jnp.int32)[None, :, None, None]
    lim = spread_rows(lim16[:, None, :, None] - step_in_tile)
    scl = spread_rows(scale[:, None, None, None])

    lim8, scale1 = lim16[0], scale[:1]

    def by_core(vec):
        v = lax.dynamic_slice_in_dim(vec.reshape(4, 4, BLK), 2 * c, 2, 1)
        return v.transpose(1, 0, 2).reshape(1, width // 2)

    vf, vr, bfor, brst = (by_core(v) for v in (forget_peep, reset_peep, forget_bias, reset_bias))
    gain, bias = norm_gain.reshape(1, width), norm_bias.reshape(1, width)

    tail = [mine]

    def run(kernel, *head, rest=(), token=-1, after=(), big=False):
        out = kernel(*head, ids, (tail[0], *after), *rest)
        tail[0] = out[token] if isinstance(out, (list, tuple)) else out
        if big:
            (tail[0],) = far_in(tail[0])
        return out

    groups = [[cc + 2 * zz for zz in range(nz)] for cc in range(2)]

    def along_z(piece):
        if nz <= 4:
            return [send(piece, shift_z(-k)) for k in range(1, nz)]
        got = lax.all_gather(piece, "dp", axis=0, tiled=True, axis_index_groups=groups)
        n = got.shape[0] // nz
        twice = jnp.concatenate([got, got], axis=0)
        return [lax.dynamic_slice_in_dim(twice, (z + 1) * n, n * (nz - 1), 0)]

    def gather_1(s, zs):
        rel = run(plane_pieces, s, rest=(zs,))
        return rel, send(rel, to_x), send(rel, to_y)

    def gather_2(s, got):
        rel, gx, gy = got
        tox, toy = run(cross_pieces, s, rest=(gx, gy))
        return rel, gx, gy, send(tox, to_x), send(toy, to_y)

    def spread(both):
        return lax.all_gather(both, "seq")

    def run_project(s, weights, before=None, after=()):
        rest = (ub, ulo, weights, lim, vf, bfor, before)
        return run(project, s, nz, rest=rest, token=4, after=after)

    def run_states(a, fwd, got, held, after=()):
        rest = (fwd, ub, ulo, cot4, cot_oth, lim, scl, vr, brst, got, held)
        out = run(states, a, nseq, rest=rest, after=after)
        return {
            "h": out[:2], "mid": (out[2:5], out[5:8]), "dzr": out[8], "u": out[9],
            "lbs": out[10], "summ": out[11], "acc": out[12],
        }

    def run_adjoints(a, fwd, m, got, after=()):
        rest = (fwd, m["mid"], m["dzr"], m["u"], vf, vr, m["lbs"], got)
        du, dzc, dzf, acc = run(adjoints, a, nseq, rest=rest, after=after)
        return {"du": du, "dz": (dzc, dzf, m["dzr"]), "acc": acc}

    def sum_1(which, dz, keep=(), after=()):
        own, xp, yp, da, db, *kept = run(
            weight_grad_part, which, nz, rest=(ubt, dz, keep), token=3, after=after
        )
        return (own, xp, yp, send(da, to_x), send(db, to_y)), kept

    def sum_2(got):
        own, xp, yp, ra, rb = got
        s1, s2 = run(relay_sums, rest=(xp, yp, ra, rb))
        return own, send(s1, to_x), send(s2, to_y)

    def fold(sets, d):
        kept, out = run(fold_z, d, rest=(sets,))
        return kept, send(out, lambda qq, zz, cc: (qq, zz ^ d, cc))

    def sum_3_now(got):
        if nz > 4:
            got, d = [got], nz // 2
            while d:
                got, d = fold(got, d), d // 2
            return run(fold_z, 0, rest=(got,))
        parts = list(run(plane_sums, nz, rest=got))
        return parts[:1] + [send(parts[k], shift_z(k)) for k in range(1, nz)]

    def fold_rest(got):
        d = nz // 4
        while d:
            got, d = fold(got, d), d // 2
        return got

    last, low = run(quarter_of, rest=(mine, recv), after=(tok_oth, cot_oth, len_oth))
    along = along_z(low)
    ub, ubt, ulo = run(
        norm_tokens, rest=(tok4, tok_oth, gain, bias), big=True, after=(lim8, scale1)
    )
    g0 = gather_1(0, along)
    every = [
        [qq * ndp + zz * 2 + cc for zz in range(nz) for qq in range(nseq)] for cc in range(2)
    ]
    last = run(hand_on, rest=(last,))
    w_hi = lax.all_gather(last, axes, axis=0, tiled=True, axis_index_groups=every)
    g0 = gather_2(0, g0)
    g1 = gather_1(1, along)
    f0 = run_project(0, (mine, recv, *g0))
    g1 = gather_2(1, g1)
    f1 = run_project(1, (mine, recv, *g1), f0[4])
    m0 = run_states(0, (f0, f1), spread(f1[4]), ())
    d0 = run_adjoints(0, (f0, f1), m0, spread(m0["summ"]))
    s0, _ = sum_1("other", d0["dz"])
    s1, first = sum_1("own", d0["dz"], (d0["du"],))
    s0 = sum_2(s0)
    f2 = run_project(2, (w_hi,))
    s1 = sum_2(s1)
    f3 = run_project(3, (w_hi,), f2[4])
    m1 = run_states(1, (f2, f3), spread(f3[4]), m0["h"], after=s0[1:])
    s01 = fold([s0, s1], nz // 2)
    hrcv = send(run(gate, rest=(m1["h"][1:], "far"))[0], to_core)
    got = spread(run(hand_on, rest=(m1["summ"],)))
    d1 = run_adjoints(1, (f2, f3), m1, got)
    s2, _ = sum_1("other", d1["dz"])
    s3, _ = sum_1("own", d1["dz"], after=(hrcv,))
    s2 = sum_2(s2)
    s01 = fold_rest(s01)
    second = (*d1["dz"], d1["du"])
    ws = (f0[5], f1[5], w_hi)
    du2 = run(unit_grads, 1, rest=(first, second, ws, ()), big=True)
    s3 = sum_2(s3)
    s2 = fold([s2], nz // 2)
    du2 = run(unit_grads, 0, rest=(first, second, ws, (du2,)), big=True)
    s0, s1 = run(fold_z, 0, rest=(s01,))
    s0 = send(s0, to_core)
    cores = [[2 * zz, 2 * zz + 1] for zz in range(nz)]
    du2 = lax.all_to_all(du2, "dp", 0, 0, axis_index_groups=cores, tiled=True)
    activations = run(activations_of, rest=(tok4, m1["h"][0], hrcv), big=True)
    s2 = fold_rest(s2)
    input_grad, sums = run(
        norm_grads,
        rest=(
            du2, tok4, cot4, lim8, scale1, gain, (m0["acc"], m1["acc"]), (d0["acc"], d1["acc"])
        ),
        after=(s0,),
    )
    if nz <= 4:
        moved = [send(sums, shift_z(k)) for k in range(1, nz)]
    s3 = sum_3_now(s3)
    s2 = send(run(fold_z, 0, rest=(s2,))[0], to_core)
    if nz <= 4:
        sums = run(add_up, rest=(sums, *moved))
    hops = [lambda qq, zz, cc, b=1 << b: (qq ^ b, zz, cc) for b in range((nseq - 1).bit_length())]
    hops.append(to_core)
    if nz > 4:
        hops += [lambda qq, zz, cc, b=1 << b: (qq, zz ^ b, cc) for b in range((nz - 1).bit_length())]
    for hop in hops:
        sums = run(add_up, rest=(sums, send(sums, hop)))
    s3 = run(fold_z, 0, rest=([s3],))
    weight_grad = run(assemble, rest=(([s1], s3, [s0], [s2]),))
    shape = tokens.shape
    return (
        activations.reshape(shape),
        input_grad.reshape(shape),
        weight_grad,
        sums[0],
        sums[1],
        sums[2],
        sums[3],
        sums[4],
        sums[5],
    )


def solution(mesh):
    whole = P("dp", "seq", None)
    in_specs = (whole, whole, P("dp", None)) + (P(),) * 6 + (P("dp"),)
    out_specs = (whole, whole, P("dp", "seq")) + (P(),) * 6
    step = functools.partial(local, mesh.shape["seq"], mesh.shape["dp"])
    return jax.shard_map(step, mesh=mesh, in_specs=in_specs, out_specs=out_specs, check_vma=False)
```

```python
import functools

import jax
import jax.numpy as jnp
from jax import lax
from jax.experimental import pallas as pl
from jax.experimental.pallas import tpu as pltpu
from jax.sharding import PartitionSpec as P

EPS = 1e-05
F32 = jnp.float32
BF = jnp.bfloat16
STEPS = 16
BLK = 128
GATES = 3
QUARTERS = 4
PARTS = 4


def params(mib, dims=1):
    return pltpu.CompilerParams(
        vmem_limit_bytes=mib * 1024 * 1024, dimension_semantics=("arbitrary",) * dims
    )


def cost(flops, bytes_accessed, transcendentals=0):
    return pl.CostEstimate(
        flops=int(flops), bytes_accessed=int(bytes_accessed), transcendentals=int(transcendentals)
    )


def sds(shape, dtype):
    return jax.ShapeDtypeStruct(shape, dtype)


def far(shape, dtype):
    return pltpu.HBM(shape, dtype)


def near(shape, dtype):
    return pltpu.VMEM(shape, dtype)


def far_in(*values):
    return [pltpu.with_memory_space_constraint(v, pltpu.HBM) for v in values]


def near_in(*values):
    return [pltpu.with_memory_space_constraint(v, pltpu.VMEM) for v in values]


ANY = pl.BlockSpec(memory_space=pl.ANY)
NEAR = pl.BlockSpec(memory_space=pltpu.VMEM)
SMEM = pl.BlockSpec(memory_space=pltpu.SMEM)


def ordered(kernel, deps):
    n = len(deps)

    def body(ids, *refs):
        return kernel(ids, *refs[n:])

    return body, list(deps), [ANY] * n


def call(kernel, name, grid, ids, deps, args, in_specs, out_specs, out_shape, mib, est, scratch=()):
    body, deps, dep_specs = ordered(kernel, deps)
    return pl.pallas_call(
        body,
        grid_spec=pltpu.PrefetchScalarGridSpec(
            num_scalar_prefetch=1,
            grid=grid,
            in_specs=dep_specs + in_specs,
            out_specs=out_specs,
            scratch_shapes=list(scratch),
        ),
        out_shape=out_shape,
        compiler_params=params(mib, len(grid)),
        cost_estimate=est,
        name=name,
    )(ids, *deps, *args)


def call_flat(kernel, name, ids, deps, args, in_specs, out_shape, mib, est, scratch=(), out_specs=None, aliases=None):
    body, deps, dep_specs = ordered(kernel, deps)
    many = isinstance(out_shape, (list, tuple))
    if out_specs is None:
        out_specs = [NEAR] * len(out_shape) if many else NEAR
    shift = 1 + len(deps)
    return pl.pallas_call(
        body,
        in_specs=[SMEM] + dep_specs + in_specs,
        out_specs=out_specs,
        out_shape=out_shape,
        scratch_shapes=list(scratch),
        input_output_aliases={k + shift: v for k, v in (aliases or {}).items()},
        compiler_params=pltpu.CompilerParams(vmem_limit_bytes=mib * 1024 * 1024),
        cost_estimate=est,
        name=name,
    )(ids, *deps, *args)


def split_kernel(ids, w, mine, theirs):
    c = ids[2]
    for s in range(4):
        a, mp = divmod(s, 2)
        for g in range(GATES):
            for mm in range(2):
                dst = s * 768 + g * 256 + mm * BLK
                base = g * 2048 + (2 * mp + mm) * 512 + a * BLK
                here = pl.multiple_of(base + c * 256, BLK)
                there = pl.multiple_of(base + (1 - c) * 256, BLK)
                mine[:, dst : dst + BLK] = w[:, pl.ds(here, BLK)]
                theirs[:, dst : dst + BLK] = w[:, pl.ds(there, BLK)]


def split_weight(ids, weight):
    rows, cols = weight.shape
    tile = rows // 2
    spec = pl.BlockSpec((tile, cols // 2), lambda i, ids: (i, 0))
    return call(
        split_kernel, "split_weight", (2,), ids, (), far_in(weight),
        [pl.BlockSpec((tile, cols), lambda i, ids: (i, 0))], [spec, spec],
        [sds((rows, cols // 2), BF)] * 2, 16, cost(0, rows * cols * 4),
    )


def quarter_kernel(ids, mine, recv, high, p0, p1):
    q, c = ids[0], ids[2]
    half = high.shape[0]
    at = pl.ds(pl.multiple_of(lax.rem(q, 2) * half, half), half)
    first = (lax.div(q, 2) == c).astype(jnp.int32) == 1
    val = jnp.where(first, mine[at, :], recv[at, :])
    high[...] = val[:, 1536:]
    p0[...] = val[:, :768]
    p1[...] = val[:, 768:1536]


def quarter_of(ids, deps, mine, recv):
    rows, cols = mine.shape
    half = rows // 2
    return call_flat(
        quarter_kernel, "quarter_of", ids, deps, [mine, recv], [NEAR, NEAR],
        [sds((half, 1536), BF), sds((half, 768), BF), sds((half, 768), BF)], 8,
        cost(0, rows * cols * 4),
    )


def copy_kernel(ids, src, dst):
    dst[...] = src[...]


def hand_on(ids, deps, value):
    return call_flat(
        copy_kernel, "hand_on", ids, deps, [value], [NEAR], sds(value.shape, value.dtype), 16,
        cost(0, value.size * 4),
    )


def gate_kernel(ids, *refs):
    pass


def gate(ids, deps, values, hold=None):
    shape = {None: sds, "far": far, "near": near}[hold]
    held = {None: lambda *v: list(v), "far": far_in, "near": near_in}[hold]
    return call_flat(
        gate_kernel, "gate", ids, deps, held(*values), [ANY] * len(values),
        [shape(v.shape, v.dtype) for v in values], 4, cost(0, 1), out_specs=[ANY] * len(values),
        aliases={n: n for n in range(len(values))},
    )


def add_kernel(ids, *refs):
    total = refs[0][...]
    for ref in refs[1:-1]:
        total = total + ref[...]
    refs[-1][...] = total


def add_up(ids, deps, *values):
    a = values[0]
    return call_flat(
        add_kernel, "add_up", ids, deps, list(values), [NEAR] * len(values), sds(a.shape, a.dtype),
        4, cost(a.size, a.size * 4 * len(values)),
    )


def plane_kernel(s, ids, *refs):
    rel = refs[-1]
    row = 0
    for ref in refs[:-1]:
        lane = s % 2 * 768 if ref.shape[1] > 768 else 0
        rel[row : row + ref.shape[0], :] = ref[:, lane : lane + 768]
        row += ref.shape[0]


def plane_pieces(s, ids, deps, parts):
    rows = sum(p.shape[0] for p in parts)
    return call_flat(
        functools.partial(plane_kernel, s), f"plane_pieces_{s}", ids, deps, list(parts),
        [NEAR] * len(parts), sds((rows, 768), BF), 8, cost(0, rows * 768 * 4),
    )


def cross_kernel(ids, gx, gy, tox, toy):
    tox[...] = gy[:, :384]
    toy[...] = gx[:, 384:]


def cross_pieces(s, ids, deps, gx, gy):
    rows = gx.shape[0]
    return call_flat(
        cross_kernel, f"cross_pieces_{s}", ids, deps, [gx, gy], [NEAR, NEAR],
        [sds((rows, 384), BF)] * 2, 16, cost(0, rows * 768 * 4),
    )


def norm_of(x):
    mean = jnp.mean(x, axis=-1, keepdims=True)
    centered = x - mean
    var = jnp.mean(centered * centered, axis=-1, keepdims=True)
    rstd = lax.rsqrt(var + EPS)
    return centered * rstd, rstd


def norm_kernel(ids, own, other, gain, bias, ub, ubt, ulo, scr):
    c = ids[2]
    seqs = own.shape[0]
    for k, ref in enumerate((own, other)):
        for st in range(8):
            sq, h = divmod(st, PARTS)
            normed, _ = norm_of(ref[sq, h].astype(F32))
            unit = normed * gain[...] + bias[...]
            for j in range(scr.shape[0]):
                scr[j, pl.ds(k * 128 + st, STEPS, stride=8), :] = unit[:, j * BLK : (j + 1) * BLK]
    for j in range(scr.shape[0]):
        low = scr[j].astype(BF)
        ub[0, :, :, j * BLK : (j + 1) * BLK] = low.reshape(2, 128, BLK)
        ubt[j * BLK : (j + 1) * BLK, :] = low.T
    for a in range(2):
        for m in range(QUARTERS):
            unit = scr[m * 4 + a + 2 * c]
            rest = (unit - unit.astype(BF).astype(F32)).astype(BF)
            dst = (a * QUARTERS + m) * BLK
            ulo[0, :, :, dst : dst + BLK] = rest.reshape(2, 128, BLK)


def tile_block(cols):
    return pl.BlockSpec((1, 2, 128, cols), lambda i, ids: (i, 0, 0, 0))


def norm_tokens(ids, deps, own, other, gain, bias):
    seqs, parts, steps, width = own.shape
    rows = seqs * parts * steps
    tiles = steps // STEPS
    nat = pl.BlockSpec((seqs, parts, STEPS, width), lambda i, ids: (0, 0, i, 0))
    vec = pl.BlockSpec((1, width), lambda i, ids: (0, 0))
    return call(
        norm_kernel, "norm_tokens", (tiles,), ids, deps, [*far_in(own, other), gain, bias],
        [nat, nat, vec, vec],
        [
            tile_block(width),
            pl.BlockSpec((width, 256), lambda i, ids: (0, i)),
            tile_block(width // 2),
        ],
        [
            far((tiles, 2, 128, width), BF),
            far((width, 2 * rows), BF),
            far((tiles, 2, 128, width // 2), BF),
        ],
        20, cost(rows * width * 20, rows * width * 14),
        scratch=[pltpu.VMEM((width // BLK, 256, BLK), F32)],
    )


def flat(ref):
    value = ref[...]
    return value.reshape(256, value.shape[-1])


def core_lane(a, m, c):
    return pl.multiple_of(m * 512 + a * BLK + c * 256, BLK)


def pairs():
    for tp in range(STEPS // 2):
        for k in range(2):
            yield k, tp * 16, k * 128 + tp * 16


def live_pair(lim, row, tile):
    live = lim[row : row + 16, :] > tile * STEPS
    return jnp.concatenate([live, live], axis=1)


def fold_streams(pr, lc, ahead):
    out = []
    order = range(PARTS) if ahead else range(PARTS - 1, -1, -1)
    for sq in range(2):
        tp = tl = None
        for h in order:
            n = sq * PARTS + h
            p, l = pr[n : n + 1], lc[n : n + 1]
            tp, tl = (p, l) if tp is None else ((p * tp, p * tl + l) if ahead else (p * tp, l + p * tl))
        out.append((tp, tl))
    return out


def proj_kernel(s, nz, joined, ids, ub, ulo, *rest):
    n_w = 1 if joined else 7
    weights, rest = rest[:n_w], rest[n_w:]
    lim, vf, bfor = rest[:3]
    rest = rest[3:]
    before = rest[0] if s % 2 else None
    cand_far, decay, rpre_far, plout, summ = rest[s % 2 : s % 2 + 5]
    rest = rest[s % 2 + 5 :]
    if joined:
        zbuf, prod, loc, wbuf, sems = rest
    else:
        wall, zbuf, prod, loc, wbuf, sems = rest
    tiles = decay.shape[0]
    width = wbuf.shape[0]
    q, z, c = ids[0], ids[1], ids[2]
    a, mp = divmod(s, 2)
    cols = slice(mp * 768, mp * 768 + 768)
    copies = []

    def put(src, row, rows, lo=0, hi=768):
        dst = wbuf.at[pl.ds(row, rows), lo:hi]
        copy = pltpu.make_async_copy(src, dst, sems.at[len(copies)])
        copy.start()
        copies.append(copy)

    if joined:
        put(weights[0].at[:, cols], 0, width)
    else:
        mine, recv, rel, gx, gy, dx, dy = weights
        zb = width // nz
        zb2, qb = zb // 2, zb // 4
        mult = lambda v: pl.multiple_of(v, qb)
        put(mine.at[:, s * 768 : (s + 1) * 768], mult(z * zb + c * zb2), zb2)
        put(recv.at[:, s * 768 : (s + 1) * 768], mult(z * zb + (1 - c) * zb2), zb2)
        for r in range(1, nz):
            base = lax.rem(z + r, nz) * zb
            lo, hi = (r - 1) * qb, r * qb
            put(rel.at[lo:hi, :], mult(base + q * qb), qb)
            put(gx.at[lo:hi, :], mult(base + (q ^ 1) * qb), qb)
            put(gy.at[lo:hi, :], mult(base + (q ^ 2) * qb), qb)
            put(dx.at[lo:hi, :], mult(base + (q ^ 3) * qb), qb, 0, 384)
            put(dy.at[lo:hi, :], mult(base + (q ^ 3) * qb), qb, 384, 768)
    for copy in copies:
        copy.wait()
    if not joined:
        keep = pltpu.make_async_copy(wbuf, wall, sems.at[len(copies)])
        keep.start()
    prod[...] = jnp.ones_like(prod)
    loc[...] = jnp.zeros_like(loc)

    def tile(ubr, ulor, cand, rpre):
        i = pl.program_id(0)
        zbuf[:, :768] = jnp.dot(flat(ubr), wbuf[...], preferred_element_type=F32)
        low = flat(ulor).astype(F32)
        for mm in range(2):
            high = ubr[:, :, :, pl.ds(core_lane(a, 2 * mp + mm, c), BLK)].reshape(256, BLK)
            zbuf[:, 768 + mm * BLK : 768 + (mm + 1) * BLK] = (
                high.astype(F32) + low[:, mm * BLK : (mm + 1) * BLK]
            )
        pr = [prod[0:8, :], prod[8:16, :]]
        lc = [loc[0:8, :], loc[8:16, :]]
        for k, r0, row in pairs():
            cd = zbuf[row : row + 16, :256]
            logit = zbuf[row : row + 16, 256:512] + vf[...] * zbuf[row : row + 16, 768:] + bfor[...]
            dec = jnp.where(live_pair(lim, row, i), jax.nn.sigmoid(logit), 1.0)
            inj = (1.0 - dec) * cd
            cand[0, k, r0 : r0 + 16, :] = cd
            decay[i, k, r0 : r0 + 16, :] = dec
            rpre[0, k, r0 : r0 + 16, :] = zbuf[row : row + 16, 512:768]
            for t in range(2):
                d = dec[t * 8 : t * 8 + 8]
                lc[k] = d * lc[k] + inj[t * 8 : t * 8 + 8]
                pr[k] = d * pr[k]
        for k in range(2):
            prod[k * 8 : k * 8 + 8, :] = pr[k]
            loc[k * 8 : k * 8 + 8, :] = lc[k]

    pltpu.emit_pipeline(
        tile,
        grid=(tiles,),
        in_specs=[
            pl.BlockSpec((1, 2, 128, width), lambda i: (i, 0, 0, 0)),
            pl.BlockSpec((1, 2, 128, 256), lambda i: (i, 0, 0, s)),
        ],
        out_specs=[pl.BlockSpec((1, 2, 128, 256), lambda i: (i, 0, 0, 0))] * 2,
    )(ub, ulo, cand_far, rpre_far)
    if s % 2:
        summ[0] = before[0]
    plout[0:16, :] = prod[...]
    plout[16:32, :] = loc[...]
    for k in range(2):
        pr, lc = prod[k * 8 : k * 8 + 8, :], loc[k * 8 : k * 8 + 8, :]
        for sq, (tp, tl) in enumerate(fold_streams(pr, lc, True)):
            ks = k * 2 + sq
            summ[s % 2, ks : ks + 1, :] = tp
            summ[s % 2, 4 + ks : 5 + ks, :] = tl
    if not joined:
        keep.wait()


def project(s, nz, ids, deps, ub, ulo, weights, lim, vf, bfor, before):
    tiles, _, _, width = ub.shape
    joined = len(weights) == 1
    shape = (tiles, 2, 128, 256)
    rows = tiles * 256
    chan = slice(s * 256, s * 256 + 256)
    args = far_in(ub, ulo, *weights) + [lim, vf[:, chan], bfor[:, chan]]
    in_specs = [ANY] * (2 + len(weights)) + [NEAR] * 3
    if s % 2:
        args.append(before)
        in_specs.append(NEAR)
    out_shape = [far(shape, F32), near(shape, F32), far(shape, F32)]
    out_shape += [near((32, 256), F32), near((2, 8, 256), F32)]
    out_specs = [ANY, NEAR, ANY, NEAR, NEAR]
    if not joined:
        out_shape.append(far((width, 768), BF))
        out_specs.append(ANY)
    return call_flat(
        functools.partial(proj_kernel, s, nz, joined), f"project_{s}", ids, deps, args, in_specs,
        out_shape, 12, cost(2 * rows * width * 768, rows * width * 2 + width * 768 * 4),
        scratch=[
            pltpu.VMEM((256, 1024), F32),
            pltpu.VMEM((16, 256), F32),
            pltpu.VMEM((16, 256), F32),
            pltpu.VMEM((width, 768), BF),
            pltpu.SemaphoreType.DMA((3 + 5 * (nz - 1),)),
        ],
        out_specs=out_specs,
    )


def halves(v):
    return v[:8], v[8:]


def enter(got, n, ahead, q, count):
    value = jnp.zeros((4, 256), F32)
    for j in range(count) if ahead else range(count - 1, -1, -1):
        used = (j < q) if ahead else (j > q)
        longer = got[j, n, 4:8, :] + got[j, n, 0:4, :] * value
        value = jnp.where(used, longer, value)
    return value


def state_kernel(a, count, held, ids, *refs):
    fwd = (refs[0:4], refs[4:8])
    ub, ulo, cot_own, cot_oth, lim, scl, vr, br, got = refs[8:17]
    rest = refs[17 + (2 if held else 0) :]
    hown, hoth = rest[:2]
    out = (rest[2:5], rest[5:8])
    dzr, uu, lbs, summ, acc, st, pp, lb, ac, scr = rest[8:]
    tiles = dzr.shape[0]
    q, c = ids[0], ids[2]
    for n in range(2):
        cand_far, decay, rpre_far, plin = fwd[n]
        bc, dstate, du0 = out[n]
        lanes = slice(n * 256, n * 256 + 256)
        carry = enter(got, n, True, q, count)
        for ks in range(4):
            cc = carry[ks : ks + 1]
            for h in range(PARTS):
                m = ks * PARTS + h
                st[m : m + 1, :] = cc
                cc = plin[m : m + 1, :] * cc + plin[16 + m : 17 + m, :]
        pp[...] = jnp.ones_like(pp)
        lb[...] = jnp.zeros_like(lb)
        ac[...] = jnp.zeros_like(ac)

        def tile(cand, rpre, u0, u1, ul, own0, own1, oth0, oth1, ho, ht):
            i = pl.program_id(0)
            for k, pair in enumerate(((own0, own1), (oth0, oth1))):
                for b, ref in enumerate(pair):
                    for m in range(8):
                        sq, h = divmod(m, PARTS)
                        scr[b, pl.ds(k * 128 + m, STEPS, stride=8), :] = ref[sq, h].astype(F32)
            cur = [st[0:8, :], st[8:16, :]]
            p = [pp[0:8, :], pp[8:16, :]]
            l = [lb[0:8, :], lb[8:16, :]]
            peep = [jnp.zeros((8, 256), F32)] * 2
            bias = [jnp.zeros((8, 256), F32)] * 2
            wr, wb = vr[:, lanes], br[:, lanes]
            for k, r0, row in pairs():
                at = slice(r0, r0 + 16)
                dec = decay[i, k, at, :]
                cd = cand[0, k, at, :]
                inj = (1.0 - dec) * cd
                befores, states = [], []
                for d, v in zip(halves(dec), halves(inj)):
                    befores.append(cur[k])
                    cur[k] = d * cur[k] + v
                    states.append(cur[k])
                before = jnp.concatenate(befores, axis=0)
                state = jnp.concatenate(states, axis=0)
                low = jnp.concatenate([u0[0, k, at, :], u1[0, k, at, :]], axis=1)
                uu[i, k, at, lanes] = low
                u = low.astype(F32) + ul[0, k, at, :].astype(F32)
                live = lim[row : row + 16, :] > i * STEPS
                sc = jnp.where(live, scl[row : row + 16, :], 0.0)
                gy = jnp.concatenate(
                    [scr[0, row : row + 16, :] * sc, scr[1, row : row + 16, :] * sc], axis=1
                )
                r = jax.nn.sigmoid(rpre[0, k, at, :] + wr * before + wb)
                gap = state - u
                hv = jnp.where(jnp.concatenate([live, live], axis=1), u + r * gap, 0.0).astype(BF)
                href = ht if k else ho
                href[0, 0, at, :] = hv[:, :BLK]
                href[0, 1, at, :] = hv[:, BLK:]
                ds = gy * r
                drl = ds * (1.0 - r) * gap
                sr = dec * ds + wr * drl
                dstate[i, k, at, :] = ds
                bc[i, k, at, :] = before - cd
                du0[i, k, at, :] = (gy - ds).astype(BF)
                dzr[i, k, at, lanes] = drl.astype(BF)
                for d, v in zip(halves(dec), halves(sr)):
                    l[k] = l[k] + p[k] * v
                    p[k] = p[k] * d
                for e, w in zip(halves(drl), befores):
                    peep[k] = peep[k] + e * w
                    bias[k] = bias[k] + e
            for k in range(2):
                st[k * 8 : k * 8 + 8, :] = cur[k]
                pp[k * 8 : k * 8 + 8, :] = p[k]
                lb[k * 8 : k * 8 + 8, :] = l[k]
            ac[0:8, :] += peep[0] + peep[1]
            ac[8:16, :] += bias[0] + bias[1]

        nat = cot_own.shape[:2]

        def unit(mm):
            return pl.BlockSpec(
                (1, 2, 128, BLK), lambda i: (i, 0, 0, (2 * n + mm) * 4 + 2 * c + a)
            )

        def tail():
            return pl.BlockSpec((1, 2, 128, 256), lambda i: (i, 0, 0, 2 * a + n))

        def nat_own(mm):
            return pl.BlockSpec(
                (*nat, STEPS, BLK), lambda i: (0, 0, i, (2 * n + mm) * 4 + 2 * c + a)
            )

        def nat_oth(mm):
            return pl.BlockSpec((*nat, STEPS, BLK), lambda i: (0, 0, i, (2 * n + mm) * 2 + a))

        one = pl.BlockSpec((1, 2, 128, 256), lambda i: (i, 0, 0, 0))
        hspec = pl.BlockSpec((1, 2, 128, BLK), lambda i: (2 * a + n, 0, i, 0))
        pltpu.emit_pipeline(
            tile,
            grid=(tiles,),
            in_specs=[one, one, unit(0), unit(1), tail(), nat_own(0), nat_own(1), nat_oth(0), nat_oth(1)],
            out_specs=[hspec, hspec],
        )(cand_far, rpre_far, ub, ub, ulo, cot_own, cot_own, cot_oth, cot_oth, hown, hoth)
        acc[n] = ac[...]
        lbs[n] = lb[...]
        for k in range(2):
            p, l = pp[k * 8 : k * 8 + 8, :], lb[k * 8 : k * 8 + 8, :]
            for sq, (tp, tl) in enumerate(fold_streams(p, l, False)):
                ks = k * 2 + sq
                summ[n, ks : ks + 1, :] = tp
                summ[n, 4 + ks : 5 + ks, :] = tl


def states(a, count, ids, deps, fwd, ub, ulo, cot_own, cot_oth, lim, scl, vr, br, got, held):
    tiles = ub.shape[0]
    rows = tiles * 128
    one = (tiles, 2, 128, 256)
    two = (tiles, 2, 128, 512)
    chan = slice(a * 512, a * 512 + 512)
    args, in_specs = [], []
    for f in fwd:
        args += far_in(f[0]) + near_in(f[1]) + far_in(f[2]) + [f[3]]
        in_specs += [ANY, NEAR, ANY, NEAR]
    args += far_in(ub, ulo, cot_own, cot_oth) + [lim, scl, vr[:, chan], br[:, chan], got]
    in_specs += [ANY] * 4 + [NEAR] * 5
    aliases = {}
    if held:
        aliases = {len(args): 0, len(args) + 1: 1}
        args += far_in(*held)
        in_specs += [ANY] * 2
    small = near((2, 16, 256), F32)
    return call_flat(
        functools.partial(state_kernel, a, count, bool(held)), f"states_{a}", ids, deps, args,
        in_specs,
        [far((4, 2, rows, BLK), BF)] * 2
        + [near(one, F32), near(one, F32), near(one, BF)] * 2
        + [near(two, BF)] * 2
        + [small, near((2, 8, 256), F32), small],
        10, cost(rows * 1024 * 60, rows * 1024 * 10, rows * 1024 * 2),
        scratch=[pltpu.VMEM((16, 256), F32)] * 4 + [pltpu.VMEM((2, 256, BLK), F32)],
        out_specs=[ANY] * 2 + [NEAR] * 11,
        aliases=aliases,
    )


def adjoint_kernel(count, ids, *refs):
    ins = (refs[0:5], refs[5:10])
    dzr, uu, vf, vr, lbs, got, du, dzc, dzf, acc, adj = refs[10:]
    tiles = du.shape[0]
    q = ids[0]
    for n in range(2):
        decay, bc, dstate, du0, plin = ins[n]
        lanes = slice(n * 256, n * 256 + 256)
        wf, wr = vf[:, lanes], vr[:, lanes]
        after = enter(got, n, False, q, count)
        for ks in range(4):
            cc = after[ks : ks + 1]
            for h in range(PARTS - 1, -1, -1):
                m = ks * PARTS + h
                adj[m : m + 1, :] = cc
                cc = lbs[n, m : m + 1, :] + plin[m : m + 1, :] * cc

        def tile(step, state):
            i = tiles - 1 - step
            cur, peep, bias = [state[0], state[1]], state[2], state[3]
            for k, r0, _ in reversed(list(pairs())):
                at = slice(r0, r0 + 16)
                dec = decay[i, k, at, :]
                ds = dstate[i, k, at, :]
                sr = dec * ds + wr * dzr[i, k, at, lanes].astype(F32)
                late = ds[8:] + cur[k]
                cur[k] = dec[8:] * cur[k] + sr[8:]
                early = ds[:8] + cur[k]
                cur[k] = dec[:8] * cur[k] + sr[:8]
                dcand = jnp.concatenate([early, late], axis=0) * (1.0 - dec)
                dfl = dcand * bc[i, k, at, :] * dec
                dzc[i, k, at, lanes] = dcand.astype(BF)
                dzf[i, k, at, lanes] = dfl.astype(BF)
                du[i, k, at, lanes] = (du0[i, k, at, :].astype(F32) + dfl * wf).astype(BF)
                w = dfl * uu[i, k, at, lanes].astype(F32)
                peep = peep + (w[:8] + w[8:])
                bias = bias + (dfl[:8] + dfl[8:])
            return cur[0], cur[1], peep, bias

        zero = jnp.zeros((8, 256), F32)
        end = lax.fori_loop(0, tiles, tile, (adj[0:8, :], adj[8:16, :], zero, zero))
        acc[n, 0:8, :] = end[2]
        acc[n, 8:16, :] = end[3]


def adjoints(a, count, ids, deps, fwd, mid, dzr, uu, vf, vr, lbs, got):
    tiles = uu.shape[0]
    rows = tiles * 128
    shape = (tiles, 2, 128, 512)
    args = []
    for f, m in zip(fwd, mid):
        args += near_in(f[1], *m) + [f[3]]
    chan = slice(a * 512, a * 512 + 512)
    args += near_in(dzr, uu) + [vf[:, chan], vr[:, chan], lbs, got]
    return call_flat(
        functools.partial(adjoint_kernel, count), f"adjoints_{a}", ids, deps, args,
        [NEAR] * len(args),
        [near(shape, BF)] * 3 + [near((2, 16, 256), F32)],
        6, cost(rows * 1024 * 20, rows * 1024 * 4), scratch=[pltpu.VMEM((16, 256), F32)],
    )


def wgrad_kernel(which, nz, n_kept, ids, ubt, dzc, dzf, dzr, *rest):
    kept, rest = rest[: max(n_kept - 3, 0)], rest[max(n_kept - 3, 0) :]
    own, xp, yp, da, db = rest[:5]
    scr, sems = rest[5 + n_kept :]
    copies = [
        pltpu.make_async_copy(src, dst, sems.at[n])
        for n, (src, dst) in enumerate(zip((dzc, dzf, dzr, *kept), rest[5 : 5 + n_kept]))
    ]
    for copy in copies:
        copy.start()
    q, c = ids[0], ids[2]
    rh = 1 - c if which == "other" else c
    half = scr.shape[0]
    rows = ubt.shape[1]

    def tile(lhs):
        i = pl.program_id(0)
        for g, dz in enumerate((dzc, dzf, dzr)):
            rhs = dz[...].reshape(rows, 512)
            scr[:, g * 512 : (g + 1) * 512] = jnp.dot(
                lhs[...], rhs, preferred_element_type=F32
            ).astype(BF)

        def block(r, j):
            return scr[:, pl.ds(pl.multiple_of(((q ^ r) * 3 + j) * BLK, BLK), BLK)]

        at = pl.ds(pl.multiple_of(i * half, half), half)
        for j in range(3):
            own[j, at, :] = block(0, j)
            xp[j, at, :] = block(1, j)
            yp[j, at, :] = block(2, j)

        @pl.when(i < nz // 2)
        def _():
            for j in range(3):
                da[j, at, :] = block(3, j)

        @pl.when(i >= nz // 2)
        def _():
            back = pl.ds(pl.multiple_of((i - nz // 2) * half, half), half)
            for j in range(3):
                db[j, back, :] = block(3, j)

    pltpu.emit_pipeline(
        tile, grid=(nz,), in_specs=[pl.BlockSpec((half, rows), lambda i: (2 * i + rh, 0))]
    )(ubt)
    for copy in copies:
        copy.wait()


def weight_grad_part(which, nz, ids, deps, ubt, dz, keep=()):
    width, rows = ubt.shape
    half = width // nz // 2
    kept = (*dz, *keep) if keep else ()
    return call_flat(
        functools.partial(wgrad_kernel, which, nz, len(kept)), "weight_grad_part", ids, deps,
        [*far_in(ubt), *near_in(*dz, *keep)], [ANY] + [NEAR] * (3 + len(keep)),
        [sds((3, nz * half, BLK), BF)] * 3
        + [sds((3, nz * half // 2, BLK), BF)] * 2
        + [far(v.shape, v.dtype) for v in kept],
        10, cost(2 * rows * nz * half * 1536, rows * width + width * 1536),
        scratch=[pltpu.VMEM((half, 1536), BF), pltpu.SemaphoreType.DMA((4,))],
        out_specs=[NEAR] * 5 + [ANY] * len(kept),
    )


def relay_kernel(ids, xp, yp, ra, rb, s1, s2):
    half = ra.shape[1]
    s1[:, :half, :] = xp[:, :half, :]
    s1[:, half:, :] = (xp[:, half:, :].astype(F32) + rb[...].astype(F32)).astype(BF)
    s2[:, :half, :] = (yp[:, :half, :].astype(F32) + ra[...].astype(F32)).astype(BF)
    s2[:, half:, :] = yp[:, half:, :]


def relay_sums(ids, deps, xp, yp, ra, rb):
    rows = xp.shape[1]
    return call_flat(
        relay_kernel, "relay_sums", ids, deps, [xp, yp, ra, rb], [NEAR] * 4,
        [sds(xp.shape, BF)] * 2, 16, cost(rows * 768, rows * 384 * 10),
    )


def plane_sum_kernel(nz, ids, own, r1, r2, *outs):
    rows = outs[0].shape[1]
    for k, out in enumerate(outs):
        start = lax.rem(ids[1] + k, nz) * rows
        at = pl.ds(pl.multiple_of(start, rows), rows)
        tot = own[:, at, :].astype(F32) + r1[:, at, :].astype(F32) + r2[:, at, :].astype(F32)
        out[...] = tot.astype(out.dtype)


def plane_sums(nz, ids, deps, own, r1, r2):
    rows = own.shape[1] // nz
    return call_flat(
        functools.partial(plane_sum_kernel, nz), "plane_sums", ids, deps, [own, r1, r2], [NEAR] * 3,
        [sds((3, rows, BLK), F32)] + [sds((3, rows, BLK), BF)] * (nz - 1), 16,
        cost(rows * 768 * nz, rows * 384 * 8 * nz),
    )


def fold_kernel(sets, d, ids, *refs):
    n = sum(len(g) for g in sets) if sets else 2
    srcs, outs = refs[:n], refs[n:]
    if sets:
        groups, at = [], 0
        for g in sets:
            groups.append(srcs[at : at + len(g)])
            at += len(g)
    else:
        groups = [[ref.at[g] for ref in srcs] for g in range(srcs[0].shape[0])]
    half = groups[0][0].shape[1] // 2
    bit = lax.rem(lax.div(ids[1], d), 2) if d else 0
    for g, parts in enumerate(groups):
        spots = ((outs[0], bit), (outs[1], 1 - bit)) if d else ((outs[g], None),)
        for out, where in spots:
            rows = slice(None) if where is None else pl.ds(pl.multiple_of(where * half, half), half)
            total = parts[0][:, rows, :].astype(F32)
            for part in parts[1:]:
                total = total + part[:, rows, :].astype(F32)
            if d:
                out[g] = total.astype(out.dtype)
            else:
                out[...] = total


def fold_z(d, ids, deps, sets):
    stacked = not isinstance(sets[0], (list, tuple))
    args = list(sets) if stacked else [v for g in sets for v in g]
    count = sets[0].shape[0] if stacked else len(sets)
    _, rows, _ = args[0].shape[-3:]
    if d:
        shape = (count, 3, rows // 2, BLK)
        out_shape = [sds(shape, F32), sds(shape, BF)]
    else:
        out_shape = [sds((3, rows, BLK), F32)] * count
    return call_flat(
        functools.partial(fold_kernel, None if stacked else [tuple(g) for g in sets], d), "fold_z",
        ids, deps, args, [NEAR] * len(args), out_shape, 8,
        cost(rows * 768 * count, rows * 384 * 10 * count),
    )


DIMS = (((1,), (1,)), ((), ()))
TILE_N = 512


def unit_kernel(k, ids, *refs):
    first, second, ws = refs[0:4], refs[4:8], refs[8:12]
    far_out, out, lhs, e0, wbuf, sems, wsems, osems = refs[13 if k == 0 else 12 :]
    c = ids[2]
    rows = out.shape[0]
    tiles = ws[0].shape[0] // TILE_N

    def fetch(m):
        slot, lane, copies = m % 2, 0, []
        for n, w in enumerate(ws):
            cols = w.shape[1]
            dst = wbuf.at[slot, :, lane : lane + cols]
            src = w.at[m * TILE_N : (m + 1) * TILE_N, :]
            copies.append(pltpu.make_async_copy(src, dst, wsems.at[slot, n]))
            lane += cols
        return copies

    copies = [(first[3].at[:, k], e0)]
    for mp in range(2):
        for g, ref in enumerate(first[:3]):
            dst = mp * 768 + g * 256
            src = ref.at[:, k, :, mp * 256 : (mp + 1) * 256]
            copies.append((src, lhs.at[:, :, dst : dst + 256]))
    copies = [pltpu.make_async_copy(a, b, sems.at[n]) for n, (a, b) in enumerate(copies)]
    for copy in copies + fetch(0):
        copy.start()
    for mp in range(2):
        for g, ref in enumerate(second[:3]):
            dst = 1536 + mp * 768 + g * 256
            lhs[:, :, dst : dst + 256] = ref[:, k, :, mp * 256 : (mp + 1) * 256]
    for copy in copies:
        copy.wait()
    moved = []
    for m in range(tiles):
        if m + 1 < tiles:
            for copy in fetch(m + 1):
                copy.start()
        for copy in fetch(m):
            copy.wait()
        lo = m * TILE_N
        left = lhs[...].reshape(rows, 3072)
        acc = lax.dot_general(left, wbuf[m % 2], DIMS, preferred_element_type=F32)
        out[:, lo : lo + TILE_N] = acc.astype(out.dtype)
        cols = slice(m * BLK, (m + 1) * BLK)
        for a, val in enumerate((e0[:, :, cols], second[3][:, k, :, cols])):
            lane = pl.ds(pl.multiple_of(lo + a * BLK + c * 256, BLK), BLK)
            total = out[:, lane].astype(F32) + val.reshape(rows, BLK).astype(F32)
            out[:, lane] = total.astype(out.dtype)
        slot = 1 - c if k else c
        done = pltpu.make_async_copy(
            out.at[:, lo : lo + TILE_N], far_out.at[slot, :, lo : lo + TILE_N], osems.at[m]
        )
        done.start()
        moved.append(done)
    for done in moved:
        done.wait()


def unit_grads(k, ids, deps, first, second, ws, held):
    tiles = first[0].shape[0]
    rows, width = tiles * 128, ws[0].shape[0]
    args = [*far_in(*first), *near_in(*second), *far_in(*ws)]
    return call_flat(
        functools.partial(unit_kernel, k), f"unit_grads_{k}", ids, deps, args + far_in(*held),
        [ANY] * 4 + [NEAR] * 4 + [ANY] * (4 + len(held)),
        far((2, rows, width), BF), 24, cost(2 * rows * width * 3072, width * 3072 * 2),
        scratch=[
            pltpu.VMEM((rows, width), BF),
            pltpu.VMEM((tiles, 128, 3072), BF),
            pltpu.VMEM((tiles, 128, 512), BF),
            pltpu.VMEM((2, TILE_N, 3072), BF),
            pltpu.SemaphoreType.DMA((7,)),
            pltpu.SemaphoreType.DMA((2, 4)),
            pltpu.SemaphoreType.DMA((width // TILE_N,)),
        ],
        out_specs=ANY, aliases={len(args): 0} if held else {},
    )


def norm_grad_kernel(ids, du2, tok, cot, lim, scl, gain, *rest):
    accb, accc = rest[:2], rest[2:4]
    out, sums, ga, ba, scr = rest[4:]
    c = ids[2]
    ga[...] = jnp.zeros_like(ga)
    ba[...] = jnp.zeros_like(ba)

    def tile(dur, tokr, cotr, outr):
        i = pl.program_id(0)
        for j in range(scr.shape[0]):
            lanes = slice(j * BLK, (j + 1) * BLK)
            scr[j] = dur[0, :, lanes].astype(F32) + dur[1, :, lanes].astype(F32)
        step = lax.broadcasted_iota(jnp.int32, (STEPS, 1), 0) + i * STEPS
        gsum = jnp.zeros(ga.shape, F32)
        bsum = jnp.zeros(ba.shape, F32)
        for st in range(8):
            sq, h = divmod(st, PARTS)
            x16 = tokr[sq, h].astype(F32)
            c16 = cotr[sq, h].astype(F32)
            for part in range(2):
                cut = slice(part * 8, part * 8 + 8)
                du = jnp.concatenate(
                    [scr[j, pl.ds(st + part * 64, 8, stride=8), :] for j in range(scr.shape[0])],
                    axis=1,
                )
                normed, rstd = norm_of(x16[cut])
                dn = du * gain[...]
                m1 = jnp.mean(dn, axis=-1, keepdims=True)
                m2 = jnp.mean(dn * normed, axis=-1, keepdims=True)
                gy = jnp.where(step[cut] < lim[st], c16[cut] * scl[0], 0.0)
                outr[sq, h, cut, :] = rstd * (dn - m1 - normed * m2) + gy
                gsum = gsum + du * normed
                bsum = bsum + du
        ga[...] += gsum
        ba[...] += bsum

    seqs, parts, steps, width = tok.shape
    nat = pl.BlockSpec((seqs, parts, STEPS, width), lambda i: (0, 0, i, 0))
    pltpu.emit_pipeline(
        tile,
        grid=(steps // STEPS,),
        in_specs=[pl.BlockSpec((2, 128, width), lambda i: (0, i, 0)), nat, nat],
        out_specs=[nat],
    )(du2, tok, cot, out)
    sums[...] = jnp.zeros_like(sums)
    sums[4:5, :] = jnp.sum(ga[...], axis=0, keepdims=True)
    sums[5:6, :] = jnp.sum(ba[...], axis=0, keepdims=True)
    for s in range(4):
        a, mp = divmod(s, 2)
        rows = (
            accc[a][mp, 0:8, :],
            accb[a][mp, 0:8, :],
            accc[a][mp, 8:16, :],
            accb[a][mp, 8:16, :],
        )
        for j, val in enumerate(rows):
            val = jnp.sum(val, axis=0, keepdims=True)
            for mm in range(2):
                lane = pl.ds(core_lane(a, 2 * mp + mm, c), BLK)
                sums[j : j + 1, lane] = val[:, mm * BLK : (mm + 1) * BLK]


def norm_grads(ids, deps, du2, tok, cot, lim8, scale, gain, accb, accc):
    _, rows, width = du2.shape
    n = rows * width
    return call_flat(
        norm_grad_kernel, "norm_grads", ids, deps,
        [*far_in(du2, tok, cot), lim8, scale, gain, *accb, *accc],
        [ANY] * 3 + [SMEM] * 2 + [NEAR] * 5,
        [far(tok.shape, F32), sds((8, width), F32)], 14, cost(n * 20, n * 8),
        scratch=[
            pltpu.VMEM((8, width), F32),
            pltpu.VMEM((8, width), F32),
            pltpu.VMEM((width // BLK, 128, BLK), F32),
        ],
        out_specs=[ANY, NEAR],
    )


def activation_kernel(ids, tok, hown, hrcv, out, scr):
    c = ids[2]
    for s in range(4):
        a, mp = divmod(s, 2)
        for mm in range(2):
            for n, (ref, core) in enumerate(((hown, c), (hrcv, 1 - c))):
                scr[n] = ref[s, mm].astype(F32)
                lane = pl.ds(core_lane(a, 2 * mp + mm, core), BLK)
                for st in range(8):
                    sq, h = divmod(st, PARTS)
                    val = scr[n, pl.ds(st, STEPS, stride=8), :]
                    out[sq, h, :, lane] = tok[sq, h, :, lane].astype(F32) + val


def activations_of(ids, deps, tok, hown, hrcv):
    seqs, parts, steps, width = tok.shape
    tiles = steps // STEPS
    nat = pl.BlockSpec((seqs, parts, STEPS, width), lambda i, ids: (0, 0, i, 0))
    hspec = pl.BlockSpec((4, 2, 128, BLK), lambda i, ids: (0, 0, i, 0))
    n = seqs * parts * steps * width
    return call(
        activation_kernel, "activations_of", (tiles,), ids, deps, far_in(tok, hown, hrcv),
        [nat, hspec, hspec], nat, far(tok.shape, F32), 16, cost(n, n * 8),
        scratch=[pltpu.VMEM((2, 128, BLK), F32)],
    )


def assemble_kernel(counts, ids, *refs):
    out = refs[-1]
    c = ids[2]
    start = 0
    for b, n in enumerate(counts):
        group = refs[start : start + n]
        start += n
        a, core = b % 2, c if b < 2 else 1 - c
        for j in range(3):
            total = group[0][j]
            for ref in group[1:]:
                total = total + ref[j].astype(F32)
            lane = pl.multiple_of(j * 512 + a * BLK + core * 256, BLK)
            out[:, pl.ds(lane, BLK)] = total


def assemble(ids, deps, groups):
    rows = groups[0][0].shape[1]
    counts = [len(g) for g in groups]
    args = [ref for group in groups for ref in group]
    return call_flat(
        functools.partial(assemble_kernel, counts), "assemble", ids, deps, args,
        [NEAR] * len(args), sds((rows, 1536), F32), 16, cost(0, rows * 1536 * 8),
    )


def local(
    nseq,
    ndp,
    tokens,
    cotangent,
    weight,
    forget_peep,
    reset_peep,
    forget_bias,
    reset_bias,
    norm_gain,
    norm_bias,
    lengths,
):
    axes = ("seq", "dp")
    nz = ndp // 2
    seqs, span, width = tokens.shape
    sub = span // PARTS
    q = lax.axis_index("seq").astype(jnp.int32)
    dp = lax.axis_index("dp").astype(jnp.int32)
    z, c = dp // 2, dp % 2
    ids = jnp.stack([q, z, c])

    def table(move):
        pairs = []
        for qq in range(nseq):
            for zz in range(nz):
                for cc in range(2):
                    to = move(qq, zz, cc)
                    if to is not None:
                        pairs.append((qq * ndp + zz * 2 + cc, to[0] * ndp + to[1] * 2 + to[2]))
        return pairs

    def send(value, move):
        return lax.ppermute(value, axes, table(move))

    def to_core(qq, zz, cc):
        return (qq, zz, 1 - cc)

    def to_x(qq, zz, cc):
        return (qq ^ 1, zz, cc)

    def to_y(qq, zz, cc):
        return (qq ^ 2, zz, cc)

    def shift_z(k):
        return lambda qq, zz, cc: (qq, (zz + k) % nz, cc)

    def shift_zc(k):
        return lambda qq, zz, cc: (qq, (zz + k) % nz, 1 - cc)

    def shift_q(k):
        return lambda qq, zz, cc: (qq + k, zz, cc) if 0 <= qq + k < nseq else None

    mine, theirs = split_weight(ids, weight)
    recv = send(theirs, to_core)
    nat = (seqs, PARTS, sub, width)
    tok4 = tokens.reshape(nat)
    cot4 = cotangent.reshape(nat)
    tok_oth = send(tokens, to_core).reshape(nat)
    cot_cols = jnp.concatenate(
        [lax.dynamic_slice_in_dim(cotangent, m * 512 + (1 - c) * 256, 256, 2) for m in range(4)],
        axis=2,
    )
    cot_oth = send(cot_cols, to_core).reshape(seqs, PARTS, sub, width // 2)
    len_oth = send(lengths, to_core)

    lens = jnp.stack([lengths, len_oth])
    counts = jnp.sum(lens, axis=1).astype(F32)
    scale = (seqs * span * nseq) / counts
    lim16 = (
        lens[:, :, None] - q * span - sub * jnp.arange(PARTS, dtype=jnp.int32)[None, None, :]
    ).reshape(2, 8)
    spread_rows = lambda v: jnp.broadcast_to(v, (2, STEPS, 8, BLK)).reshape(256, BLK)
    step_in_tile = jnp.arange(STEPS, dtype=jnp.int32)[None, :, None, None]
    lim = spread_rows(lim16[:, None, :, None] - step_in_tile)
    scl = spread_rows(scale[:, None, None, None])

    lim8, scale1 = lim16[0], scale[:1]

    def by_core(vec):
        v = lax.dynamic_slice_in_dim(vec.reshape(4, 4, BLK), 2 * c, 2, 1)
        return v.transpose(1, 0, 2).reshape(1, width // 2)

    vf, vr, bfor, brst = (by_core(v) for v in (forget_peep, reset_peep, forget_bias, reset_bias))
    gain, bias = norm_gain.reshape(1, width), norm_bias.reshape(1, width)

    tail = [mine]

    def run(kernel, *head, rest=(), token=-1, after=(), big=False):
        out = kernel(*head, ids, (tail[0], *after), *rest)
        tail[0] = out[token] if isinstance(out, (list, tuple)) else out
        if big:
            (tail[0],) = far_in(tail[0])
        return out

    groups = [[cc + 2 * zz for zz in range(nz)] for cc in range(2)]

    def along_z(piece):
        if nz <= 4:
            return [send(piece, shift_z(-k)) for k in range(1, nz)]
        got = lax.all_gather(piece, "dp", axis=0, tiled=True, axis_index_groups=groups)
        n = got.shape[0] // nz
        twice = jnp.concatenate([got, got], axis=0)
        return [lax.dynamic_slice_in_dim(twice, (z + 1) * n, n * (nz - 1), 0)]

    def gather_1(s, zs, after=()):
        rel = run(plane_pieces, s, rest=(zs,), after=after)
        return rel, send(rel, to_x), send(rel, to_y)

    def gather_2(s, got, after=()):
        rel, gx, gy = got
        tox, toy = run(cross_pieces, s, rest=(gx, gy), after=after)
        return rel, gx, gy, send(tox, to_x), send(toy, to_y)

    def spread(both):
        return lax.all_gather(both, "seq")

    def run_project(s, weights, before=None, after=()):
        rest = (ub, ulo, weights, lim, vf, bfor, before)
        return run(project, s, nz, rest=rest, token=4, after=after)

    def run_states(a, fwd, got, held, after=()):
        rest = (fwd, ub, ulo, cot4, cot_oth, lim, scl, vr, brst, got, held)
        out = run(states, a, nseq, rest=rest, after=after)
        return {
            "h": out[:2], "mid": (out[2:5], out[5:8]), "dzr": out[8], "u": out[9],
            "lbs": out[10], "summ": out[11], "acc": out[12],
        }

    def run_adjoints(a, fwd, m, got, after=()):
        rest = (fwd, m["mid"], m["dzr"], m["u"], vf, vr, m["lbs"], got)
        du, dzc, dzf, acc = run(adjoints, a, nseq, rest=rest, after=after)
        return {"du": du, "dz": (dzc, dzf, m["dzr"]), "acc": acc}

    def sum_1(which, dz, keep=(), after=(), hold=False):
        own, xp, yp, da, db, *kept = run(
            weight_grad_part, which, nz, rest=(ubt, dz, keep), token=3, after=after
        )
        if hold:
            da, db = run(gate, rest=((da, db),))
        return (own, xp, yp, send(da, to_x), send(db, to_y)), kept

    def sum_2(got, after=()):
        own, xp, yp, ra, rb = got
        s1, s2 = run(relay_sums, rest=(xp, yp, ra, rb), after=after)
        return own, send(s1, to_x), send(s2, to_y)

    def fold(sets, d):
        kept, out = run(fold_z, d, rest=(sets,))
        return kept, send(out, lambda qq, zz, cc: (qq, zz ^ d, cc))

    def sum_3_now(got):
        if nz > 4:
            got, d = [got], nz // 2
            while d:
                got, d = fold(got, d), d // 2
            return run(fold_z, 0, rest=(got,))
        parts = list(run(plane_sums, nz, rest=got))
        return parts[:1] + [send(parts[k], shift_z(k)) for k in range(1, nz)]

    def fold_rest(got):
        d = nz // 4
        while d:
            got, d = fold(got, d), d // 2
        return got

    high, p0, p1 = run(quarter_of, rest=(mine, recv), after=(tok_oth, cot_oth, len_oth))
    z0 = along_z(p0)
    z1 = along_z(p1)
    ub, ubt, ulo = run(
        norm_tokens, rest=(tok4, tok_oth, gain, bias), big=True, after=(lim8, scale1, lim, scl)
    )
    g0 = gather_1(0, z0)
    g0 = gather_2(0, g0)
    g1 = gather_1(1, z1)
    z23 = along_z(run(hand_on, rest=(high,)))
    f0 = run_project(0, (mine, recv, *g0))
    g1 = gather_2(1, g1)
    f1 = run_project(1, (mine, recv, *g1), f0[4])
    got = spread(f1[4])
    g2 = gather_1(2, z23, after=(got,))
    m0 = run_states(0, (f0, f1), got, ())
    got = spread(m0["summ"])
    g2 = gather_2(2, g2, after=(got,))
    d0 = run_adjoints(0, (f0, f1), m0, got)
    s0, _ = sum_1("other", d0["dz"])
    g3 = gather_1(3, z23, after=g2[3:])
    f2 = run_project(2, (mine, recv, *g2))
    g3 = gather_2(3, g3)
    s0 = sum_2(s0)
    s1, first = sum_1("own", d0["dz"], (d0["du"],))
    f3 = run_project(3, (mine, recv, *g3), f2[4])
    got = spread(f3[4])
    s1 = sum_2(s1, after=(got,))
    m1 = run_states(1, (f2, f3), got, m0["h"], after=s0[1:])
    s01 = fold([s0, s1], nz // 2)
    hrcv = send(run(gate, rest=(m1["h"][1:], "far"))[0], to_core)
    got = spread(run(hand_on, rest=(m1["summ"],)))
    d1 = run_adjoints(1, (f2, f3), m1, got)
    s2, _ = sum_1("other", d1["dz"])
    s3, _ = sum_1("own", d1["dz"], after=(hrcv,))
    s2 = sum_2(s2)
    s01 = fold_rest(s01)
    second = (*d1["dz"], d1["du"])
    ws = (f0[5], f1[5], f2[5], f3[5])
    du2 = run(unit_grads, 1, rest=(first, second, ws, ()), big=True)
    s3 = sum_2(s3)
    s2 = fold([s2], nz // 2)
    du2 = run(unit_grads, 0, rest=(first, second, ws, (du2,)), big=True)
    s0, s1 = run(fold_z, 0, rest=(s01,))
    s0 = send(s0, to_core)
    s3 = sum_3_now(s3)
    cores = [[2 * zz, 2 * zz + 1] for zz in range(nz)]
    du2 = lax.all_to_all(du2, "dp", 0, 0, axis_index_groups=cores, tiled=True)
    activations = run(activations_of, rest=(tok4, m1["h"][0], hrcv), big=True)
    s2 = fold_rest(s2)
    input_grad, sums = run(
        norm_grads,
        rest=(
            du2, tok4, cot4, lim8, scale1, gain, (m0["acc"], m1["acc"]), (d0["acc"], d1["acc"])
        ),
        after=(s0,),
    )
    s2 = send(run(fold_z, 0, rest=(s2,))[0], to_core)
    s3 = run(fold_z, 0, rest=([s3],))
    if nz <= 4:
        sums = run(add_up, rest=(sums, *[send(sums, shift_z(k)) for k in range(1, nz)]))
    else:
        for b in range((nz - 1).bit_length()):
            hop = lambda qq, zz, cc, b=1 << b: (qq, zz ^ b, cc)
            sums = run(add_up, rest=(sums, send(sums, hop)))
    moved = [send(sums, lambda qq, zz, cc, b=b: (qq ^ b, zz, cc)) for b in range(1, nseq)]
    sums = run(add_up, rest=(sums, *moved))
    moved = send(sums, to_core)
    sums = run(add_up, rest=(sums, moved))
    weight_grad = run(assemble, rest=(([s1], s3, [s0], [s2]),))
    shape = tokens.shape
    return (
        activations.reshape(shape),
        input_grad.reshape(shape),
        weight_grad,
        sums[0],
        sums[1],
        sums[2],
        sums[3],
        sums[4],
        sums[5],
    )


def solution(mesh):
    whole = P("dp", "seq", None)
    in_specs = (whole, whole, P("dp", None)) + (P(),) * 6 + (P("dp"),)
    out_specs = (whole, whole, P("dp", "seq")) + (P(),) * 6
    step = functools.partial(local, mesh.shape["seq"], mesh.shape["dp"])
    return jax.shard_map(step, mesh=mesh, in_specs=in_specs, out_specs=out_specs, check_vma=False)
```

```python
import functools

import jax
import jax.numpy as jnp
from jax import lax
from jax.experimental import pallas as pl
from jax.experimental.pallas import tpu as pltpu
from jax.sharding import PartitionSpec as P

EPS = 1e-05
F32 = jnp.float32
BF = jnp.bfloat16
STEPS = 16
BLK = 128
GATES = 3
QUARTERS = 4
PARTS = 4


def params(mib, dims=1):
    return pltpu.CompilerParams(
        vmem_limit_bytes=mib * 1024 * 1024, dimension_semantics=("arbitrary",) * dims
    )


def cost(flops, bytes_accessed, transcendentals=0):
    return pl.CostEstimate(
        flops=int(flops), bytes_accessed=int(bytes_accessed), transcendentals=int(transcendentals)
    )


def sds(shape, dtype):
    return jax.ShapeDtypeStruct(shape, dtype)


def far(shape, dtype):
    return pltpu.HBM(shape, dtype)


def near(shape, dtype):
    return pltpu.VMEM(shape, dtype)


def far_in(*values):
    return [pltpu.with_memory_space_constraint(v, pltpu.HBM) for v in values]


def near_in(*values):
    return [pltpu.with_memory_space_constraint(v, pltpu.VMEM) for v in values]


ANY = pl.BlockSpec(memory_space=pl.ANY)
NEAR = pl.BlockSpec(memory_space=pltpu.VMEM)
SMEM = pl.BlockSpec(memory_space=pltpu.SMEM)


def ordered(kernel, deps):
    n = len(deps)

    def body(ids, *refs):
        return kernel(ids, *refs[n:])

    return body, list(deps), [ANY] * n


def call(kernel, name, grid, ids, deps, args, in_specs, out_specs, out_shape, mib, est, scratch=()):
    body, deps, dep_specs = ordered(kernel, deps)
    return pl.pallas_call(
        body,
        grid_spec=pltpu.PrefetchScalarGridSpec(
            num_scalar_prefetch=1,
            grid=grid,
            in_specs=dep_specs + in_specs,
            out_specs=out_specs,
            scratch_shapes=list(scratch),
        ),
        out_shape=out_shape,
        compiler_params=params(mib, len(grid)),
        cost_estimate=est,
        name=name,
    )(ids, *deps, *args)


def call_flat(kernel, name, ids, deps, args, in_specs, out_shape, mib, est, scratch=(), out_specs=None, aliases=None):
    body, deps, dep_specs = ordered(kernel, deps)
    many = isinstance(out_shape, (list, tuple))
    if out_specs is None:
        out_specs = [NEAR] * len(out_shape) if many else NEAR
    shift = 1 + len(deps)
    return pl.pallas_call(
        body,
        in_specs=[SMEM] + dep_specs + in_specs,
        out_specs=out_specs,
        out_shape=out_shape,
        scratch_shapes=list(scratch),
        input_output_aliases={k + shift: v for k, v in (aliases or {}).items()},
        compiler_params=pltpu.CompilerParams(vmem_limit_bytes=mib * 1024 * 1024),
        cost_estimate=est,
        name=name,
    )(ids, *deps, *args)


def split_kernel(ids, w, mine, theirs):
    c = ids[2]
    for s in range(4):
        a, mp = divmod(s, 2)
        for g in range(GATES):
            for mm in range(2):
                dst = s * 768 + g * 256 + mm * BLK
                base = g * 2048 + (2 * mp + mm) * 512 + a * BLK
                here = pl.multiple_of(base + c * 256, BLK)
                there = pl.multiple_of(base + (1 - c) * 256, BLK)
                mine[:, dst : dst + BLK] = w[:, pl.ds(here, BLK)]
                theirs[:, dst : dst + BLK] = w[:, pl.ds(there, BLK)]


def split_weight(ids, weight):
    rows, cols = weight.shape
    tile = rows // 2
    spec = pl.BlockSpec((tile, cols // 2), lambda i, ids: (i, 0))
    return call(
        split_kernel, "split_weight", (2,), ids, (), far_in(weight),
        [pl.BlockSpec((tile, cols), lambda i, ids: (i, 0))], [spec, spec],
        [sds((rows, cols // 2), BF)] * 2, 16, cost(0, rows * cols * 4),
    )


def quarter_kernel(ids, mine, recv, high, p0, p1):
    q, c = ids[0], ids[2]
    half = high.shape[0]
    at = pl.ds(pl.multiple_of(lax.rem(q, 2) * half, half), half)
    first = (lax.div(q, 2) == c).astype(jnp.int32) == 1
    val = jnp.where(first, mine[at, :], recv[at, :])
    high[...] = val[:, 1536:]
    p0[...] = val[:, :768]
    p1[...] = val[:, 768:1536]


def quarter_of(ids, deps, mine, recv):
    rows, cols = mine.shape
    half = rows // 2
    return call_flat(
        quarter_kernel, "quarter_of", ids, deps, [mine, recv], [NEAR, NEAR],
        [sds((half, 1536), BF), sds((half, 768), BF), sds((half, 768), BF)], 8,
        cost(0, rows * cols * 4),
    )


def columns_kernel(ids, src, dst):
    there = 1 - ids[2]
    for m in range(QUARTERS):
        lane = pl.ds(pl.multiple_of(m * 512 + there * 256, BLK), 256)
        dst[:, :, m * 256 : (m + 1) * 256] = src[:, :, lane]


def other_columns(ids, deps, value):
    seqs, span, width = value.shape
    step = span // 4
    return call(
        columns_kernel, "other_columns", (4,), ids, deps, far_in(value),
        [pl.BlockSpec((seqs, step, width), lambda i, ids: (0, i, 0))],
        pl.BlockSpec((seqs, step, width // 2), lambda i, ids: (0, i, 0)),
        far((seqs, span, width // 2), value.dtype), 12, cost(0, value.size * 3),
    )


def copy_kernel(ids, src, dst):
    dst[...] = src[...]


def hand_on(ids, deps, value):
    return call_flat(
        copy_kernel, "hand_on", ids, deps, [value], [NEAR], sds(value.shape, value.dtype), 16,
        cost(0, value.size * 4),
    )


def gate_kernel(ids, *refs):
    pass


def gate(ids, deps, values, hold=None):
    shape = {None: sds, "far": far, "near": near}[hold]
    held = {None: lambda *v: list(v), "far": far_in, "near": near_in}[hold]
    return call_flat(
        gate_kernel, "gate", ids, deps, held(*values), [ANY] * len(values),
        [shape(v.shape, v.dtype) for v in values], 4, cost(0, 1), out_specs=[ANY] * len(values),
        aliases={n: n for n in range(len(values))},
    )


def add_kernel(ids, *refs):
    total = refs[0][...]
    for ref in refs[1:-1]:
        total = total + ref[...]
    refs[-1][...] = total


def add_up(ids, deps, *values):
    a = values[0]
    return call_flat(
        add_kernel, "add_up", ids, deps, list(values), [NEAR] * len(values), sds(a.shape, a.dtype),
        4, cost(a.size, a.size * 4 * len(values)),
    )


def plane_kernel(s, ids, *refs):
    rel = refs[-1]
    row = 0
    for ref in refs[:-1]:
        lane = s % 2 * 768 if ref.shape[1] > 768 else 0
        rel[row : row + ref.shape[0], :] = ref[:, lane : lane + 768]
        row += ref.shape[0]


def plane_pieces(s, ids, deps, parts):
    rows = sum(p.shape[0] for p in parts)
    return call_flat(
        functools.partial(plane_kernel, s), f"plane_pieces_{s}", ids, deps, list(parts),
        [NEAR] * len(parts), sds((rows, 768), BF), 8, cost(0, rows * 768 * 4),
    )


def cross_kernel(ids, gx, gy, tox, toy):
    tox[...] = gy[:, :384]
    toy[...] = gx[:, 384:]


def cross_pieces(s, ids, deps, gx, gy):
    rows = gx.shape[0]
    return call_flat(
        cross_kernel, f"cross_pieces_{s}", ids, deps, [gx, gy], [NEAR, NEAR],
        [sds((rows, 384), BF)] * 2, 16, cost(0, rows * 768 * 4),
    )


def norm_of(x):
    mean = jnp.mean(x, axis=-1, keepdims=True)
    centered = x - mean
    var = jnp.mean(centered * centered, axis=-1, keepdims=True)
    rstd = lax.rsqrt(var + EPS)
    return centered * rstd, rstd


def norm_kernel(ids, own, other, gain, bias, ub, ubt, ulo, scr):
    c = ids[2]
    seqs = own.shape[0]
    for k, ref in enumerate((own, other)):
        for st in range(8):
            sq, h = divmod(st, PARTS)
            normed, _ = norm_of(ref[sq, h].astype(F32))
            unit = normed * gain[...] + bias[...]
            for j in range(scr.shape[0]):
                scr[j, pl.ds(k * 128 + st, STEPS, stride=8), :] = unit[:, j * BLK : (j + 1) * BLK]
    for j in range(scr.shape[0]):
        low = scr[j].astype(BF)
        ub[0, :, :, j * BLK : (j + 1) * BLK] = low.reshape(2, 128, BLK)
        ubt[j * BLK : (j + 1) * BLK, :] = low.T
    for a in range(2):
        for m in range(QUARTERS):
            unit = scr[m * 4 + a + 2 * c]
            rest = (unit - unit.astype(BF).astype(F32)).astype(BF)
            dst = (a * QUARTERS + m) * BLK
            ulo[0, :, :, dst : dst + BLK] = rest.reshape(2, 128, BLK)


def tile_block(cols):
    return pl.BlockSpec((1, 2, 128, cols), lambda i, ids: (i, 0, 0, 0))


def norm_tokens(ids, deps, own, other, gain, bias):
    seqs, parts, steps, width = own.shape
    rows = seqs * parts * steps
    tiles = steps // STEPS
    nat = pl.BlockSpec((seqs, parts, STEPS, width), lambda i, ids: (0, 0, i, 0))
    vec = pl.BlockSpec((1, width), lambda i, ids: (0, 0))
    return call(
        norm_kernel, "norm_tokens", (tiles,), ids, deps, [*far_in(own, other), gain, bias],
        [nat, nat, vec, vec],
        [
            tile_block(width),
            pl.BlockSpec((width, 256), lambda i, ids: (0, i)),
            tile_block(width // 2),
        ],
        [
            far((tiles, 2, 128, width), BF),
            far((width, 2 * rows), BF),
            far((tiles, 2, 128, width // 2), BF),
        ],
        20, cost(rows * width * 20, rows * width * 14),
        scratch=[pltpu.VMEM((width // BLK, 256, BLK), F32)],
    )


def flat(ref):
    value = ref[...]
    return value.reshape(256, value.shape[-1])


def core_lane(a, m, c):
    return pl.multiple_of(m * 512 + a * BLK + c * 256, BLK)


def pairs():
    for tp in range(STEPS // 2):
        for k in range(2):
            yield k, tp * 16, k * 128 + tp * 16


def live_pair(lim, row, tile):
    live = lim[row : row + 16, :] > tile * STEPS
    return jnp.concatenate([live, live], axis=1)


def fold_streams(pr, lc, ahead):
    out = []
    order = range(PARTS) if ahead else range(PARTS - 1, -1, -1)
    for sq in range(2):
        tp = tl = None
        for h in order:
            n = sq * PARTS + h
            p, l = pr[n : n + 1], lc[n : n + 1]
            tp, tl = (p, l) if tp is None else ((p * tp, p * tl + l) if ahead else (p * tp, l + p * tl))
        out.append((tp, tl))
    return out


def proj_kernel(s, nz, joined, ids, ub, ulo, *rest):
    n_w = 1 if joined else 7
    weights, rest = rest[:n_w], rest[n_w:]
    lim, vf, bfor = rest[:3]
    rest = rest[3:]
    before = rest[0] if s % 2 else None
    cand_far, decay, rpre_far, plout, summ = rest[s % 2 : s % 2 + 5]
    rest = rest[s % 2 + 5 :]
    if joined:
        zbuf, prod, loc, wbuf, sems = rest
    else:
        wall, zbuf, prod, loc, wbuf, sems = rest
    tiles = decay.shape[0]
    width = wbuf.shape[0]
    q, z, c = ids[0], ids[1], ids[2]
    a, mp = divmod(s, 2)
    cols = slice(mp * 768, mp * 768 + 768)
    copies = []

    def put(src, row, rows, lo=0, hi=768):
        dst = wbuf.at[pl.ds(row, rows), lo:hi]
        copy = pltpu.make_async_copy(src, dst, sems.at[len(copies)])
        copy.start()
        copies.append(copy)

    if joined:
        put(weights[0].at[:, cols], 0, width)
    else:
        mine, recv, rel, gx, gy, dx, dy = weights
        zb = width // nz
        zb2, qb = zb // 2, zb // 4
        mult = lambda v: pl.multiple_of(v, qb)
        put(mine.at[:, s * 768 : (s + 1) * 768], mult(z * zb + c * zb2), zb2)
        put(recv.at[:, s * 768 : (s + 1) * 768], mult(z * zb + (1 - c) * zb2), zb2)
        for r in range(1, nz):
            base = lax.rem(z + r, nz) * zb
            lo, hi = (r - 1) * qb, r * qb
            put(rel.at[lo:hi, :], mult(base + q * qb), qb)
            put(gx.at[lo:hi, :], mult(base + (q ^ 1) * qb), qb)
            put(gy.at[lo:hi, :], mult(base + (q ^ 2) * qb), qb)
            put(dx.at[lo:hi, :], mult(base + (q ^ 3) * qb), qb, 0, 384)
            put(dy.at[lo:hi, :], mult(base + (q ^ 3) * qb), qb, 384, 768)
    for copy in copies:
        copy.wait()
    if not joined:
        keep = pltpu.make_async_copy(wbuf, wall, sems.at[len(copies)])
        keep.start()
    prod[...] = jnp.ones_like(prod)
    loc[...] = jnp.zeros_like(loc)

    def tile(ubr, ulor, cand, rpre):
        i = pl.program_id(0)
        zbuf[:, :768] = jnp.dot(flat(ubr), wbuf[...], preferred_element_type=F32)
        low = flat(ulor).astype(F32)
        for mm in range(2):
            high = ubr[:, :, :, pl.ds(core_lane(a, 2 * mp + mm, c), BLK)].reshape(256, BLK)
            zbuf[:, 768 + mm * BLK : 768 + (mm + 1) * BLK] = (
                high.astype(F32) + low[:, mm * BLK : (mm + 1) * BLK]
            )
        pr = [prod[0:8, :], prod[8:16, :]]
        lc = [loc[0:8, :], loc[8:16, :]]
        for k, r0, row in pairs():
            cd = zbuf[row : row + 16, :256]
            logit = zbuf[row : row + 16, 256:512] + vf[...] * zbuf[row : row + 16, 768:] + bfor[...]
            dec = jnp.where(live_pair(lim, row, i), jax.nn.sigmoid(logit), 1.0)
            inj = (1.0 - dec) * cd
            cand[0, k, r0 : r0 + 16, :] = cd
            decay[i, k, r0 : r0 + 16, :] = dec
            rpre[0, k, r0 : r0 + 16, :] = zbuf[row : row + 16, 512:768]
            for t in range(2):
                d = dec[t * 8 : t * 8 + 8]
                lc[k] = d * lc[k] + inj[t * 8 : t * 8 + 8]
                pr[k] = d * pr[k]
        for k in range(2):
            prod[k * 8 : k * 8 + 8, :] = pr[k]
            loc[k * 8 : k * 8 + 8, :] = lc[k]

    pltpu.emit_pipeline(
        tile,
        grid=(tiles,),
        in_specs=[
            pl.BlockSpec((1, 2, 128, width), lambda i: (i, 0, 0, 0)),
            pl.BlockSpec((1, 2, 128, 256), lambda i: (i, 0, 0, s)),
        ],
        out_specs=[pl.BlockSpec((1, 2, 128, 256), lambda i: (i, 0, 0, 0))] * 2,
    )(ub, ulo, cand_far, rpre_far)
    if s % 2:
        summ[0] = before[0]
    plout[0:16, :] = prod[...]
    plout[16:32, :] = loc[...]
    for k in range(2):
        pr, lc = prod[k * 8 : k * 8 + 8, :], loc[k * 8 : k * 8 + 8, :]
        for sq, (tp, tl) in enumerate(fold_streams(pr, lc, True)):
            ks = k * 2 + sq
            summ[s % 2, ks : ks + 1, :] = tp
            summ[s % 2, 4 + ks : 5 + ks, :] = tl
    if not joined:
        keep.wait()


def project(s, nz, ids, deps, ub, ulo, weights, lim, vf, bfor, before):
    tiles, _, _, width = ub.shape
    joined = len(weights) == 1
    shape = (tiles, 2, 128, 256)
    rows = tiles * 256
    chan = slice(s * 256, s * 256 + 256)
    args = far_in(ub, ulo, *weights) + [lim, vf[:, chan], bfor[:, chan]]
    in_specs = [ANY] * (2 + len(weights)) + [NEAR] * 3
    if s % 2:
        args.append(before)
        in_specs.append(NEAR)
    out_shape = [far(shape, F32), near(shape, F32), far(shape, F32)]
    out_shape += [near((32, 256), F32), near((2, 8, 256), F32)]
    out_specs = [ANY, NEAR, ANY, NEAR, NEAR]
    if not joined:
        out_shape.append(far((width, 768), BF))
        out_specs.append(ANY)
    return call_flat(
        functools.partial(proj_kernel, s, nz, joined), f"project_{s}", ids, deps, args, in_specs,
        out_shape, 12, cost(2 * rows * width * 768, rows * width * 2 + width * 768 * 4),
        scratch=[
            pltpu.VMEM((256, 1024), F32),
            pltpu.VMEM((16, 256), F32),
            pltpu.VMEM((16, 256), F32),
            pltpu.VMEM((width, 768), BF),
            pltpu.SemaphoreType.DMA((3 + 5 * (nz - 1),)),
        ],
        out_specs=out_specs,
    )


def halves(v):
    return v[:8], v[8:]


def enter(got, n, ahead, q, count):
    value = jnp.zeros((4, 256), F32)
    for j in range(count) if ahead else range(count - 1, -1, -1):
        used = (j < q) if ahead else (j > q)
        longer = got[j, n, 4:8, :] + got[j, n, 0:4, :] * value
        value = jnp.where(used, longer, value)
    return value


def state_kernel(a, count, held, ids, *refs):
    fwd = (refs[0:4], refs[4:8])
    ub, ulo, cot_own, cot_oth, lim, scl, vr, br, got = refs[8:17]
    rest = refs[17 + (2 if held else 0) :]
    hown, hoth = rest[:2]
    out = (rest[2:5], rest[5:8])
    dzr, uu, lbs, summ, acc, st, pp, lb, ac, scr = rest[8:]
    tiles = dzr.shape[0]
    q, c = ids[0], ids[2]
    for n in range(2):
        cand_far, decay, rpre_far, plin = fwd[n]
        bc, dstate, du0 = out[n]
        lanes = slice(n * 256, n * 256 + 256)
        carry = enter(got, n, True, q, count)
        for ks in range(4):
            cc = carry[ks : ks + 1]
            for h in range(PARTS):
                m = ks * PARTS + h
                st[m : m + 1, :] = cc
                cc = plin[m : m + 1, :] * cc + plin[16 + m : 17 + m, :]
        pp[...] = jnp.ones_like(pp)
        lb[...] = jnp.zeros_like(lb)
        ac[...] = jnp.zeros_like(ac)

        def tile(cand, rpre, u0, u1, ul, own0, own1, oth0, oth1, ho, ht):
            i = pl.program_id(0)
            for k, pair in enumerate(((own0, own1), (oth0, oth1))):
                for b, ref in enumerate(pair):
                    for m in range(8):
                        sq, h = divmod(m, PARTS)
                        scr[b, pl.ds(k * 128 + m, STEPS, stride=8), :] = ref[sq, h].astype(F32)
            cur = [st[0:8, :], st[8:16, :]]
            p = [pp[0:8, :], pp[8:16, :]]
            l = [lb[0:8, :], lb[8:16, :]]
            peep = [jnp.zeros((8, 256), F32)] * 2
            bias = [jnp.zeros((8, 256), F32)] * 2
            wr, wb = vr[:, lanes], br[:, lanes]
            for k, r0, row in pairs():
                at = slice(r0, r0 + 16)
                dec = decay[i, k, at, :]
                cd = cand[0, k, at, :]
                inj = (1.0 - dec) * cd
                befores, states = [], []
                for d, v in zip(halves(dec), halves(inj)):
                    befores.append(cur[k])
                    cur[k] = d * cur[k] + v
                    states.append(cur[k])
                before = jnp.concatenate(befores, axis=0)
                state = jnp.concatenate(states, axis=0)
                low = jnp.concatenate([u0[0, k, at, :], u1[0, k, at, :]], axis=1)
                uu[i, k, at, lanes] = low
                u = low.astype(F32) + ul[0, k, at, :].astype(F32)
                live = lim[row : row + 16, :] > i * STEPS
                sc = jnp.where(live, scl[row : row + 16, :], 0.0)
                gy = jnp.concatenate(
                    [scr[0, row : row + 16, :] * sc, scr[1, row : row + 16, :] * sc], axis=1
                )
                r = jax.nn.sigmoid(rpre[0, k, at, :] + wr * before + wb)
                gap = state - u
                hv = jnp.where(jnp.concatenate([live, live], axis=1), u + r * gap, 0.0).astype(BF)
                href = ht if k else ho
                href[0, 0, at, :] = hv[:, :BLK]
                href[0, 1, at, :] = hv[:, BLK:]
                ds = gy * r
                drl = ds * (1.0 - r) * gap
                sr = dec * ds + wr * drl
                dstate[i, k, at, :] = ds
                bc[i, k, at, :] = before - cd
                du0[i, k, at, :] = (gy - ds).astype(BF)
                dzr[i, k, at, lanes] = drl.astype(BF)
                for d, v in zip(halves(dec), halves(sr)):
                    l[k] = l[k] + p[k] * v
                    p[k] = p[k] * d
                for e, w in zip(halves(drl), befores):
                    peep[k] = peep[k] + e * w
                    bias[k] = bias[k] + e
            for k in range(2):
                st[k * 8 : k * 8 + 8, :] = cur[k]
                pp[k * 8 : k * 8 + 8, :] = p[k]
                lb[k * 8 : k * 8 + 8, :] = l[k]
            ac[0:8, :] += peep[0] + peep[1]
            ac[8:16, :] += bias[0] + bias[1]

        nat = cot_own.shape[:2]

        def unit(mm):
            return pl.BlockSpec(
                (1, 2, 128, BLK), lambda i: (i, 0, 0, (2 * n + mm) * 4 + 2 * c + a)
            )

        def tail():
            return pl.BlockSpec((1, 2, 128, 256), lambda i: (i, 0, 0, 2 * a + n))

        def nat_own(mm):
            return pl.BlockSpec(
                (*nat, STEPS, BLK), lambda i: (0, 0, i, (2 * n + mm) * 4 + 2 * c + a)
            )

        def nat_oth(mm):
            return pl.BlockSpec((*nat, STEPS, BLK), lambda i: (0, 0, i, (2 * n + mm) * 2 + a))

        one = pl.BlockSpec((1, 2, 128, 256), lambda i: (i, 0, 0, 0))
        hspec = pl.BlockSpec((1, 2, 128, BLK), lambda i: (2 * a + n, 0, i, 0))
        pltpu.emit_pipeline(
            tile,
            grid=(tiles,),
            in_specs=[one, one, unit(0), unit(1), tail(), nat_own(0), nat_own(1), nat_oth(0), nat_oth(1)],
            out_specs=[hspec, hspec],
        )(cand_far, rpre_far, ub, ub, ulo, cot_own, cot_own, cot_oth, cot_oth, hown, hoth)
        acc[n] = ac[...]
        lbs[n] = lb[...]
        for k in range(2):
            p, l = pp[k * 8 : k * 8 + 8, :], lb[k * 8 : k * 8 + 8, :]
            for sq, (tp, tl) in enumerate(fold_streams(p, l, False)):
                ks = k * 2 + sq
                summ[n, ks : ks + 1, :] = tp
                summ[n, 4 + ks : 5 + ks, :] = tl


def states(a, count, ids, deps, fwd, ub, ulo, cot_own, cot_oth, lim, scl, vr, br, got, held):
    tiles = ub.shape[0]
    rows = tiles * 128
    one = (tiles, 2, 128, 256)
    two = (tiles, 2, 128, 512)
    chan = slice(a * 512, a * 512 + 512)
    args, in_specs = [], []
    for f in fwd:
        args += far_in(f[0]) + near_in(f[1]) + far_in(f[2]) + [f[3]]
        in_specs += [ANY, NEAR, ANY, NEAR]
    args += far_in(ub, ulo, cot_own, cot_oth) + [lim, scl, vr[:, chan], br[:, chan], got]
    in_specs += [ANY] * 4 + [NEAR] * 5
    aliases = {}
    if held:
        aliases = {len(args): 0, len(args) + 1: 1}
        args += far_in(*held)
        in_specs += [ANY] * 2
    small = near((2, 16, 256), F32)
    return call_flat(
        functools.partial(state_kernel, a, count, bool(held)), f"states_{a}", ids, deps, args,
        in_specs,
        [far((4, 2, rows, BLK), BF)] * 2
        + [near(one, F32), near(one, F32), near(one, BF)] * 2
        + [near(two, BF)] * 2
        + [small, near((2, 8, 256), F32), small],
        10, cost(rows * 1024 * 60, rows * 1024 * 10, rows * 1024 * 2),
        scratch=[pltpu.VMEM((16, 256), F32)] * 4 + [pltpu.VMEM((2, 256, BLK), F32)],
        out_specs=[ANY] * 2 + [NEAR] * 11,
        aliases=aliases,
    )


def adjoint_kernel(count, ids, *refs):
    ins = (refs[0:5], refs[5:10])
    dzr, uu, vf, vr, lbs, got, du, dzc, dzf, acc, adj = refs[10:]
    tiles = du.shape[0]
    q = ids[0]
    for n in range(2):
        decay, bc, dstate, du0, plin = ins[n]
        lanes = slice(n * 256, n * 256 + 256)
        wf, wr = vf[:, lanes], vr[:, lanes]
        after = enter(got, n, False, q, count)
        for ks in range(4):
            cc = after[ks : ks + 1]
            for h in range(PARTS - 1, -1, -1):
                m = ks * PARTS + h
                adj[m : m + 1, :] = cc
                cc = lbs[n, m : m + 1, :] + plin[m : m + 1, :] * cc

        def tile(step, state):
            i = tiles - 1 - step
            cur, peep, bias = [state[0], state[1]], state[2], state[3]
            for k, r0, _ in reversed(list(pairs())):
                at = slice(r0, r0 + 16)
                dec = decay[i, k, at, :]
                ds = dstate[i, k, at, :]
                sr = dec * ds + wr * dzr[i, k, at, lanes].astype(F32)
                late = ds[8:] + cur[k]
                cur[k] = dec[8:] * cur[k] + sr[8:]
                early = ds[:8] + cur[k]
                cur[k] = dec[:8] * cur[k] + sr[:8]
                dcand = jnp.concatenate([early, late], axis=0) * (1.0 - dec)
                dfl = dcand * bc[i, k, at, :] * dec
                dzc[i, k, at, lanes] = dcand.astype(BF)
                dzf[i, k, at, lanes] = dfl.astype(BF)
                du[i, k, at, lanes] = (du0[i, k, at, :].astype(F32) + dfl * wf).astype(BF)
                w = dfl * uu[i, k, at, lanes].astype(F32)
                peep = peep + (w[:8] + w[8:])
                bias = bias + (dfl[:8] + dfl[8:])
            return cur[0], cur[1], peep, bias

        zero = jnp.zeros((8, 256), F32)
        end = lax.fori_loop(0, tiles, tile, (adj[0:8, :], adj[8:16, :], zero, zero))
        acc[n, 0:8, :] = end[2]
        acc[n, 8:16, :] = end[3]


def adjoints(a, count, ids, deps, fwd, mid, dzr, uu, vf, vr, lbs, got):
    tiles = uu.shape[0]
    rows = tiles * 128
    shape = (tiles, 2, 128, 512)
    args = []
    for f, m in zip(fwd, mid):
        args += near_in(f[1], *m) + [f[3]]
    chan = slice(a * 512, a * 512 + 512)
    args += near_in(dzr, uu) + [vf[:, chan], vr[:, chan], lbs, got]
    return call_flat(
        functools.partial(adjoint_kernel, count), f"adjoints_{a}", ids, deps, args,
        [NEAR] * len(args),
        [near(shape, BF)] * 3 + [near((2, 16, 256), F32)],
        6, cost(rows * 1024 * 20, rows * 1024 * 4), scratch=[pltpu.VMEM((16, 256), F32)],
    )


def wgrad_kernel(which, nz, n_kept, ids, ubt, dzc, dzf, dzr, *rest):
    kept, rest = rest[: max(n_kept - 3, 0)], rest[max(n_kept - 3, 0) :]
    own, xp, yp, da, db = rest[:5]
    scr, sems = rest[5 + n_kept :]
    copies = [
        pltpu.make_async_copy(src, dst, sems.at[n])
        for n, (src, dst) in enumerate(zip((dzc, dzf, dzr, *kept), rest[5 : 5 + n_kept]))
    ]
    for copy in copies:
        copy.start()
    q, c = ids[0], ids[2]
    rh = 1 - c if which == "other" else c
    half = scr.shape[0]
    rows = ubt.shape[1]

    def tile(lhs):
        i = pl.program_id(0)
        for g, dz in enumerate((dzc, dzf, dzr)):
            rhs = dz[...].reshape(rows, 512)
            scr[:, g * 512 : (g + 1) * 512] = jnp.dot(
                lhs[...], rhs, preferred_element_type=F32
            ).astype(BF)

        def block(r, j):
            return scr[:, pl.ds(pl.multiple_of(((q ^ r) * 3 + j) * BLK, BLK), BLK)]

        at = pl.ds(pl.multiple_of(i * half, half), half)
        for j in range(3):
            own[j, at, :] = block(0, j)
            xp[j, at, :] = block(1, j)
            yp[j, at, :] = block(2, j)

        @pl.when(i < nz // 2)
        def _():
            for j in range(3):
                da[j, at, :] = block(3, j)

        @pl.when(i >= nz // 2)
        def _():
            back = pl.ds(pl.multiple_of((i - nz // 2) * half, half), half)
            for j in range(3):
                db[j, back, :] = block(3, j)

    pltpu.emit_pipeline(
        tile, grid=(nz,), in_specs=[pl.BlockSpec((half, rows), lambda i: (2 * i + rh, 0))]
    )(ubt)
    for copy in copies:
        copy.wait()


def weight_grad_part(which, nz, ids, deps, ubt, dz, keep=()):
    width, rows = ubt.shape
    half = width // nz // 2
    kept = (*dz, *keep) if keep else ()
    return call_flat(
        functools.partial(wgrad_kernel, which, nz, len(kept)), "weight_grad_part", ids, deps,
        [*far_in(ubt), *near_in(*dz, *keep)], [ANY] + [NEAR] * (3 + len(keep)),
        [sds((3, nz * half, BLK), BF)] * 3
        + [sds((3, nz * half // 2, BLK), BF)] * 2
        + [far(v.shape, v.dtype) for v in kept],
        10, cost(2 * rows * nz * half * 1536, rows * width + width * 1536),
        scratch=[pltpu.VMEM((half, 1536), BF), pltpu.SemaphoreType.DMA((4,))],
        out_specs=[NEAR] * 5 + [ANY] * len(kept),
    )


def relay_kernel(ids, xp, yp, ra, rb, s1, s2):
    half = ra.shape[1]
    s1[:, :half, :] = xp[:, :half, :]
    s1[:, half:, :] = (xp[:, half:, :].astype(F32) + rb[...].astype(F32)).astype(BF)
    s2[:, :half, :] = (yp[:, :half, :].astype(F32) + ra[...].astype(F32)).astype(BF)
    s2[:, half:, :] = yp[:, half:, :]


def relay_sums(ids, deps, xp, yp, ra, rb):
    rows = xp.shape[1]
    return call_flat(
        relay_kernel, "relay_sums", ids, deps, [xp, yp, ra, rb], [NEAR] * 4,
        [sds(xp.shape, BF)] * 2, 16, cost(rows * 768, rows * 384 * 10),
    )


def plane_sum_kernel(nz, ids, own, r1, r2, *outs):
    rows = outs[0].shape[1]
    for k, out in enumerate(outs):
        start = lax.rem(ids[1] + k, nz) * rows
        at = pl.ds(pl.multiple_of(start, rows), rows)
        tot = own[:, at, :].astype(F32) + r1[:, at, :].astype(F32) + r2[:, at, :].astype(F32)
        out[...] = tot.astype(out.dtype)


def plane_sums(nz, ids, deps, own, r1, r2):
    rows = own.shape[1] // nz
    return call_flat(
        functools.partial(plane_sum_kernel, nz), "plane_sums", ids, deps, [own, r1, r2], [NEAR] * 3,
        [sds((3, rows, BLK), F32)] + [sds((3, rows, BLK), BF)] * (nz - 1), 16,
        cost(rows * 768 * nz, rows * 384 * 8 * nz),
    )


def fold_kernel(sets, d, ids, *refs):
    n = sum(len(g) for g in sets) if sets else 2
    srcs, outs = refs[:n], refs[n:]
    if sets:
        groups, at = [], 0
        for g in sets:
            groups.append(srcs[at : at + len(g)])
            at += len(g)
    else:
        groups = [[ref.at[g] for ref in srcs] for g in range(srcs[0].shape[0])]
    half = groups[0][0].shape[1] // 2
    bit = lax.rem(lax.div(ids[1], d), 2) if d else 0
    for g, parts in enumerate(groups):
        spots = ((outs[0], bit), (outs[1], 1 - bit)) if d else ((outs[g], None),)
        for out, where in spots:
            rows = slice(None) if where is None else pl.ds(pl.multiple_of(where * half, half), half)
            total = parts[0][:, rows, :].astype(F32)
            for part in parts[1:]:
                total = total + part[:, rows, :].astype(F32)
            if d:
                out[g] = total.astype(out.dtype)
            else:
                out[...] = total


def fold_z(d, ids, deps, sets):
    stacked = not isinstance(sets[0], (list, tuple))
    args = list(sets) if stacked else [v for g in sets for v in g]
    count = sets[0].shape[0] if stacked else len(sets)
    _, rows, _ = args[0].shape[-3:]
    if d:
        shape = (count, 3, rows // 2, BLK)
        out_shape = [sds(shape, F32), sds(shape, BF)]
    else:
        out_shape = [sds((3, rows, BLK), F32)] * count
    return call_flat(
        functools.partial(fold_kernel, None if stacked else [tuple(g) for g in sets], d), "fold_z",
        ids, deps, args, [NEAR] * len(args), out_shape, 8,
        cost(rows * 768 * count, rows * 384 * 10 * count),
    )


DIMS = (((1,), (1,)), ((), ()))
TILE_N = 512


def unit_kernel(k, ids, *refs):
    first, second, ws = refs[0:4], refs[4:8], refs[8:12]
    far_out, out, lhs, e0, wbuf, sems, wsems, osems = refs[13 if k == 0 else 12 :]
    c = ids[2]
    rows = out.shape[0]
    tiles = ws[0].shape[0] // TILE_N

    def fetch(m):
        slot, lane, copies = m % 2, 0, []
        for n, w in enumerate(ws):
            cols = w.shape[1]
            dst = wbuf.at[slot, :, lane : lane + cols]
            src = w.at[m * TILE_N : (m + 1) * TILE_N, :]
            copies.append(pltpu.make_async_copy(src, dst, wsems.at[slot, n]))
            lane += cols
        return copies

    copies = [(first[3].at[:, k], e0)]
    for mp in range(2):
        for g, ref in enumerate(first[:3]):
            dst = mp * 768 + g * 256
            src = ref.at[:, k, :, mp * 256 : (mp + 1) * 256]
            copies.append((src, lhs.at[:, :, dst : dst + 256]))
    copies = [pltpu.make_async_copy(a, b, sems.at[n]) for n, (a, b) in enumerate(copies)]
    for copy in copies + fetch(0):
        copy.start()
    for mp in range(2):
        for g, ref in enumerate(second[:3]):
            dst = 1536 + mp * 768 + g * 256
            lhs[:, :, dst : dst + 256] = ref[:, k, :, mp * 256 : (mp + 1) * 256]
    for copy in copies:
        copy.wait()
    moved = []
    for m in range(tiles):
        if m + 1 < tiles:
            for copy in fetch(m + 1):
                copy.start()
        for copy in fetch(m):
            copy.wait()
        lo = m * TILE_N
        left = lhs[...].reshape(rows, 3072)
        acc = lax.dot_general(left, wbuf[m % 2], DIMS, preferred_element_type=F32)
        out[:, lo : lo + TILE_N] = acc.astype(out.dtype)
        cols = slice(m * BLK, (m + 1) * BLK)
        for a, val in enumerate((e0[:, :, cols], second[3][:, k, :, cols])):
            lane = pl.ds(pl.multiple_of(lo + a * BLK + c * 256, BLK), BLK)
            total = out[:, lane].astype(F32) + val.reshape(rows, BLK).astype(F32)
            out[:, lane] = total.astype(out.dtype)
        slot = 1 - c if k else c
        done = pltpu.make_async_copy(
            out.at[:, lo : lo + TILE_N], far_out.at[slot, :, lo : lo + TILE_N], osems.at[m]
        )
        done.start()
        moved.append(done)
    for done in moved:
        done.wait()


def unit_grads(k, ids, deps, first, second, ws, held):
    tiles = first[0].shape[0]
    rows, width = tiles * 128, ws[0].shape[0]
    args = [*far_in(*first), *near_in(*second), *far_in(*ws)]
    return call_flat(
        functools.partial(unit_kernel, k), f"unit_grads_{k}", ids, deps, args + far_in(*held),
        [ANY] * 4 + [NEAR] * 4 + [ANY] * (4 + len(held)),
        far((2, rows, width), BF), 24, cost(2 * rows * width * 3072, width * 3072 * 2),
        scratch=[
            pltpu.VMEM((rows, width), BF),
            pltpu.VMEM((tiles, 128, 3072), BF),
            pltpu.VMEM((tiles, 128, 512), BF),
            pltpu.VMEM((2, TILE_N, 3072), BF),
            pltpu.SemaphoreType.DMA((7,)),
            pltpu.SemaphoreType.DMA((2, 4)),
            pltpu.SemaphoreType.DMA((width // TILE_N,)),
        ],
        out_specs=ANY, aliases={len(args): 0} if held else {},
    )


def norm_grad_kernel(ids, du2, tok, cot, lim, scl, gain, *rest):
    accb, accc = rest[:2], rest[2:4]
    out, sums, ga, ba, scr = rest[4:]
    c = ids[2]
    ga[...] = jnp.zeros_like(ga)
    ba[...] = jnp.zeros_like(ba)

    def tile(dur, tokr, cotr, outr):
        i = pl.program_id(0)
        for j in range(scr.shape[0]):
            lanes = slice(j * BLK, (j + 1) * BLK)
            scr[j] = dur[0, :, lanes].astype(F32) + dur[1, :, lanes].astype(F32)
        step = lax.broadcasted_iota(jnp.int32, (STEPS, 1), 0) + i * STEPS
        gsum = jnp.zeros(ga.shape, F32)
        bsum = jnp.zeros(ba.shape, F32)
        for st in range(8):
            sq, h = divmod(st, PARTS)
            x16 = tokr[sq, h].astype(F32)
            c16 = cotr[sq, h].astype(F32)
            for part in range(2):
                cut = slice(part * 8, part * 8 + 8)
                du = jnp.concatenate(
                    [scr[j, pl.ds(st + part * 64, 8, stride=8), :] for j in range(scr.shape[0])],
                    axis=1,
                )
                normed, rstd = norm_of(x16[cut])
                dn = du * gain[...]
                m1 = jnp.mean(dn, axis=-1, keepdims=True)
                m2 = jnp.mean(dn * normed, axis=-1, keepdims=True)
                gy = jnp.where(step[cut] < lim[st], c16[cut] * scl[0], 0.0)
                outr[sq, h, cut, :] = rstd * (dn - m1 - normed * m2) + gy
                gsum = gsum + du * normed
                bsum = bsum + du
        ga[...] += gsum
        ba[...] += bsum

    seqs, parts, steps, width = tok.shape
    nat = pl.BlockSpec((seqs, parts, STEPS, width), lambda i: (0, 0, i, 0))
    pltpu.emit_pipeline(
        tile,
        grid=(steps // STEPS,),
        in_specs=[pl.BlockSpec((2, 128, width), lambda i: (0, i, 0)), nat, nat],
        out_specs=[nat],
    )(du2, tok, cot, out)
    sums[...] = jnp.zeros_like(sums)
    sums[4:5, :] = jnp.sum(ga[...], axis=0, keepdims=True)
    sums[5:6, :] = jnp.sum(ba[...], axis=0, keepdims=True)
    for s in range(4):
        a, mp = divmod(s, 2)
        rows = (
            accc[a][mp, 0:8, :],
            accb[a][mp, 0:8, :],
            accc[a][mp, 8:16, :],
            accb[a][mp, 8:16, :],
        )
        for j, val in enumerate(rows):
            val = jnp.sum(val, axis=0, keepdims=True)
            for mm in range(2):
                lane = pl.ds(core_lane(a, 2 * mp + mm, c), BLK)
                sums[j : j + 1, lane] = val[:, mm * BLK : (mm + 1) * BLK]


def norm_grads(ids, deps, du2, tok, cot, lim8, scale, gain, accb, accc):
    _, rows, width = du2.shape
    n = rows * width
    return call_flat(
        norm_grad_kernel, "norm_grads", ids, deps,
        [*far_in(du2, tok, cot), lim8, scale, gain, *accb, *accc],
        [ANY] * 3 + [SMEM] * 2 + [NEAR] * 5,
        [far(tok.shape, F32), sds((8, width), F32)], 14, cost(n * 20, n * 8),
        scratch=[
            pltpu.VMEM((8, width), F32),
            pltpu.VMEM((8, width), F32),
            pltpu.VMEM((width // BLK, 128, BLK), F32),
        ],
        out_specs=[ANY, NEAR],
    )


def activation_kernel(ids, tok, hown, hrcv, out, scr):
    c = ids[2]
    for s in range(4):
        a, mp = divmod(s, 2)
        for mm in range(2):
            for n, (ref, core) in enumerate(((hown, c), (hrcv, 1 - c))):
                scr[n] = ref[s, mm].astype(F32)
                lane = pl.ds(core_lane(a, 2 * mp + mm, core), BLK)
                for st in range(8):
                    sq, h = divmod(st, PARTS)
                    val = scr[n, pl.ds(st, STEPS, stride=8), :]
                    out[sq, h, :, lane] = tok[sq, h, :, lane].astype(F32) + val


def activations_of(ids, deps, tok, hown, hrcv):
    seqs, parts, steps, width = tok.shape
    tiles = steps // STEPS
    nat = pl.BlockSpec((seqs, parts, STEPS, width), lambda i, ids: (0, 0, i, 0))
    hspec = pl.BlockSpec((4, 2, 128, BLK), lambda i, ids: (0, 0, i, 0))
    n = seqs * parts * steps * width
    return call(
        activation_kernel, "activations_of", (tiles,), ids, deps, far_in(tok, hown, hrcv),
        [nat, hspec, hspec], nat, far(tok.shape, F32), 16, cost(n, n * 8),
        scratch=[pltpu.VMEM((2, 128, BLK), F32)],
    )


def assemble_kernel(counts, ids, *refs):
    out = refs[-1]
    c = ids[2]
    start = 0
    for b, n in enumerate(counts):
        group = refs[start : start + n]
        start += n
        a, core = b % 2, c if b < 2 else 1 - c
        for j in range(3):
            total = group[0][j]
            for ref in group[1:]:
                total = total + ref[j].astype(F32)
            lane = pl.multiple_of(j * 512 + a * BLK + core * 256, BLK)
            out[:, pl.ds(lane, BLK)] = total


def assemble(ids, deps, groups):
    rows = groups[0][0].shape[1]
    counts = [len(g) for g in groups]
    args = [ref for group in groups for ref in group]
    return call_flat(
        functools.partial(assemble_kernel, counts), "assemble", ids, deps, args,
        [NEAR] * len(args), sds((rows, 1536), F32), 16, cost(0, rows * 1536 * 8),
    )


def local(
    nseq,
    ndp,
    tokens,
    cotangent,
    weight,
    forget_peep,
    reset_peep,
    forget_bias,
    reset_bias,
    norm_gain,
    norm_bias,
    lengths,
):
    axes = ("seq", "dp")
    nz = ndp // 2
    seqs, span, width = tokens.shape
    sub = span // PARTS
    q = lax.axis_index("seq").astype(jnp.int32)
    dp = lax.axis_index("dp").astype(jnp.int32)
    z, c = dp // 2, dp % 2
    ids = jnp.stack([q, z, c])

    def table(move):
        pairs = []
        for qq in range(nseq):
            for zz in range(nz):
                for cc in range(2):
                    to = move(qq, zz, cc)
                    if to is not None:
                        pairs.append((qq * ndp + zz * 2 + cc, to[0] * ndp + to[1] * 2 + to[2]))
        return pairs

    def send(value, move):
        return lax.ppermute(value, axes, table(move))

    def to_core(qq, zz, cc):
        return (qq, zz, 1 - cc)

    def to_x(qq, zz, cc):
        return (qq ^ 1, zz, cc)

    def to_y(qq, zz, cc):
        return (qq ^ 2, zz, cc)

    def shift_z(k):
        return lambda qq, zz, cc: (qq, (zz + k) % nz, cc)

    def shift_zc(k):
        return lambda qq, zz, cc: (qq, (zz + k) % nz, 1 - cc)

    def shift_q(k):
        return lambda qq, zz, cc: (qq + k, zz, cc) if 0 <= qq + k < nseq else None

    mine, theirs = split_weight(ids, weight)
    recv = send(theirs, to_core)
    nat = (seqs, PARTS, sub, width)
    tok4 = tokens.reshape(nat)
    cot4 = cotangent.reshape(nat)
    tok_oth = send(tokens, to_core).reshape(nat)
    len_oth = send(lengths, to_core)

    lens = jnp.stack([lengths, len_oth])
    counts = jnp.sum(lens, axis=1).astype(F32)
    scale = (seqs * span * nseq) / counts
    lim16 = (
        lens[:, :, None] - q * span - sub * jnp.arange(PARTS, dtype=jnp.int32)[None, None, :]
    ).reshape(2, 8)
    spread_rows = lambda v: jnp.broadcast_to(v, (2, STEPS, 8, BLK)).reshape(256, BLK)
    step_in_tile = jnp.arange(STEPS, dtype=jnp.int32)[None, :, None, None]
    lim = spread_rows(lim16[:, None, :, None] - step_in_tile)
    scl = spread_rows(scale[:, None, None, None])

    lim8, scale1 = lim16[0], scale[:1]

    def by_core(vec):
        v = lax.dynamic_slice_in_dim(vec.reshape(4, 4, BLK), 2 * c, 2, 1)
        return v.transpose(1, 0, 2).reshape(1, width // 2)

    vf, vr, bfor, brst = (by_core(v) for v in (forget_peep, reset_peep, forget_bias, reset_bias))
    gain, bias = norm_gain.reshape(1, width), norm_bias.reshape(1, width)

    tail = [mine]

    def run(kernel, *head, rest=(), token=-1, after=(), big=False):
        out = kernel(*head, ids, (tail[0], *after), *rest)
        tail[0] = out[token] if isinstance(out, (list, tuple)) else out
        if big:
            (tail[0],) = far_in(tail[0])
        return out

    groups = [[cc + 2 * zz for zz in range(nz)] for cc in range(2)]

    def along_z(piece):
        if nz <= 4:
            return [send(piece, shift_z(-k)) for k in range(1, nz)]
        got = lax.all_gather(piece, "dp", axis=0, tiled=True, axis_index_groups=groups)
        n = got.shape[0] // nz
        twice = jnp.concatenate([got, got], axis=0)
        return [lax.dynamic_slice_in_dim(twice, (z + 1) * n, n * (nz - 1), 0)]

    def gather_1(s, zs, after=()):
        rel = run(plane_pieces, s, rest=(zs,), after=after)
        return rel, send(rel, to_x), send(rel, to_y)

    def gather_2(s, got, after=()):
        rel, gx, gy = got
        tox, toy = run(cross_pieces, s, rest=(gx, gy), after=after)
        return rel, gx, gy, send(tox, to_x), send(toy, to_y)

    def spread(both):
        return lax.all_gather(both, "seq")

    def run_project(s, weights, before=None, after=()):
        rest = (ub, ulo, weights, lim, vf, bfor, before)
        return run(project, s, nz, rest=rest, token=4, after=after)

    def run_states(a, fwd, got, held, after=()):
        rest = (fwd, ub, ulo, cot4, cot_oth, lim, scl, vr, brst, got, held)
        out = run(states, a, nseq, rest=rest, after=after)
        return {
            "h": out[:2], "mid": (out[2:5], out[5:8]), "dzr": out[8], "u": out[9],
            "lbs": out[10], "summ": out[11], "acc": out[12],
        }

    def run_adjoints(a, fwd, m, got, after=()):
        rest = (fwd, m["mid"], m["dzr"], m["u"], vf, vr, m["lbs"], got)
        du, dzc, dzf, acc = run(adjoints, a, nseq, rest=rest, after=after)
        return {"du": du, "dz": (dzc, dzf, m["dzr"]), "acc": acc}

    def sum_1(which, dz, keep=(), after=(), hold=False):
        own, xp, yp, da, db, *kept = run(
            weight_grad_part, which, nz, rest=(ubt, dz, keep), token=3, after=after
        )
        if hold:
            da, db = run(gate, rest=((da, db),))
        return (own, xp, yp, send(da, to_x), send(db, to_y)), kept

    def sum_2(got, after=()):
        own, xp, yp, ra, rb = got
        s1, s2 = run(relay_sums, rest=(xp, yp, ra, rb), after=after)
        return own, send(s1, to_x), send(s2, to_y)

    def fold(sets, d):
        kept, out = run(fold_z, d, rest=(sets,))
        return kept, send(out, lambda qq, zz, cc: (qq, zz ^ d, cc))

    def sum_3_now(got):
        if nz > 4:
            got, d = [got], nz // 2
            while d:
                got, d = fold(got, d), d // 2
            return run(fold_z, 0, rest=(got,))
        parts = list(run(plane_sums, nz, rest=got))
        return parts[:1] + [send(parts[k], shift_z(k)) for k in range(1, nz)]

    def fold_rest(got):
        d = nz // 4
        while d:
            got, d = fold(got, d), d // 2
        return got

    high, p0, p1 = run(quarter_of, rest=(mine, recv), after=(tok_oth, len_oth))
    z0 = along_z(p0)
    cot_cols = run(other_columns, rest=(cotangent,), big=True)
    cot_oth = send(cot_cols, to_core).reshape(seqs, PARTS, sub, width // 2)
    z1 = along_z(p1)
    ub, ubt, ulo = run(
        norm_tokens, rest=(tok4, tok_oth, gain, bias), big=True, after=(lim8, scale1, lim, scl, cot_oth)
    )
    g0 = gather_1(0, z0)
    g0 = gather_2(0, g0)
    g1 = gather_1(1, z1)
    z23 = along_z(run(hand_on, rest=(high,)))
    f0 = run_project(0, (mine, recv, *g0))
    g1 = gather_2(1, g1)
    f1 = run_project(1, (mine, recv, *g1), f0[4])
    got = spread(f1[4])
    g2 = gather_1(2, z23, after=(got,))
    m0 = run_states(0, (f0, f1), got, ())
    got = spread(m0["summ"])
    g2 = gather_2(2, g2, after=(got,))
    d0 = run_adjoints(0, (f0, f1), m0, got)
    s0, _ = sum_1("other", d0["dz"])
    g3 = gather_1(3, z23, after=g2[3:])
    f2 = run_project(2, (mine, recv, *g2))
    g3 = gather_2(3, g3)
    s0 = sum_2(s0)
    s1, first = sum_1("own", d0["dz"], (d0["du"],))
    f3 = run_project(3, (mine, recv, *g3), f2[4])
    got = spread(f3[4])
    s1 = sum_2(s1, after=(got,))
    m1 = run_states(1, (f2, f3), got, m0["h"], after=s0[1:])
    s01 = fold([s0, s1], nz // 2)
    hrcv = send(run(gate, rest=(m1["h"][1:], "far"))[0], to_core)
    got = spread(run(hand_on, rest=(m1["summ"],)))
    d1 = run_adjoints(1, (f2, f3), m1, got)
    s2, _ = sum_1("other", d1["dz"])
    s3, _ = sum_1("own", d1["dz"], after=(hrcv,))
    s2 = sum_2(s2)
    s01 = fold_rest(s01)
    second = (*d1["dz"], d1["du"])
    ws = (f0[5], f1[5], f2[5], f3[5])
    du2 = run(unit_grads, 1, rest=(first, second, ws, ()), big=True)
    s3 = sum_2(s3)
    du2 = run(unit_grads, 0, rest=(first, second, ws, (du2,)), big=True)
    s2 = fold([s2], nz // 2)
    s0, s1 = run(fold_z, 0, rest=(s01,))
    s0 = send(s0, to_core)
    s3 = sum_3_now(s3)
    cores = [[2 * zz, 2 * zz + 1] for zz in range(nz)]
    du2 = lax.all_to_all(du2, "dp", 0, 0, axis_index_groups=cores, tiled=True)
    activations = run(activations_of, rest=(tok4, m1["h"][0], hrcv), big=True)
    input_grad, sums = run(
        norm_grads,
        rest=(
            du2, tok4, cot4, lim8, scale1, gain, (m0["acc"], m1["acc"]), (d0["acc"], d1["acc"])
        ),
        after=(s0,),
    )
    s2 = fold_rest(s2)
    s3 = run(fold_z, 0, rest=([s3],))
    if nz <= 4:
        sums = run(add_up, rest=(sums, *[send(sums, shift_z(k)) for k in range(1, nz)]))
    else:
        for b in range((nz - 1).bit_length()):
            hop = lambda qq, zz, cc, b=1 << b: (qq, zz ^ b, cc)
            sums = run(add_up, rest=(sums, send(sums, hop)))
    s2 = send(run(fold_z, 0, rest=(s2,))[0], to_core)
    moved = [send(sums, lambda qq, zz, cc, b=b: (qq ^ b, zz, cc)) for b in range(1, nseq)]
    sums = run(add_up, rest=(sums, *moved))
    moved = send(sums, to_core)
    sums = run(add_up, rest=(sums, moved))
    weight_grad = run(assemble, rest=(([s1], s3, [s0], [s2]),))
    shape = tokens.shape
    return (
        activations.reshape(shape),
        input_grad.reshape(shape),
        weight_grad,
        sums[0],
        sums[1],
        sums[2],
        sums[3],
        sums[4],
        sums[5],
    )


def solution(mesh):
    whole = P("dp", "seq", None)
    in_specs = (whole, whole, P("dp", None)) + (P(),) * 6 + (P("dp"),)
    out_specs = (whole, whole, P("dp", "seq")) + (P(),) * 6
    step = functools.partial(local, mesh.shape["seq"], mesh.shape["dp"])
    return jax.shard_map(step, mesh=mesh, in_specs=in_specs, out_specs=out_specs, check_vma=False)
```

```python
import functools

import jax
import jax.numpy as jnp
from jax import lax
from jax.experimental import pallas as pl
from jax.experimental.pallas import tpu as pltpu
from jax.sharding import PartitionSpec as P

EPS = 1e-05
F32 = jnp.float32
BF = jnp.bfloat16
STEPS = 16
BLK = 128
GATES = 3
QUARTERS = 4
PARTS = 4


def params(mib, dims=1):
    return pltpu.CompilerParams(
        vmem_limit_bytes=mib * 1024 * 1024, dimension_semantics=("arbitrary",) * dims
    )


def cost(flops, bytes_accessed, transcendentals=0):
    return pl.CostEstimate(
        flops=int(flops), bytes_accessed=int(bytes_accessed), transcendentals=int(transcendentals)
    )


def sds(shape, dtype):
    return jax.ShapeDtypeStruct(shape, dtype)


def far(shape, dtype):
    return pltpu.HBM(shape, dtype)


def near(shape, dtype):
    return pltpu.VMEM(shape, dtype)


def far_in(*values):
    return [pltpu.with_memory_space_constraint(v, pltpu.HBM) for v in values]


def near_in(*values):
    return [pltpu.with_memory_space_constraint(v, pltpu.VMEM) for v in values]


ANY = pl.BlockSpec(memory_space=pl.ANY)
NEAR = pl.BlockSpec(memory_space=pltpu.VMEM)
SMEM = pl.BlockSpec(memory_space=pltpu.SMEM)


def ordered(kernel, deps):
    n = len(deps)

    def body(ids, *refs):
        return kernel(ids, *refs[n:])

    return body, list(deps), [ANY] * n


def call(kernel, name, grid, ids, deps, args, in_specs, out_specs, out_shape, mib, est, scratch=()):
    body, deps, dep_specs = ordered(kernel, deps)
    return pl.pallas_call(
        body,
        grid_spec=pltpu.PrefetchScalarGridSpec(
            num_scalar_prefetch=1,
            grid=grid,
            in_specs=dep_specs + in_specs,
            out_specs=out_specs,
            scratch_shapes=list(scratch),
        ),
        out_shape=out_shape,
        compiler_params=params(mib, len(grid)),
        cost_estimate=est,
        name=name,
    )(ids, *deps, *args)


def call_flat(kernel, name, ids, deps, args, in_specs, out_shape, mib, est, scratch=(), out_specs=None, aliases=None):
    body, deps, dep_specs = ordered(kernel, deps)
    many = isinstance(out_shape, (list, tuple))
    if out_specs is None:
        out_specs = [NEAR] * len(out_shape) if many else NEAR
    shift = 1 + len(deps)
    return pl.pallas_call(
        body,
        in_specs=[SMEM] + dep_specs + in_specs,
        out_specs=out_specs,
        out_shape=out_shape,
        scratch_shapes=list(scratch),
        input_output_aliases={k + shift: v for k, v in (aliases or {}).items()},
        compiler_params=pltpu.CompilerParams(vmem_limit_bytes=mib * 1024 * 1024),
        cost_estimate=est,
        name=name,
    )(ids, *deps, *args)


def split_kernel(ids, w, mine, theirs):
    c = ids[2]
    for s in range(4):
        a, mp = divmod(s, 2)
        for g in range(GATES):
            for mm in range(2):
                dst = s * 768 + g * 256 + mm * BLK
                base = g * 2048 + (2 * mp + mm) * 512 + a * BLK
                here = pl.multiple_of(base + c * 256, BLK)
                there = pl.multiple_of(base + (1 - c) * 256, BLK)
                mine[:, dst : dst + BLK] = w[:, pl.ds(here, BLK)]
                theirs[:, dst : dst + BLK] = w[:, pl.ds(there, BLK)]


def split_weight(ids, weight):
    rows, cols = weight.shape
    tile = rows // 2
    spec = pl.BlockSpec((tile, cols // 2), lambda i, ids: (i, 0))
    return call(
        split_kernel, "split_weight", (2,), ids, (), far_in(weight),
        [pl.BlockSpec((tile, cols), lambda i, ids: (i, 0))], [spec, spec],
        [sds((rows, cols // 2), BF)] * 2, 16, cost(0, rows * cols * 4),
    )


def quarter_kernel(ids, mine, recv, high, p0, p1):
    q, c = ids[0], ids[2]
    half = high.shape[0]
    at = pl.ds(pl.multiple_of(lax.rem(q, 2) * half, half), half)
    first = (lax.div(q, 2) == c).astype(jnp.int32) == 1
    val = jnp.where(first, mine[at, :], recv[at, :])
    high[...] = val[:, 1536:]
    p0[...] = val[:, :768]
    p1[...] = val[:, 768:1536]


def quarter_of(ids, deps, mine, recv):
    rows, cols = mine.shape
    half = rows // 2
    return call_flat(
        quarter_kernel, "quarter_of", ids, deps, [mine, recv], [NEAR, NEAR],
        [sds((half, 1536), BF), sds((half, 768), BF), sds((half, 768), BF)], 8,
        cost(0, rows * cols * 4),
    )


def columns_kernel(ids, src, dst):
    there = 1 - ids[2]
    for m in range(QUARTERS):
        lane = pl.ds(pl.multiple_of(m * 512 + there * 256, BLK), 256)
        dst[:, :, m * 256 : (m + 1) * 256] = src[:, :, lane]


def other_columns(ids, deps, value):
    seqs, span, width = value.shape
    step = span // 4
    return call(
        columns_kernel, "other_columns", (4,), ids, deps, far_in(value),
        [pl.BlockSpec((seqs, step, width), lambda i, ids: (0, i, 0))],
        pl.BlockSpec((seqs, step, width // 2), lambda i, ids: (0, i, 0)),
        far((seqs, span, width // 2), value.dtype), 12, cost(0, value.size * 3),
    )


def copy_kernel(ids, src, dst):
    dst[...] = src[...]


def hand_on(ids, deps, value):
    return call_flat(
        copy_kernel, "hand_on", ids, deps, [value], [NEAR], sds(value.shape, value.dtype), 16,
        cost(0, value.size * 4),
    )


def gate_kernel(ids, *refs):
    pass


def gate(ids, deps, values, hold=None):
    shape = {None: sds, "far": far, "near": near}[hold]
    held = {None: lambda *v: list(v), "far": far_in, "near": near_in}[hold]
    return call_flat(
        gate_kernel, "gate", ids, deps, held(*values), [ANY] * len(values),
        [shape(v.shape, v.dtype) for v in values], 4, cost(0, 1), out_specs=[ANY] * len(values),
        aliases={n: n for n in range(len(values))},
    )


def add_kernel(ids, *refs):
    total = refs[0][...]
    for ref in refs[1:-1]:
        total = total + ref[...]
    refs[-1][...] = total


def add_up(ids, deps, *values):
    a = values[0]
    return call_flat(
        add_kernel, "add_up", ids, deps, list(values), [NEAR] * len(values), sds(a.shape, a.dtype),
        4, cost(a.size, a.size * 4 * len(values)),
    )


def plane_kernel(s, ids, *refs):
    rel = refs[-1]
    row = 0
    for ref in refs[:-1]:
        lane = s % 2 * 768 if ref.shape[1] > 768 else 0
        rel[row : row + ref.shape[0], :] = ref[:, lane : lane + 768]
        row += ref.shape[0]


def plane_pieces(s, ids, deps, parts):
    rows = sum(p.shape[0] for p in parts)
    return call_flat(
        functools.partial(plane_kernel, s), f"plane_pieces_{s}", ids, deps, list(parts),
        [NEAR] * len(parts), sds((rows, 768), BF), 8, cost(0, rows * 768 * 4),
    )


def cross_kernel(ids, gx, gy, tox, toy):
    tox[...] = gy[:, :384]
    toy[...] = gx[:, 384:]


def cross_pieces(s, ids, deps, gx, gy):
    rows = gx.shape[0]
    return call_flat(
        cross_kernel, f"cross_pieces_{s}", ids, deps, [gx, gy], [NEAR, NEAR],
        [sds((rows, 384), BF)] * 2, 16, cost(0, rows * 768 * 4),
    )


def norm_of(x):
    mean = jnp.mean(x, axis=-1, keepdims=True)
    centered = x - mean
    var = jnp.mean(centered * centered, axis=-1, keepdims=True)
    rstd = lax.rsqrt(var + EPS)
    return centered * rstd, rstd


def norm_kernel(ids, own, other, gain, bias, ub, ubt, ulo, scr):
    c = ids[2]
    seqs = own.shape[0]
    for k, ref in enumerate((own, other)):
        for st in range(8):
            sq, h = divmod(st, PARTS)
            normed, _ = norm_of(ref[sq, h].astype(F32))
            unit = normed * gain[...] + bias[...]
            for j in range(scr.shape[0]):
                scr[j, pl.ds(k * 128 + st, STEPS, stride=8), :] = unit[:, j * BLK : (j + 1) * BLK]
    for j in range(scr.shape[0]):
        low = scr[j, 0:256, :].astype(BF)
        ub[0, :, :, j * BLK : (j + 1) * BLK] = low.reshape(2, 128, BLK)
        ubt[j * BLK : (j + 1) * BLK, :] = low.T
    for a in range(2):
        for m in range(QUARTERS):
            unit = scr[m * 4 + a + 2 * c, 0:256, :]
            rest = (unit - unit.astype(BF).astype(F32)).astype(BF)
            dst = (a * QUARTERS + m) * BLK
            ulo[0, :, :, dst : dst + BLK] = rest.reshape(2, 128, BLK)


def tile_block(cols):
    return pl.BlockSpec((1, 2, 128, cols), lambda i, ids: (i, 0, 0, 0))


def norm_tokens(ids, deps, own, other, gain, bias):
    seqs, parts, steps, width = own.shape
    rows = seqs * parts * steps
    tiles = steps // STEPS
    nat = pl.BlockSpec((seqs, parts, STEPS, width), lambda i, ids: (0, 0, i, 0))
    vec = pl.BlockSpec((1, width), lambda i, ids: (0, 0))
    return call(
        norm_kernel, "norm_tokens", (tiles,), ids, deps, [*far_in(own, other), gain, bias],
        [nat, nat, vec, vec],
        [
            tile_block(width),
            pl.BlockSpec((width, 256), lambda i, ids: (0, i)),
            tile_block(width // 2),
        ],
        [
            far((tiles, 2, 128, width), BF),
            far((width, 2 * rows), BF),
            far((tiles, 2, 128, width // 2), BF),
        ],
        20, cost(rows * width * 20, rows * width * 14),
        scratch=[pltpu.VMEM((width // BLK, 264, BLK), F32)],
    )


def flat(ref):
    value = ref[...]
    return value.reshape(256, value.shape[-1])


def core_lane(a, m, c):
    return pl.multiple_of(m * 512 + a * BLK + c * 256, BLK)


def pairs():
    for tp in range(STEPS // 2):
        for k in range(2):
            yield k, tp * 16, k * 128 + tp * 16


def live_pair(lim, row, tile):
    live = lim[row : row + 16, :] > tile * STEPS
    return jnp.concatenate([live, live], axis=1)


def fold_streams(pr, lc, ahead):
    out = []
    order = range(PARTS) if ahead else range(PARTS - 1, -1, -1)
    for sq in range(2):
        tp = tl = None
        for h in order:
            n = sq * PARTS + h
            p, l = pr[n : n + 1], lc[n : n + 1]
            tp, tl = (p, l) if tp is None else ((p * tp, p * tl + l) if ahead else (p * tp, l + p * tl))
        out.append((tp, tl))
    return out


def proj_kernel(s, nz, joined, ids, ub, ulo, *rest):
    n_w = 1 if joined else 7
    weights, rest = rest[:n_w], rest[n_w:]
    lim, vf, bfor = rest[:3]
    rest = rest[3:]
    before = rest[0] if s % 2 else None
    cand_far, decay, rpre_far, plout, summ = rest[s % 2 : s % 2 + 5]
    rest = rest[s % 2 + 5 :]
    if joined:
        zbuf, prod, loc, wbuf, sems = rest
    else:
        wall, zbuf, prod, loc, wbuf, sems = rest
    tiles = decay.shape[0]
    width = wbuf.shape[0]
    q, z, c = ids[0], ids[1], ids[2]
    a, mp = divmod(s, 2)
    cols = slice(mp * 768, mp * 768 + 768)
    copies = []

    def put(src, row, rows, lo=0, hi=768):
        dst = wbuf.at[pl.ds(row, rows), lo:hi]
        copy = pltpu.make_async_copy(src, dst, sems.at[len(copies)])
        copy.start()
        copies.append(copy)

    if joined:
        put(weights[0].at[:, cols], 0, width)
    else:
        mine, recv, rel, gx, gy, dx, dy = weights
        zb = width // nz
        zb2, qb = zb // 2, zb // 4
        mult = lambda v: pl.multiple_of(v, qb)
        put(mine.at[:, s * 768 : (s + 1) * 768], mult(z * zb + c * zb2), zb2)
        put(recv.at[:, s * 768 : (s + 1) * 768], mult(z * zb + (1 - c) * zb2), zb2)
        for r in range(1, nz):
            base = lax.rem(z + r, nz) * zb
            lo, hi = (r - 1) * qb, r * qb
            put(rel.at[lo:hi, :], mult(base + q * qb), qb)
            put(gx.at[lo:hi, :], mult(base + (q ^ 1) * qb), qb)
            put(gy.at[lo:hi, :], mult(base + (q ^ 2) * qb), qb)
            put(dx.at[lo:hi, :], mult(base + (q ^ 3) * qb), qb, 0, 384)
            put(dy.at[lo:hi, :], mult(base + (q ^ 3) * qb), qb, 384, 768)
    for copy in copies:
        copy.wait()
    if not joined:
        keep = pltpu.make_async_copy(wbuf, wall, sems.at[len(copies)])
        keep.start()
    prod[...] = jnp.ones_like(prod)
    loc[...] = jnp.zeros_like(loc)

    def tile(ubr, ulor, cand, rpre):
        i = pl.program_id(0)
        zbuf[:, :768] = jnp.dot(flat(ubr), wbuf[...], preferred_element_type=F32)
        low = flat(ulor).astype(F32)
        for mm in range(2):
            high = ubr[:, :, :, pl.ds(core_lane(a, 2 * mp + mm, c), BLK)].reshape(256, BLK)
            zbuf[:, 768 + mm * BLK : 768 + (mm + 1) * BLK] = (
                high.astype(F32) + low[:, mm * BLK : (mm + 1) * BLK]
            )
        pr = [prod[0:8, :], prod[8:16, :]]
        lc = [loc[0:8, :], loc[8:16, :]]
        for k, r0, row in pairs():
            cd = zbuf[row : row + 16, :256]
            logit = zbuf[row : row + 16, 256:512] + vf[...] * zbuf[row : row + 16, 768:] + bfor[...]
            dec = jnp.where(live_pair(lim, row, i), jax.nn.sigmoid(logit), 1.0)
            inj = (1.0 - dec) * cd
            cand[0, k, r0 : r0 + 16, :] = cd
            decay[i, k, r0 : r0 + 16, :] = dec
            rpre[0, k, r0 : r0 + 16, :] = zbuf[row : row + 16, 512:768]
            for t in range(2):
                d = dec[t * 8 : t * 8 + 8]
                lc[k] = d * lc[k] + inj[t * 8 : t * 8 + 8]
                pr[k] = d * pr[k]
        for k in range(2):
            prod[k * 8 : k * 8 + 8, :] = pr[k]
            loc[k * 8 : k * 8 + 8, :] = lc[k]

    pltpu.emit_pipeline(
        tile,
        grid=(tiles,),
        in_specs=[
            pl.BlockSpec((1, 2, 128, width), lambda i: (i, 0, 0, 0)),
            pl.BlockSpec((1, 2, 128, 256), lambda i: (i, 0, 0, s)),
        ],
        out_specs=[pl.BlockSpec((1, 2, 128, 256), lambda i: (i, 0, 0, 0))] * 2,
    )(ub, ulo, cand_far, rpre_far)
    if s % 2:
        summ[0] = before[0]
    plout[0:16, :] = prod[...]
    plout[16:32, :] = loc[...]
    for k in range(2):
        pr, lc = prod[k * 8 : k * 8 + 8, :], loc[k * 8 : k * 8 + 8, :]
        for sq, (tp, tl) in enumerate(fold_streams(pr, lc, True)):
            ks = k * 2 + sq
            summ[s % 2, ks : ks + 1, :] = tp
            summ[s % 2, 4 + ks : 5 + ks, :] = tl
    if not joined:
        keep.wait()


def project(s, nz, ids, deps, ub, ulo, weights, lim, vf, bfor, before):
    tiles, _, _, width = ub.shape
    joined = len(weights) == 1
    shape = (tiles, 2, 128, 256)
    rows = tiles * 256
    chan = slice(s * 256, s * 256 + 256)
    args = far_in(ub, ulo, *weights) + [lim, vf[:, chan], bfor[:, chan]]
    in_specs = [ANY] * (2 + len(weights)) + [NEAR] * 3
    if s % 2:
        args.append(before)
        in_specs.append(NEAR)
    out_shape = [far(shape, F32), near(shape, F32), far(shape, F32)]
    out_shape += [near((32, 256), F32), near((2, 8, 256), F32)]
    out_specs = [ANY, NEAR, ANY, NEAR, NEAR]
    if not joined:
        out_shape.append(far((width, 768), BF))
        out_specs.append(ANY)
    return call_flat(
        functools.partial(proj_kernel, s, nz, joined), f"project_{s}", ids, deps, args, in_specs,
        out_shape, 12, cost(2 * rows * width * 768, rows * width * 2 + width * 768 * 4),
        scratch=[
            pltpu.VMEM((256, 1024), F32),
            pltpu.VMEM((16, 256), F32),
            pltpu.VMEM((16, 256), F32),
            pltpu.VMEM((width, 768), BF),
            pltpu.SemaphoreType.DMA((3 + 5 * (nz - 1),)),
        ],
        out_specs=out_specs,
    )


def halves(v):
    return v[:8], v[8:]


def enter(got, n, ahead, q, count):
    value = jnp.zeros((4, 256), F32)
    for j in range(count) if ahead else range(count - 1, -1, -1):
        used = (j < q) if ahead else (j > q)
        longer = got[j, n, 4:8, :] + got[j, n, 0:4, :] * value
        value = jnp.where(used, longer, value)
    return value


def state_kernel(a, count, held, ids, *refs):
    fwd = (refs[0:4], refs[4:8])
    ub, ulo, cot_own, cot_oth, lim, scl, vr, br, got = refs[8:17]
    rest = refs[17 + (2 if held else 0) :]
    hown, hoth = rest[:2]
    out = (rest[2:5], rest[5:8])
    dzr, uu, lbs, summ, acc, st, pp, lb, ac, scr = rest[8:]
    tiles = dzr.shape[0]
    q, c = ids[0], ids[2]
    for n in range(2):
        cand_far, decay, rpre_far, plin = fwd[n]
        bc, dstate, du0 = out[n]
        lanes = slice(n * 256, n * 256 + 256)
        carry = enter(got, n, True, q, count)
        for ks in range(4):
            cc = carry[ks : ks + 1]
            for h in range(PARTS):
                m = ks * PARTS + h
                st[m : m + 1, :] = cc
                cc = plin[m : m + 1, :] * cc + plin[16 + m : 17 + m, :]
        pp[...] = jnp.ones_like(pp)
        lb[...] = jnp.zeros_like(lb)
        ac[...] = jnp.zeros_like(ac)

        def tile(cand, rpre, u0, u1, ul, own0, own1, oth0, oth1, ho, ht):
            i = pl.program_id(0)
            for k, pair in enumerate(((own0, own1), (oth0, oth1))):
                for b, ref in enumerate(pair):
                    for m in range(8):
                        sq, h = divmod(m, PARTS)
                        scr[b, pl.ds(k * 128 + m, STEPS, stride=8), :] = ref[sq, h].astype(F32)
            cur = [st[0:8, :], st[8:16, :]]
            p = [pp[0:8, :], pp[8:16, :]]
            l = [lb[0:8, :], lb[8:16, :]]
            peep = [jnp.zeros((8, 256), F32)] * 2
            bias = [jnp.zeros((8, 256), F32)] * 2
            wr, wb = vr[:, lanes], br[:, lanes]
            for k, r0, row in pairs():
                at = slice(r0, r0 + 16)
                dec = decay[i, k, at, :]
                cd = cand[0, k, at, :]
                inj = (1.0 - dec) * cd
                befores, states = [], []
                for d, v in zip(halves(dec), halves(inj)):
                    befores.append(cur[k])
                    cur[k] = d * cur[k] + v
                    states.append(cur[k])
                before = jnp.concatenate(befores, axis=0)
                state = jnp.concatenate(states, axis=0)
                low = jnp.concatenate([u0[0, k, at, :], u1[0, k, at, :]], axis=1)
                uu[i, k, at, lanes] = low
                u = low.astype(F32) + ul[0, k, at, :].astype(F32)
                live = lim[row : row + 16, :] > i * STEPS
                sc = jnp.where(live, scl[row : row + 16, :], 0.0)
                gy = jnp.concatenate(
                    [scr[0, row : row + 16, :] * sc, scr[1, row : row + 16, :] * sc], axis=1
                )
                r = jax.nn.sigmoid(rpre[0, k, at, :] + wr * before + wb)
                gap = state - u
                hv = jnp.where(jnp.concatenate([live, live], axis=1), u + r * gap, 0.0).astype(BF)
                href = ht if k else ho
                href[0, 0, at, :] = hv[:, :BLK]
                href[0, 1, at, :] = hv[:, BLK:]
                ds = gy * r
                drl = ds * (1.0 - r) * gap
                sr = dec * ds + wr * drl
                dstate[i, k, at, :] = ds
                bc[i, k, at, :] = before - cd
                du0[i, k, at, :] = (gy - ds).astype(BF)
                dzr[i, k, at, lanes] = drl.astype(BF)
                for d, v in zip(halves(dec), halves(sr)):
                    l[k] = l[k] + p[k] * v
                    p[k] = p[k] * d
                for e, w in zip(halves(drl), befores):
                    peep[k] = peep[k] + e * w
                    bias[k] = bias[k] + e
            for k in range(2):
                st[k * 8 : k * 8 + 8, :] = cur[k]
                pp[k * 8 : k * 8 + 8, :] = p[k]
                lb[k * 8 : k * 8 + 8, :] = l[k]
            ac[0:8, :] += peep[0] + peep[1]
            ac[8:16, :] += bias[0] + bias[1]

        nat = cot_own.shape[:2]

        def unit(mm):
            return pl.BlockSpec(
                (1, 2, 128, BLK), lambda i: (i, 0, 0, (2 * n + mm) * 4 + 2 * c + a)
            )

        def tail():
            return pl.BlockSpec((1, 2, 128, 256), lambda i: (i, 0, 0, 2 * a + n))

        def nat_own(mm):
            return pl.BlockSpec(
                (*nat, STEPS, BLK), lambda i: (0, 0, i, (2 * n + mm) * 4 + 2 * c + a)
            )

        def nat_oth(mm):
            return pl.BlockSpec((*nat, STEPS, BLK), lambda i: (0, 0, i, (2 * n + mm) * 2 + a))

        one = pl.BlockSpec((1, 2, 128, 256), lambda i: (i, 0, 0, 0))
        hspec = pl.BlockSpec((1, 2, 128, BLK), lambda i: (2 * a + n, 0, i, 0))
        pltpu.emit_pipeline(
            tile,
            grid=(tiles,),
            in_specs=[one, one, unit(0), unit(1), tail(), nat_own(0), nat_own(1), nat_oth(0), nat_oth(1)],
            out_specs=[hspec, hspec],
        )(cand_far, rpre_far, ub, ub, ulo, cot_own, cot_own, cot_oth, cot_oth, hown, hoth)
        acc[n] = ac[...]
        lbs[n] = lb[...]
        for k in range(2):
            p, l = pp[k * 8 : k * 8 + 8, :], lb[k * 8 : k * 8 + 8, :]
            for sq, (tp, tl) in enumerate(fold_streams(p, l, False)):
                ks = k * 2 + sq
                summ[n, ks : ks + 1, :] = tp
                summ[n, 4 + ks : 5 + ks, :] = tl


def states(a, count, ids, deps, fwd, ub, ulo, cot_own, cot_oth, lim, scl, vr, br, got, held):
    tiles = ub.shape[0]
    rows = tiles * 128
    one = (tiles, 2, 128, 256)
    two = (tiles, 2, 128, 512)
    chan = slice(a * 512, a * 512 + 512)
    args, in_specs = [], []
    for f in fwd:
        args += far_in(f[0]) + near_in(f[1]) + far_in(f[2]) + [f[3]]
        in_specs += [ANY, NEAR, ANY, NEAR]
    args += far_in(ub, ulo, cot_own, cot_oth) + [lim, scl, vr[:, chan], br[:, chan], got]
    in_specs += [ANY] * 4 + [NEAR] * 5
    aliases = {}
    if held:
        aliases = {len(args): 0, len(args) + 1: 1}
        args += far_in(*held)
        in_specs += [ANY] * 2
    small = near((2, 16, 256), F32)
    return call_flat(
        functools.partial(state_kernel, a, count, bool(held)), f"states_{a}", ids, deps, args,
        in_specs,
        [far((4, 2, rows, BLK), BF)] * 2
        + [near(one, F32), near(one, F32), near(one, BF)] * 2
        + [near(two, BF)] * 2
        + [small, near((2, 8, 256), F32), small],
        10, cost(rows * 1024 * 60, rows * 1024 * 10, rows * 1024 * 2),
        scratch=[pltpu.VMEM((16, 256), F32)] * 4 + [pltpu.VMEM((2, 264, BLK), F32)],
        out_specs=[ANY] * 2 + [NEAR] * 11,
        aliases=aliases,
    )


def adjoint_kernel(count, ids, *refs):
    ins = (refs[0:5], refs[5:10])
    dzr, uu, vf, vr, lbs, got, du, dzc, dzf, acc, adj = refs[10:]
    tiles = du.shape[0]
    q = ids[0]
    for n in range(2):
        decay, bc, dstate, du0, plin = ins[n]
        lanes = slice(n * 256, n * 256 + 256)
        wf, wr = vf[:, lanes], vr[:, lanes]
        after = enter(got, n, False, q, count)
        for ks in range(4):
            cc = after[ks : ks + 1]
            for h in range(PARTS - 1, -1, -1):
                m = ks * PARTS + h
                adj[m : m + 1, :] = cc
                cc = lbs[n, m : m + 1, :] + plin[m : m + 1, :] * cc

        def tile(step, state):
            i = tiles - 1 - step
            cur, peep, bias = [state[0], state[1]], state[2], state[3]
            for k, r0, _ in reversed(list(pairs())):
                at = slice(r0, r0 + 16)
                dec = decay[i, k, at, :]
                ds = dstate[i, k, at, :]
                sr = dec * ds + wr * dzr[i, k, at, lanes].astype(F32)
                late = ds[8:] + cur[k]
                cur[k] = dec[8:] * cur[k] + sr[8:]
                early = ds[:8] + cur[k]
                cur[k] = dec[:8] * cur[k] + sr[:8]
                dcand = jnp.concatenate([early, late], axis=0) * (1.0 - dec)
                dfl = dcand * bc[i, k, at, :] * dec
                dzc[i, k, at, lanes] = dcand.astype(BF)
                dzf[i, k, at, lanes] = dfl.astype(BF)
                du[i, k, at, lanes] = (du0[i, k, at, :].astype(F32) + dfl * wf).astype(BF)
                w = dfl * uu[i, k, at, lanes].astype(F32)
                peep = peep + (w[:8] + w[8:])
                bias = bias + (dfl[:8] + dfl[8:])
            return cur[0], cur[1], peep, bias

        zero = jnp.zeros((8, 256), F32)
        end = lax.fori_loop(0, tiles, tile, (adj[0:8, :], adj[8:16, :], zero, zero))
        acc[n, 0:8, :] = end[2]
        acc[n, 8:16, :] = end[3]


def adjoints(a, count, ids, deps, fwd, mid, dzr, uu, vf, vr, lbs, got):
    tiles = uu.shape[0]
    rows = tiles * 128
    shape = (tiles, 2, 128, 512)
    args = []
    for f, m in zip(fwd, mid):
        args += near_in(f[1], *m) + [f[3]]
    chan = slice(a * 512, a * 512 + 512)
    args += near_in(dzr, uu) + [vf[:, chan], vr[:, chan], lbs, got]
    return call_flat(
        functools.partial(adjoint_kernel, count), f"adjoints_{a}", ids, deps, args,
        [NEAR] * len(args),
        [near(shape, BF)] * 3 + [near((2, 16, 256), F32)],
        6, cost(rows * 1024 * 20, rows * 1024 * 4), scratch=[pltpu.VMEM((16, 256), F32)],
    )


def wgrad_kernel(which, nz, n_kept, ids, ubt, dzc, dzf, dzr, *rest):
    kept, rest = rest[: max(n_kept - 3, 0)], rest[max(n_kept - 3, 0) :]
    own, xp, yp, da, db = rest[:5]
    scr, sems = rest[5 + n_kept :]
    copies = [
        pltpu.make_async_copy(src, dst, sems.at[n])
        for n, (src, dst) in enumerate(zip((dzc, dzf, dzr, *kept), rest[5 : 5 + n_kept]))
    ]
    for copy in copies:
        copy.start()
    q, c = ids[0], ids[2]
    rh = 1 - c if which == "other" else c
    half = scr.shape[0]
    rows = ubt.shape[1]

    def tile(lhs):
        i = pl.program_id(0)
        for g, dz in enumerate((dzc, dzf, dzr)):
            rhs = dz[...].reshape(rows, 512)
            scr[:, g * 512 : (g + 1) * 512] = jnp.dot(
                lhs[...], rhs, preferred_element_type=F32
            ).astype(BF)

        def block(r, j):
            return scr[:, pl.ds(pl.multiple_of(((q ^ r) * 3 + j) * BLK, BLK), BLK)]

        at = pl.ds(pl.multiple_of(i * half, half), half)
        for j in range(3):
            own[j, at, :] = block(0, j)
            xp[j, at, :] = block(1, j)
            yp[j, at, :] = block(2, j)

        @pl.when(i < nz // 2)
        def _():
            for j in range(3):
                da[j, at, :] = block(3, j)

        @pl.when(i >= nz // 2)
        def _():
            back = pl.ds(pl.multiple_of((i - nz // 2) * half, half), half)
            for j in range(3):
                db[j, back, :] = block(3, j)

    pltpu.emit_pipeline(
        tile, grid=(nz,), in_specs=[pl.BlockSpec((half, rows), lambda i: (2 * i + rh, 0))]
    )(ubt)
    for copy in copies:
        copy.wait()


def weight_grad_part(which, nz, ids, deps, ubt, dz, keep=()):
    width, rows = ubt.shape
    half = width // nz // 2
    kept = (*dz, *keep) if keep else ()
    return call_flat(
        functools.partial(wgrad_kernel, which, nz, len(kept)), "weight_grad_part", ids, deps,
        [*far_in(ubt), *near_in(*dz, *keep)], [ANY] + [NEAR] * (3 + len(keep)),
        [sds((3, nz * half, BLK), BF)] * 3
        + [sds((3, nz * half // 2, BLK), BF)] * 2
        + [far(v.shape, v.dtype) for v in kept],
        10, cost(2 * rows * nz * half * 1536, rows * width + width * 1536),
        scratch=[pltpu.VMEM((half, 1536), BF), pltpu.SemaphoreType.DMA((4,))],
        out_specs=[NEAR] * 5 + [ANY] * len(kept),
    )


def relay_kernel(ids, xp, yp, ra, rb, s1, s2):
    half = ra.shape[1]
    s1[:, :half, :] = xp[:, :half, :]
    s1[:, half:, :] = (xp[:, half:, :].astype(F32) + rb[...].astype(F32)).astype(BF)
    s2[:, :half, :] = (yp[:, :half, :].astype(F32) + ra[...].astype(F32)).astype(BF)
    s2[:, half:, :] = yp[:, half:, :]


def relay_sums(ids, deps, xp, yp, ra, rb):
    rows = xp.shape[1]
    return call_flat(
        relay_kernel, "relay_sums", ids, deps, [xp, yp, ra, rb], [NEAR] * 4,
        [sds(xp.shape, BF)] * 2, 16, cost(rows * 768, rows * 384 * 10),
    )


def plane_sum_kernel(nz, ids, own, r1, r2, *outs):
    rows = outs[0].shape[1]
    for k, out in enumerate(outs):
        start = lax.rem(ids[1] + k, nz) * rows
        at = pl.ds(pl.multiple_of(start, rows), rows)
        tot = own[:, at, :].astype(F32) + r1[:, at, :].astype(F32) + r2[:, at, :].astype(F32)
        out[...] = tot.astype(out.dtype)


def plane_sums(nz, ids, deps, own, r1, r2):
    rows = own.shape[1] // nz
    return call_flat(
        functools.partial(plane_sum_kernel, nz), "plane_sums", ids, deps, [own, r1, r2], [NEAR] * 3,
        [sds((3, rows, BLK), F32)] + [sds((3, rows, BLK), BF)] * (nz - 1), 16,
        cost(rows * 768 * nz, rows * 384 * 8 * nz),
    )


def fold_kernel(sets, d, ids, *refs):
    n = sum(len(g) for g in sets) if sets else 2
    srcs, outs = refs[:n], refs[n:]
    if sets:
        groups, at = [], 0
        for g in sets:
            groups.append(srcs[at : at + len(g)])
            at += len(g)
    else:
        groups = [[ref.at[g] for ref in srcs] for g in range(srcs[0].shape[0])]
    half = groups[0][0].shape[1] // 2
    bit = lax.rem(lax.div(ids[1], d), 2) if d else 0
    for g, parts in enumerate(groups):
        spots = ((outs[0], bit), (outs[1], 1 - bit)) if d else ((outs[g], None),)
        for out, where in spots:
            rows = slice(None) if where is None else pl.ds(pl.multiple_of(where * half, half), half)
            total = parts[0][:, rows, :].astype(F32)
            for part in parts[1:]:
                total = total + part[:, rows, :].astype(F32)
            if d:
                out[g] = total.astype(out.dtype)
            else:
                out[...] = total


def fold_z(d, ids, deps, sets):
    stacked = not isinstance(sets[0], (list, tuple))
    args = list(sets) if stacked else [v for g in sets for v in g]
    count = sets[0].shape[0] if stacked else len(sets)
    _, rows, _ = args[0].shape[-3:]
    if d:
        shape = (count, 3, rows // 2, BLK)
        out_shape = [sds(shape, F32), sds(shape, BF)]
    else:
        out_shape = [sds((3, rows, BLK), F32)] * count
    return call_flat(
        functools.partial(fold_kernel, None if stacked else [tuple(g) for g in sets], d), "fold_z",
        ids, deps, args, [NEAR] * len(args), out_shape, 8,
        cost(rows * 768 * count, rows * 384 * 10 * count),
    )


DIMS = (((1,), (1,)), ((), ()))
TILE_N = 512


def unit_kernel(k, ids, *refs):
    first, second, ws = refs[0:4], refs[4:8], refs[8:12]
    far_out, out, lhs, e0, wbuf, sems, wsems, osems = refs[13 if k == 0 else 12 :]
    c = ids[2]
    rows = out.shape[0]
    tiles = ws[0].shape[0] // TILE_N

    def fetch(m):
        slot, lane, copies = m % 2, 0, []
        for n, w in enumerate(ws):
            cols = w.shape[1]
            dst = wbuf.at[slot, :, lane : lane + cols]
            src = w.at[m * TILE_N : (m + 1) * TILE_N, :]
            copies.append(pltpu.make_async_copy(src, dst, wsems.at[slot, n]))
            lane += cols
        return copies

    copies = [(first[3].at[:, k], e0)]
    for mp in range(2):
        for g, ref in enumerate(first[:3]):
            dst = mp * 768 + g * 256
            src = ref.at[:, k, :, mp * 256 : (mp + 1) * 256]
            copies.append((src, lhs.at[:, :, dst : dst + 256]))
    copies = [pltpu.make_async_copy(a, b, sems.at[n]) for n, (a, b) in enumerate(copies)]
    for copy in copies + fetch(0):
        copy.start()
    for mp in range(2):
        for g, ref in enumerate(second[:3]):
            dst = 1536 + mp * 768 + g * 256
            lhs[:, :, dst : dst + 256] = ref[:, k, :, mp * 256 : (mp + 1) * 256]
    for copy in copies:
        copy.wait()
    moved = []
    for m in range(tiles):
        if m + 1 < tiles:
            for copy in fetch(m + 1):
                copy.start()
        for copy in fetch(m):
            copy.wait()
        lo = m * TILE_N
        left = lhs[...].reshape(rows, 3072)
        acc = lax.dot_general(left, wbuf[m % 2], DIMS, preferred_element_type=F32)
        out[:, lo : lo + TILE_N] = acc.astype(out.dtype)
        cols = slice(m * BLK, (m + 1) * BLK)
        for a, val in enumerate((e0[:, :, cols], second[3][:, k, :, cols])):
            lane = pl.ds(pl.multiple_of(lo + a * BLK + c * 256, BLK), BLK)
            total = out[:, lane].astype(F32) + val.reshape(rows, BLK).astype(F32)
            out[:, lane] = total.astype(out.dtype)
        slot = 1 - c if k else c
        done = pltpu.make_async_copy(
            out.at[:, lo : lo + TILE_N], far_out.at[slot, :, lo : lo + TILE_N], osems.at[m]
        )
        done.start()
        moved.append(done)
    for done in moved:
        done.wait()


def unit_grads(k, ids, deps, first, second, ws, held):
    tiles = first[0].shape[0]
    rows, width = tiles * 128, ws[0].shape[0]
    args = [*far_in(*first), *near_in(*second), *far_in(*ws)]
    return call_flat(
        functools.partial(unit_kernel, k), f"unit_grads_{k}", ids, deps, args + far_in(*held),
        [ANY] * 4 + [NEAR] * 4 + [ANY] * (4 + len(held)),
        far((2, rows, width), BF), 24, cost(2 * rows * width * 3072, width * 3072 * 2),
        scratch=[
            pltpu.VMEM((rows, width), BF),
            pltpu.VMEM((tiles, 128, 3072), BF),
            pltpu.VMEM((tiles, 128, 512), BF),
            pltpu.VMEM((2, TILE_N, 3072), BF),
            pltpu.SemaphoreType.DMA((7,)),
            pltpu.SemaphoreType.DMA((2, 4)),
            pltpu.SemaphoreType.DMA((width // TILE_N,)),
        ],
        out_specs=ANY, aliases={len(args): 0} if held else {},
    )


def norm_grad_kernel(ids, du2, tok, cot, lim, scl, gain, *rest):
    accb, accc = rest[:2], rest[2:4]
    out, sums, ga, ba, scr = rest[4:]
    c = ids[2]
    ga[...] = jnp.zeros_like(ga)
    ba[...] = jnp.zeros_like(ba)

    def tile(dur, tokr, cotr, outr):
        i = pl.program_id(0)
        for j in range(scr.shape[0]):
            lanes = slice(j * BLK, (j + 1) * BLK)
            scr[j, 0:128, :] = dur[0, :, lanes].astype(F32) + dur[1, :, lanes].astype(F32)
        step = lax.broadcasted_iota(jnp.int32, (STEPS, 1), 0) + i * STEPS
        gsum = jnp.zeros(ga.shape, F32)
        bsum = jnp.zeros(ba.shape, F32)
        for st in range(8):
            sq, h = divmod(st, PARTS)
            x16 = tokr[sq, h].astype(F32)
            c16 = cotr[sq, h].astype(F32)
            for part in range(2):
                cut = slice(part * 8, part * 8 + 8)
                du = jnp.concatenate(
                    [scr[j, pl.ds(st + part * 64, 8, stride=8), :] for j in range(scr.shape[0])],
                    axis=1,
                )
                normed, rstd = norm_of(x16[cut])
                dn = du * gain[...]
                m1 = jnp.mean(dn, axis=-1, keepdims=True)
                m2 = jnp.mean(dn * normed, axis=-1, keepdims=True)
                gy = jnp.where(step[cut] < lim[st], c16[cut] * scl[0], 0.0)
                outr[sq, h, cut, :] = rstd * (dn - m1 - normed * m2) + gy
                gsum = gsum + du * normed
                bsum = bsum + du
        ga[...] += gsum
        ba[...] += bsum

    seqs, parts, steps, width = tok.shape
    nat = pl.BlockSpec((seqs, parts, STEPS, width), lambda i: (0, 0, i, 0))
    pltpu.emit_pipeline(
        tile,
        grid=(steps // STEPS,),
        in_specs=[pl.BlockSpec((2, 128, width), lambda i: (0, i, 0)), nat, nat],
        out_specs=[nat],
    )(du2, tok, cot, out)
    sums[...] = jnp.zeros_like(sums)
    sums[4:5, :] = jnp.sum(ga[...], axis=0, keepdims=True)
    sums[5:6, :] = jnp.sum(ba[...], axis=0, keepdims=True)
    for s in range(4):
        a, mp = divmod(s, 2)
        rows = (
            accc[a][mp, 0:8, :],
            accb[a][mp, 0:8, :],
            accc[a][mp, 8:16, :],
            accb[a][mp, 8:16, :],
        )
        for j, val in enumerate(rows):
            val = jnp.sum(val, axis=0, keepdims=True)
            for mm in range(2):
                lane = pl.ds(core_lane(a, 2 * mp + mm, c), BLK)
                sums[j : j + 1, lane] = val[:, mm * BLK : (mm + 1) * BLK]


def norm_grads(ids, deps, du2, tok, cot, lim8, scale, gain, accb, accc):
    _, rows, width = du2.shape
    n = rows * width
    return call_flat(
        norm_grad_kernel, "norm_grads", ids, deps,
        [*far_in(du2, tok, cot), lim8, scale, gain, *accb, *accc],
        [ANY] * 3 + [SMEM] * 2 + [NEAR] * 5,
        [far(tok.shape, F32), sds((8, width), F32)], 14, cost(n * 20, n * 8),
        scratch=[
            pltpu.VMEM((8, width), F32),
            pltpu.VMEM((8, width), F32),
            pltpu.VMEM((width // BLK, 136, BLK), F32),
        ],
        out_specs=[ANY, NEAR],
    )


def activation_kernel(ids, tok, hown, hrcv, out, scr):
    c = ids[2]
    for s in range(4):
        a, mp = divmod(s, 2)
        for mm in range(2):
            for n, (ref, core) in enumerate(((hown, c), (hrcv, 1 - c))):
                scr[n, 0:128, :] = ref[s, mm].astype(F32)
                lane = pl.ds(core_lane(a, 2 * mp + mm, core), BLK)
                for st in range(8):
                    sq, h = divmod(st, PARTS)
                    val = scr[n, pl.ds(st, STEPS, stride=8), :]
                    out[sq, h, :, lane] = tok[sq, h, :, lane].astype(F32) + val


def activations_of(ids, deps, tok, hown, hrcv):
    seqs, parts, steps, width = tok.shape
    tiles = steps // STEPS
    nat = pl.BlockSpec((seqs, parts, STEPS, width), lambda i, ids: (0, 0, i, 0))
    hspec = pl.BlockSpec((4, 2, 128, BLK), lambda i, ids: (0, 0, i, 0))
    n = seqs * parts * steps * width
    return call(
        activation_kernel, "activations_of", (tiles,), ids, deps, far_in(tok, hown, hrcv),
        [nat, hspec, hspec], nat, far(tok.shape, F32), 16, cost(n, n * 8),
        scratch=[pltpu.VMEM((2, 136, BLK), F32)],
    )


def assemble_kernel(counts, ids, *refs):
    out = refs[-1]
    c = ids[2]
    start = 0
    for b, n in enumerate(counts):
        group = refs[start : start + n]
        start += n
        a, core = b % 2, c if b < 2 else 1 - c
        for j in range(3):
            total = group[0][j]
            for ref in group[1:]:
                total = total + ref[j].astype(F32)
            lane = pl.multiple_of(j * 512 + a * BLK + core * 256, BLK)
            out[:, pl.ds(lane, BLK)] = total


def assemble(ids, deps, groups):
    rows = groups[0][0].shape[1]
    counts = [len(g) for g in groups]
    args = [ref for group in groups for ref in group]
    return call_flat(
        functools.partial(assemble_kernel, counts), "assemble", ids, deps, args,
        [NEAR] * len(args), sds((rows, 1536), F32), 16, cost(0, rows * 1536 * 8),
    )


def local(
    nseq,
    ndp,
    tokens,
    cotangent,
    weight,
    forget_peep,
    reset_peep,
    forget_bias,
    reset_bias,
    norm_gain,
    norm_bias,
    lengths,
):
    axes = ("seq", "dp")
    nz = ndp // 2
    seqs, span, width = tokens.shape
    sub = span // PARTS
    q = lax.axis_index("seq").astype(jnp.int32)
    dp = lax.axis_index("dp").astype(jnp.int32)
    z, c = dp // 2, dp % 2
    ids = jnp.stack([q, z, c])

    def table(move):
        pairs = []
        for qq in range(nseq):
            for zz in range(nz):
                for cc in range(2):
                    to = move(qq, zz, cc)
                    if to is not None:
                        pairs.append((qq * ndp + zz * 2 + cc, to[0] * ndp + to[1] * 2 + to[2]))
        return pairs

    def send(value, move):
        return lax.ppermute(value, axes, table(move))

    def to_core(qq, zz, cc):
        return (qq, zz, 1 - cc)

    def to_x(qq, zz, cc):
        return (qq ^ 1, zz, cc)

    def to_y(qq, zz, cc):
        return (qq ^ 2, zz, cc)

    def shift_z(k):
        return lambda qq, zz, cc: (qq, (zz + k) % nz, cc)

    def shift_zc(k):
        return lambda qq, zz, cc: (qq, (zz + k) % nz, 1 - cc)

    def shift_q(k):
        return lambda qq, zz, cc: (qq + k, zz, cc) if 0 <= qq + k < nseq else None

    mine, theirs = split_weight(ids, weight)
    recv = send(theirs, to_core)
    nat = (seqs, PARTS, sub, width)
    tok4 = tokens.reshape(nat)
    cot4 = cotangent.reshape(nat)
    tok_oth = send(tokens, to_core).reshape(nat)
    len_oth = send(lengths, to_core)

    lens = jnp.stack([lengths, len_oth])
    counts = jnp.sum(lens, axis=1).astype(F32)
    scale = (seqs * span * nseq) / counts
    lim16 = (
        lens[:, :, None] - q * span - sub * jnp.arange(PARTS, dtype=jnp.int32)[None, None, :]
    ).reshape(2, 8)
    spread_rows = lambda v: jnp.broadcast_to(v, (2, STEPS, 8, BLK)).reshape(256, BLK)
    step_in_tile = jnp.arange(STEPS, dtype=jnp.int32)[None, :, None, None]
    lim = spread_rows(lim16[:, None, :, None] - step_in_tile)
    scl = spread_rows(scale[:, None, None, None])

    lim8, scale1 = lim16[0], scale[:1]

    def by_core(vec):
        v = lax.dynamic_slice_in_dim(vec.reshape(4, 4, BLK), 2 * c, 2, 1)
        return v.transpose(1, 0, 2).reshape(1, width // 2)

    vf, vr, bfor, brst = (by_core(v) for v in (forget_peep, reset_peep, forget_bias, reset_bias))
    gain, bias = norm_gain.reshape(1, width), norm_bias.reshape(1, width)

    tail = [mine]

    def run(kernel, *head, rest=(), token=-1, after=(), big=False):
        out = kernel(*head, ids, (tail[0], *after), *rest)
        tail[0] = out[token] if isinstance(out, (list, tuple)) else out
        if big:
            (tail[0],) = far_in(tail[0])
        return out

    groups = [[cc + 2 * zz for zz in range(nz)] for cc in range(2)]

    def along_z(piece):
        if nz <= 4:
            return [send(piece, shift_z(-k)) for k in range(1, nz)]
        got = lax.all_gather(piece, "dp", axis=0, tiled=True, axis_index_groups=groups)
        n = got.shape[0] // nz
        twice = jnp.concatenate([got, got], axis=0)
        return [lax.dynamic_slice_in_dim(twice, (z + 1) * n, n * (nz - 1), 0)]

    def gather_1(s, zs, after=()):
        rel = run(plane_pieces, s, rest=(zs,), after=after)
        return rel, send(rel, to_x), send(rel, to_y)

    def gather_2(s, got, after=()):
        rel, gx, gy = got
        tox, toy = run(cross_pieces, s, rest=(gx, gy), after=after)
        return rel, gx, gy, send(tox, to_x), send(toy, to_y)

    def spread(both):
        return lax.all_gather(both, "seq")

    def run_project(s, weights, before=None, after=()):
        rest = (ub, ulo, weights, lim, vf, bfor, before)
        return run(project, s, nz, rest=rest, token=4, after=after)

    def run_states(a, fwd, got, held, after=()):
        rest = (fwd, ub, ulo, cot4, cot_oth, lim, scl, vr, brst, got, held)
        out = run(states, a, nseq, rest=rest, after=after)
        return {
            "h": out[:2], "mid": (out[2:5], out[5:8]), "dzr": out[8], "u": out[9],
            "lbs": out[10], "summ": out[11], "acc": out[12],
        }

    def run_adjoints(a, fwd, m, got, after=()):
        rest = (fwd, m["mid"], m["dzr"], m["u"], vf, vr, m["lbs"], got)
        du, dzc, dzf, acc = run(adjoints, a, nseq, rest=rest, after=after)
        return {"du": du, "dz": (dzc, dzf, m["dzr"]), "acc": acc}

    def sum_1(which, dz, keep=(), after=(), hold=False):
        own, xp, yp, da, db, *kept = run(
            weight_grad_part, which, nz, rest=(ubt, dz, keep), token=3, after=after
        )
        if hold:
            da, db = run(gate, rest=((da, db),))
        return (own, xp, yp, send(da, to_x), send(db, to_y)), kept

    def sum_2(got, after=()):
        own, xp, yp, ra, rb = got
        s1, s2 = run(relay_sums, rest=(xp, yp, ra, rb), after=after)
        return own, send(s1, to_x), send(s2, to_y)

    def fold(sets, d):
        kept, out = run(fold_z, d, rest=(sets,))
        return kept, send(out, lambda qq, zz, cc: (qq, zz ^ d, cc))

    def sum_3_now(got):
        if nz > 4:
            got, d = [got], nz // 2
            while d:
                got, d = fold(got, d), d // 2
            return run(fold_z, 0, rest=(got,))
        parts = list(run(plane_sums, nz, rest=got))
        return parts[:1] + [send(parts[k], shift_z(k)) for k in range(1, nz)]

    def fold_rest(got):
        d = nz // 4
        while d:
            got, d = fold(got, d), d // 2
        return got

    high, p0, p1 = run(quarter_of, rest=(mine, recv), after=(tok_oth, len_oth))
    z0 = along_z(p0)
    cot_cols = run(other_columns, rest=(cotangent,), big=True)
    cot_oth = send(cot_cols, to_core).reshape(seqs, PARTS, sub, width // 2)
    z1 = along_z(p1)
    ub, ubt, ulo = run(
        norm_tokens, rest=(tok4, tok_oth, gain, bias), big=True, after=(lim8, scale1, lim, scl, cot_oth)
    )
    g0 = gather_1(0, z0)
    g0 = gather_2(0, g0)
    g1 = gather_1(1, z1)
    z23 = along_z(run(hand_on, rest=(high,)))
    f0 = run_project(0, (mine, recv, *g0))
    g1 = gather_2(1, g1)
    f1 = run_project(1, (mine, recv, *g1), f0[4])
    got = spread(f1[4])
    g2 = gather_1(2, z23, after=(got,))
    m0 = run_states(0, (f0, f1), got, ())
    got = spread(m0["summ"])
    g2 = gather_2(2, g2, after=(got,))
    d0 = run_adjoints(0, (f0, f1), m0, got)
    s0, _ = sum_1("other", d0["dz"])
    g3 = gather_1(3, z23, after=g2[3:])
    f2 = run_project(2, (mine, recv, *g2))
    g3 = gather_2(3, g3)
    s0 = sum_2(s0)
    s1, first = sum_1("own", d0["dz"], (d0["du"],))
    f3 = run_project(3, (mine, recv, *g3), f2[4])
    got = spread(f3[4])
    s1 = sum_2(s1, after=(got,))
    m1 = run_states(1, (f2, f3), got, m0["h"], after=s0[1:])
    s01 = fold([s0, s1], nz // 2)
    hrcv = send(run(gate, rest=(m1["h"][1:], "far"))[0], to_core)
    got = spread(run(hand_on, rest=(m1["summ"],)))
    d1 = run_adjoints(1, (f2, f3), m1, got)
    s2, _ = sum_1("other", d1["dz"])
    s3, _ = sum_1("own", d1["dz"], after=(hrcv,))
    s2 = sum_2(s2)
    s01 = fold_rest(s01)
    second = (*d1["dz"], d1["du"])
    ws = (f0[5], f1[5], f2[5], f3[5])
    du2 = run(unit_grads, 1, rest=(first, second, ws, ()), big=True)
    s3 = sum_2(s3)
    du2 = run(unit_grads, 0, rest=(first, second, ws, (du2,)), big=True)
    s2 = fold([s2], nz // 2)
    s0, s1 = run(fold_z, 0, rest=(s01,))
    s0 = send(s0, to_core)
    s3 = sum_3_now(s3)
    cores = [[2 * zz, 2 * zz + 1] for zz in range(nz)]
    du2 = lax.all_to_all(du2, "dp", 0, 0, axis_index_groups=cores, tiled=True)
    activations = run(activations_of, rest=(tok4, m1["h"][0], hrcv), big=True)
    input_grad, sums = run(
        norm_grads,
        rest=(
            du2, tok4, cot4, lim8, scale1, gain, (m0["acc"], m1["acc"]), (d0["acc"], d1["acc"])
        ),
        after=(s0,),
    )
    s2 = fold_rest(s2)
    s3 = run(fold_z, 0, rest=([s3],))
    if nz <= 4:
        sums = run(add_up, rest=(sums, *[send(sums, shift_z(k)) for k in range(1, nz)]))
    else:
        for b in range((nz - 1).bit_length()):
            hop = lambda qq, zz, cc, b=1 << b: (qq, zz ^ b, cc)
            sums = run(add_up, rest=(sums, send(sums, hop)))
    s2 = send(run(fold_z, 0, rest=(s2,))[0], to_core)
    moved = [send(sums, lambda qq, zz, cc, b=b: (qq ^ b, zz, cc)) for b in range(1, nseq)]
    sums = run(add_up, rest=(sums, *moved))
    moved = send(sums, to_core)
    sums = run(add_up, rest=(sums, moved))
    weight_grad = run(assemble, rest=(([s1], s3, [s0], [s2]),))
    shape = tokens.shape
    return (
        activations.reshape(shape),
        input_grad.reshape(shape),
        weight_grad,
        sums[0],
        sums[1],
        sums[2],
        sums[3],
        sums[4],
        sums[5],
    )


def solution(mesh):
    whole = P("dp", "seq", None)
    in_specs = (whole, whole, P("dp", None)) + (P(),) * 6 + (P("dp"),)
    out_specs = (whole, whole, P("dp", "seq")) + (P(),) * 6
    step = functools.partial(local, mesh.shape["seq"], mesh.shape["dp"])
    return jax.shard_map(step, mesh=mesh, in_specs=in_specs, out_specs=out_specs, check_vma=False)
```

```python
import functools

import jax
import jax.numpy as jnp
from jax import lax
from jax.experimental import pallas as pl
from jax.experimental.pallas import tpu as pltpu
from jax.sharding import PartitionSpec as P

EPS = 1e-05
F32 = jnp.float32
BF = jnp.bfloat16
STEPS = 16
BLK = 128
GATES = 3
QUARTERS = 4
PARTS = 4


def params(mib, dims=1):
    return pltpu.CompilerParams(
        vmem_limit_bytes=mib * 1024 * 1024, dimension_semantics=("arbitrary",) * dims
    )


def cost(flops, bytes_accessed, transcendentals=0):
    return pl.CostEstimate(
        flops=int(flops), bytes_accessed=int(bytes_accessed), transcendentals=int(transcendentals)
    )


def sds(shape, dtype):
    return jax.ShapeDtypeStruct(shape, dtype)


def far(shape, dtype):
    return pltpu.HBM(shape, dtype)


def near(shape, dtype):
    return pltpu.VMEM(shape, dtype)


def far_in(*values):
    return [pltpu.with_memory_space_constraint(v, pltpu.HBM) for v in values]


def near_in(*values):
    return [pltpu.with_memory_space_constraint(v, pltpu.VMEM) for v in values]


ANY = pl.BlockSpec(memory_space=pl.ANY)
NEAR = pl.BlockSpec(memory_space=pltpu.VMEM)
SMEM = pl.BlockSpec(memory_space=pltpu.SMEM)


def ordered(kernel, deps):
    n = len(deps)

    def body(ids, *refs):
        return kernel(ids, *refs[n:])

    return body, list(deps), [ANY] * n


def call(kernel, name, grid, ids, deps, args, in_specs, out_specs, out_shape, mib, est, scratch=()):
    body, deps, dep_specs = ordered(kernel, deps)
    return pl.pallas_call(
        body,
        grid_spec=pltpu.PrefetchScalarGridSpec(
            num_scalar_prefetch=1,
            grid=grid,
            in_specs=dep_specs + in_specs,
            out_specs=out_specs,
            scratch_shapes=list(scratch),
        ),
        out_shape=out_shape,
        compiler_params=params(mib, len(grid)),
        cost_estimate=est,
        name=name,
    )(ids, *deps, *args)


def call_flat(kernel, name, ids, deps, args, in_specs, out_shape, mib, est, scratch=(), out_specs=None, aliases=None):
    body, deps, dep_specs = ordered(kernel, deps)
    many = isinstance(out_shape, (list, tuple))
    if out_specs is None:
        out_specs = [NEAR] * len(out_shape) if many else NEAR
    shift = 1 + len(deps)
    return pl.pallas_call(
        body,
        in_specs=[SMEM] + dep_specs + in_specs,
        out_specs=out_specs,
        out_shape=out_shape,
        scratch_shapes=list(scratch),
        input_output_aliases={k + shift: v for k, v in (aliases or {}).items()},
        compiler_params=pltpu.CompilerParams(vmem_limit_bytes=mib * 1024 * 1024),
        cost_estimate=est,
        name=name,
    )(ids, *deps, *args)


def split_kernel(ids, w, mine, theirs):
    c = ids[2]
    for s in range(4):
        a, mp = divmod(s, 2)
        for g in range(GATES):
            for mm in range(2):
                dst = s * 768 + g * 256 + mm * BLK
                base = g * 2048 + (2 * mp + mm) * 512 + a * BLK
                here = pl.multiple_of(base + c * 256, BLK)
                there = pl.multiple_of(base + (1 - c) * 256, BLK)
                mine[:, dst : dst + BLK] = w[:, pl.ds(here, BLK)]
                theirs[:, dst : dst + BLK] = w[:, pl.ds(there, BLK)]


def split_weight(ids, weight):
    rows, cols = weight.shape
    tile = max(rows // 4, 16)
    spec = pl.BlockSpec((tile, cols // 2), lambda i, ids: (i, 0))
    return call(
        split_kernel, "split_weight", (rows // tile,), ids, (), far_in(weight),
        [pl.BlockSpec((tile, cols), lambda i, ids: (i, 0))], [spec, spec],
        [sds((rows, cols // 2), BF)] * 2, 16, cost(0, rows * cols * 4),
    )


def quarter_kernel(ids, mine, recv, high, p0, p1):
    q, c = ids[0], ids[2]
    half = high.shape[0]
    at = pl.ds(pl.multiple_of(lax.rem(q, 2) * half, half), half)
    first = (lax.div(q, 2) == c).astype(jnp.int32) == 1
    val = jnp.where(first, mine[at, :], recv[at, :])
    high[...] = val[:, 1536:]
    p0[...] = val[:, :768]
    p1[...] = val[:, 768:1536]


def quarter_of(ids, deps, mine, recv):
    rows, cols = mine.shape
    half = rows // 2
    return call_flat(
        quarter_kernel, "quarter_of", ids, deps, [mine, recv], [NEAR, NEAR],
        [sds((half, 1536), BF), sds((half, 768), BF), sds((half, 768), BF)], 8,
        cost(0, rows * cols * 4),
    )


def columns_kernel(ids, *refs):
    dst = refs[-1]
    for m, src in enumerate(refs[:-1]):
        dst[:, :, m * 256 : (m + 1) * 256] = src[...]


def other_columns(ids, deps, value):
    seqs, span, width = value.shape
    step = span // 4

    def part(m):
        return pl.BlockSpec((seqs, step, 256), lambda i, ids: (0, i, 2 * m + 1 - ids[2]))

    return call(
        columns_kernel, "other_columns", (4,), ids, deps, far_in(*[value] * QUARTERS),
        [part(m) for m in range(QUARTERS)],
        pl.BlockSpec((seqs, step, width // 2), lambda i, ids: (0, i, 0)),
        far((seqs, span, width // 2), value.dtype), 12, cost(0, value.size * 3),
    )


def copy_kernel(ids, src, dst):
    dst[...] = src[...]


def hand_on(ids, deps, value):
    return call_flat(
        copy_kernel, "hand_on", ids, deps, [value], [NEAR], sds(value.shape, value.dtype), 16,
        cost(0, value.size * 4),
    )


def gate_kernel(ids, *refs):
    pass


def gate(ids, deps, values, hold=None):
    shape = {None: sds, "far": far, "near": near}[hold]
    held = {None: lambda *v: list(v), "far": far_in, "near": near_in}[hold]
    return call_flat(
        gate_kernel, "gate", ids, deps, held(*values), [ANY] * len(values),
        [shape(v.shape, v.dtype) for v in values], 4, cost(0, 1), out_specs=[ANY] * len(values),
        aliases={n: n for n in range(len(values))},
    )


def add_kernel(ids, *refs):
    total = refs[0][...]
    for ref in refs[1:-1]:
        total = total + ref[...]
    refs[-1][...] = total


def add_up(ids, deps, *values):
    a = values[0]
    return call_flat(
        add_kernel, "add_up", ids, deps, list(values), [NEAR] * len(values), sds(a.shape, a.dtype),
        4, cost(a.size, a.size * 4 * len(values)),
    )


def plane_kernel(s, ids, *refs):
    rel = refs[-1]
    row = 0
    for ref in refs[:-1]:
        lane = s % 2 * 768 if ref.shape[1] > 768 else 0
        rel[row : row + ref.shape[0], :] = ref[:, lane : lane + 768]
        row += ref.shape[0]


def plane_pieces(s, ids, deps, parts):
    rows = sum(p.shape[0] for p in parts)
    return call_flat(
        functools.partial(plane_kernel, s), f"plane_pieces_{s}", ids, deps, list(parts),
        [NEAR] * len(parts), sds((rows, 768), BF), 8, cost(0, rows * 768 * 4),
    )


def cross_kernel(ids, gx, gy, tox, toy):
    tox[...] = gy[:, :384]
    toy[...] = gx[:, 384:]


def cross_pieces(s, ids, deps, gx, gy):
    rows = gx.shape[0]
    return call_flat(
        cross_kernel, f"cross_pieces_{s}", ids, deps, [gx, gy], [NEAR, NEAR],
        [sds((rows, 384), BF)] * 2, 16, cost(0, rows * 768 * 4),
    )


def norm_of(x):
    mean = jnp.mean(x, axis=-1, keepdims=True)
    centered = x - mean
    var = jnp.mean(centered * centered, axis=-1, keepdims=True)
    rstd = lax.rsqrt(var + EPS)
    return centered * rstd, rstd


def norm_kernel(ids, own, other, gain, bias, ub, ubt, ulo, scr):
    c = ids[2]
    seqs = own.shape[0]
    for k, ref in enumerate((own, other)):
        for st in range(8):
            sq, h = divmod(st, PARTS)
            normed, _ = norm_of(ref[sq, h].astype(F32))
            unit = normed * gain[...] + bias[...]
            for j in range(scr.shape[0]):
                scr[j, pl.ds(k * 128 + st, STEPS, stride=8), :] = unit[:, j * BLK : (j + 1) * BLK]
    for j in range(scr.shape[0]):
        low = scr[j, 0:256, :].astype(BF)
        ub[0, :, :, j * BLK : (j + 1) * BLK] = low.reshape(2, 128, BLK)
        ubt[j * BLK : (j + 1) * BLK, :] = low.T
    for a in range(2):
        for m in range(QUARTERS):
            unit = scr[m * 4 + a + 2 * c, 0:256, :]
            rest = (unit - unit.astype(BF).astype(F32)).astype(BF)
            dst = (a * QUARTERS + m) * BLK
            ulo[0, :, :, dst : dst + BLK] = rest.reshape(2, 128, BLK)


def tile_block(cols):
    return pl.BlockSpec((1, 2, 128, cols), lambda i, ids: (i, 0, 0, 0))


def norm_tokens(ids, deps, own, other, gain, bias):
    seqs, parts, steps, width = own.shape
    rows = seqs * parts * steps
    tiles = steps // STEPS
    nat = pl.BlockSpec((seqs, parts, STEPS, width), lambda i, ids: (0, 0, i, 0))
    vec = pl.BlockSpec((1, width), lambda i, ids: (0, 0))
    return call(
        norm_kernel, "norm_tokens", (tiles,), ids, deps, [*far_in(own, other), gain, bias],
        [nat, nat, vec, vec],
        [
            tile_block(width),
            pl.BlockSpec((width, 256), lambda i, ids: (0, i)),
            tile_block(width // 2),
        ],
        [
            far((tiles, 2, 128, width), BF),
            far((width, 2 * rows), BF),
            far((tiles, 2, 128, width // 2), BF),
        ],
        20, cost(rows * width * 20, rows * width * 14),
        scratch=[pltpu.VMEM((width // BLK, 264, BLK), F32)],
    )


def flat(ref):
    value = ref[...]
    return value.reshape(256, value.shape[-1])


def core_lane(a, m, c):
    return pl.multiple_of(m * 512 + a * BLK + c * 256, BLK)


def pairs():
    for tp in range(STEPS // 2):
        for k in range(2):
            yield k, tp * 16, k * 128 + tp * 16


def live_pair(lim, row, tile):
    live = lim[row : row + 16, :] > tile * STEPS
    return jnp.concatenate([live, live], axis=1)


def fold_streams(pr, lc, ahead):
    out = []
    order = range(PARTS) if ahead else range(PARTS - 1, -1, -1)
    for sq in range(2):
        tp = tl = None
        for h in order:
            n = sq * PARTS + h
            p, l = pr[n : n + 1], lc[n : n + 1]
            tp, tl = (p, l) if tp is None else ((p * tp, p * tl + l) if ahead else (p * tp, l + p * tl))
        out.append((tp, tl))
    return out


def proj_kernel(s, nz, joined, ids, ub, ulo, *rest):
    n_w = 1 if joined else 7
    weights, rest = rest[:n_w], rest[n_w:]
    lim, vf, bfor = rest[:3]
    rest = rest[3:]
    before = rest[0] if s % 2 else None
    cand_far, decay, rpre_far, plout, summ = rest[s % 2 : s % 2 + 5]
    rest = rest[s % 2 + 5 :]
    if joined:
        zbuf, prod, loc, wbuf, sems = rest
    else:
        wall, zbuf, prod, loc, wbuf, sems = rest
    tiles = decay.shape[0]
    width = wbuf.shape[0]
    q, z, c = ids[0], ids[1], ids[2]
    a, mp = divmod(s, 2)
    cols = slice(mp * 768, mp * 768 + 768)
    copies = []

    def put(src, row, rows, lo=0, hi=768):
        dst = wbuf.at[pl.ds(row, rows), lo:hi]
        copy = pltpu.make_async_copy(src, dst, sems.at[len(copies)])
        copy.start()
        copies.append(copy)

    if joined:
        put(weights[0].at[:, cols], 0, width)
    else:
        mine, recv, rel, gx, gy, dx, dy = weights
        zb = width // nz
        zb2, qb = zb // 2, zb // 4
        mult = lambda v: pl.multiple_of(v, qb)
        put(mine.at[:, s * 768 : (s + 1) * 768], mult(z * zb + c * zb2), zb2)
        put(recv.at[:, s * 768 : (s + 1) * 768], mult(z * zb + (1 - c) * zb2), zb2)
        for r in range(1, nz):
            base = lax.rem(z + r, nz) * zb
            lo, hi = (r - 1) * qb, r * qb
            put(rel.at[lo:hi, :], mult(base + q * qb), qb)
            put(gx.at[lo:hi, :], mult(base + (q ^ 1) * qb), qb)
            put(gy.at[lo:hi, :], mult(base + (q ^ 2) * qb), qb)
            put(dx.at[lo:hi, :], mult(base + (q ^ 3) * qb), qb, 0, 384)
            put(dy.at[lo:hi, :], mult(base + (q ^ 3) * qb), qb, 384, 768)
    for copy in copies:
        copy.wait()
    if not joined:
        keep = pltpu.make_async_copy(wbuf, wall, sems.at[len(copies)])
        keep.start()
    prod[...] = jnp.ones_like(prod)
    loc[...] = jnp.zeros_like(loc)

    def tile(ubr, ulor, cand, rpre):
        i = pl.program_id(0)
        zbuf[:, :768] = jnp.dot(flat(ubr), wbuf[...], preferred_element_type=F32)
        low = flat(ulor).astype(F32)
        for mm in range(2):
            high = ubr[:, :, :, pl.ds(core_lane(a, 2 * mp + mm, c), BLK)].reshape(256, BLK)
            zbuf[:, 768 + mm * BLK : 768 + (mm + 1) * BLK] = (
                high.astype(F32) + low[:, mm * BLK : (mm + 1) * BLK]
            )
        pr = [prod[0:8, :], prod[8:16, :]]
        lc = [loc[0:8, :], loc[8:16, :]]
        for k, r0, row in pairs():
            cd = zbuf[row : row + 16, :256]
            logit = zbuf[row : row + 16, 256:512] + vf[...] * zbuf[row : row + 16, 768:] + bfor[...]
            dec = jnp.where(live_pair(lim, row, i), jax.nn.sigmoid(logit), 1.0)
            inj = (1.0 - dec) * cd
            cand[0, k, r0 : r0 + 16, :] = cd
            decay[i, k, r0 : r0 + 16, :] = dec
            rpre[0, k, r0 : r0 + 16, :] = zbuf[row : row + 16, 512:768]
            for t in range(2):
                d = dec[t * 8 : t * 8 + 8]
                lc[k] = d * lc[k] + inj[t * 8 : t * 8 + 8]
                pr[k] = d * pr[k]
        for k in range(2):
            prod[k * 8 : k * 8 + 8, :] = pr[k]
            loc[k * 8 : k * 8 + 8, :] = lc[k]

    pltpu.emit_pipeline(
        tile,
        grid=(tiles,),
        in_specs=[
            pl.BlockSpec((1, 2, 128, width), lambda i: (i, 0, 0, 0)),
            pl.BlockSpec((1, 2, 128, 256), lambda i: (i, 0, 0, s)),
        ],
        out_specs=[pl.BlockSpec((1, 2, 128, 256), lambda i: (i, 0, 0, 0))] * 2,
    )(ub, ulo, cand_far, rpre_far)
    if s % 2:
        summ[0] = before[0]
    plout[0:16, :] = prod[...]
    plout[16:32, :] = loc[...]
    for k in range(2):
        pr, lc = prod[k * 8 : k * 8 + 8, :], loc[k * 8 : k * 8 + 8, :]
        for sq, (tp, tl) in enumerate(fold_streams(pr, lc, True)):
            ks = k * 2 + sq
            summ[s % 2, ks : ks + 1, :] = tp
            summ[s % 2, 4 + ks : 5 + ks, :] = tl
    if not joined:
        keep.wait()


def project(s, nz, ids, deps, ub, ulo, weights, lim, vf, bfor, before):
    tiles, _, _, width = ub.shape
    joined = len(weights) == 1
    shape = (tiles, 2, 128, 256)
    rows = tiles * 256
    chan = slice(s * 256, s * 256 + 256)
    args = far_in(ub, ulo, *weights) + [lim, vf[:, chan], bfor[:, chan]]
    in_specs = [ANY] * (2 + len(weights)) + [NEAR] * 3
    if s % 2:
        args.append(before)
        in_specs.append(NEAR)
    out_shape = [far(shape, F32), near(shape, F32), far(shape, F32)]
    out_shape += [near((32, 256), F32), near((2, 8, 256), F32)]
    out_specs = [ANY, NEAR, ANY, NEAR, NEAR]
    if not joined:
        out_shape.append(far((width, 768), BF))
        out_specs.append(ANY)
    return call_flat(
        functools.partial(proj_kernel, s, nz, joined), f"project_{s}", ids, deps, args, in_specs,
        out_shape, 12, cost(2 * rows * width * 768, rows * width * 2 + width * 768 * 4),
        scratch=[
            pltpu.VMEM((256, 1024), F32),
            pltpu.VMEM((16, 256), F32),
            pltpu.VMEM((16, 256), F32),
            pltpu.VMEM((width, 768), BF),
            pltpu.SemaphoreType.DMA((3 + 5 * (nz - 1),)),
        ],
        out_specs=out_specs,
    )


def halves(v):
    return v[:8], v[8:]


def enter(got, n, ahead, q, count):
    value = jnp.zeros((4, 256), F32)
    for j in range(count) if ahead else range(count - 1, -1, -1):
        used = (j < q) if ahead else (j > q)
        longer = got[j, n, 4:8, :] + got[j, n, 0:4, :] * value
        value = jnp.where(used, longer, value)
    return value


def state_kernel(a, count, held, ids, *refs):
    fwd = (refs[0:4], refs[4:8])
    ub, ulo, cot_own, cot_oth, lim, scl, vr, br, got = refs[8:17]
    rest = refs[17 + (2 if held else 0) :]
    hown, hoth = rest[:2]
    out = (rest[2:5], rest[5:8])
    dzr, uu, lbs, summ, acc, st, pp, lb, ac, scr = rest[8:]
    tiles = dzr.shape[0]
    q, c = ids[0], ids[2]
    for n in range(2):
        cand_far, decay, rpre_far, plin = fwd[n]
        bc, dstate, du0 = out[n]
        lanes = slice(n * 256, n * 256 + 256)
        carry = enter(got, n, True, q, count)
        for ks in range(4):
            cc = carry[ks : ks + 1]
            for h in range(PARTS):
                m = ks * PARTS + h
                st[m : m + 1, :] = cc
                cc = plin[m : m + 1, :] * cc + plin[16 + m : 17 + m, :]
        pp[...] = jnp.ones_like(pp)
        lb[...] = jnp.zeros_like(lb)
        ac[...] = jnp.zeros_like(ac)

        def tile(cand, rpre, u0, u1, ul, own0, own1, oth0, oth1, ho, ht):
            i = pl.program_id(0)
            for k, pair in enumerate(((own0, own1), (oth0, oth1))):
                for b, ref in enumerate(pair):
                    for m in range(8):
                        sq, h = divmod(m, PARTS)
                        scr[b, pl.ds(k * 128 + m, STEPS, stride=8), :] = ref[sq, h].astype(F32)
            cur = [st[0:8, :], st[8:16, :]]
            p = [pp[0:8, :], pp[8:16, :]]
            l = [lb[0:8, :], lb[8:16, :]]
            peep = [jnp.zeros((8, 256), F32)] * 2
            bias = [jnp.zeros((8, 256), F32)] * 2
            wr, wb = vr[:, lanes], br[:, lanes]
            for k, r0, row in pairs():
                at = slice(r0, r0 + 16)
                dec = decay[i, k, at, :]
                cd = cand[0, k, at, :]
                inj = (1.0 - dec) * cd
                befores, states = [], []
                for d, v in zip(halves(dec), halves(inj)):
                    befores.append(cur[k])
                    cur[k] = d * cur[k] + v
                    states.append(cur[k])
                before = jnp.concatenate(befores, axis=0)
                state = jnp.concatenate(states, axis=0)
                low = jnp.concatenate([u0[0, k, at, :], u1[0, k, at, :]], axis=1)
                uu[i, k, at, lanes] = low
                u = low.astype(F32) + ul[0, k, at, :].astype(F32)
                live = lim[row : row + 16, :] > i * STEPS
                sc = jnp.where(live, scl[row : row + 16, :], 0.0)
                gy = jnp.concatenate(
                    [scr[0, row : row + 16, :] * sc, scr[1, row : row + 16, :] * sc], axis=1
                )
                r = jax.nn.sigmoid(rpre[0, k, at, :] + wr * before + wb)
                gap = state - u
                hv = jnp.where(jnp.concatenate([live, live], axis=1), u + r * gap, 0.0).astype(BF)
                href = ht if k else ho
                href[0, 0, at, :] = hv[:, :BLK]
                href[0, 1, at, :] = hv[:, BLK:]
                ds = gy * r
                drl = ds * (1.0 - r) * gap
                sr = dec * ds + wr * drl
                dstate[i, k, at, :] = ds
                bc[i, k, at, :] = before - cd
                du0[i, k, at, :] = (gy - ds).astype(BF)
                dzr[i, k, at, lanes] = drl.astype(BF)
                for d, v in zip(halves(dec), halves(sr)):
                    l[k] = l[k] + p[k] * v
                    p[k] = p[k] * d
                for e, w in zip(halves(drl), befores):
                    peep[k] = peep[k] + e * w
                    bias[k] = bias[k] + e
            for k in range(2):
                st[k * 8 : k * 8 + 8, :] = cur[k]
                pp[k * 8 : k * 8 + 8, :] = p[k]
                lb[k * 8 : k * 8 + 8, :] = l[k]
            ac[0:8, :] += peep[0] + peep[1]
            ac[8:16, :] += bias[0] + bias[1]

        nat = cot_own.shape[:2]

        def unit(mm):
            return pl.BlockSpec(
                (1, 2, 128, BLK), lambda i: (i, 0, 0, (2 * n + mm) * 4 + 2 * c + a)
            )

        def tail():
            return pl.BlockSpec((1, 2, 128, 256), lambda i: (i, 0, 0, 2 * a + n))

        def nat_own(mm):
            return pl.BlockSpec(
                (*nat, STEPS, BLK), lambda i: (0, 0, i, (2 * n + mm) * 4 + 2 * c + a)
            )

        def nat_oth(mm):
            return pl.BlockSpec((*nat, STEPS, BLK), lambda i: (0, 0, i, (2 * n + mm) * 2 + a))

        one = pl.BlockSpec((1, 2, 128, 256), lambda i: (i, 0, 0, 0))
        hspec = pl.BlockSpec((1, 2, 128, BLK), lambda i: (2 * a + n, 0, i, 0))
        pltpu.emit_pipeline(
            tile,
            grid=(tiles,),
            in_specs=[one, one, unit(0), unit(1), tail(), nat_own(0), nat_own(1), nat_oth(0), nat_oth(1)],
            out_specs=[hspec, hspec],
        )(cand_far, rpre_far, ub, ub, ulo, cot_own, cot_own, cot_oth, cot_oth, hown, hoth)
        acc[n] = ac[...]
        lbs[n] = lb[...]
        for k in range(2):
            p, l = pp[k * 8 : k * 8 + 8, :], lb[k * 8 : k * 8 + 8, :]
            for sq, (tp, tl) in enumerate(fold_streams(p, l, False)):
                ks = k * 2 + sq
                summ[n, ks : ks + 1, :] = tp
                summ[n, 4 + ks : 5 + ks, :] = tl


def states(a, count, ids, deps, fwd, ub, ulo, cot_own, cot_oth, lim, scl, vr, br, got, held):
    tiles = ub.shape[0]
    rows = tiles * 128
    one = (tiles, 2, 128, 256)
    two = (tiles, 2, 128, 512)
    chan = slice(a * 512, a * 512 + 512)
    args, in_specs = [], []
    for f in fwd:
        args += far_in(f[0]) + near_in(f[1]) + far_in(f[2]) + [f[3]]
        in_specs += [ANY, NEAR, ANY, NEAR]
    args += far_in(ub, ulo, cot_own, cot_oth) + [lim, scl, vr[:, chan], br[:, chan], got]
    in_specs += [ANY] * 4 + [NEAR] * 5
    aliases = {}
    if held:
        aliases = {len(args): 0, len(args) + 1: 1}
        args += far_in(*held)
        in_specs += [ANY] * 2
    small = near((2, 16, 256), F32)
    return call_flat(
        functools.partial(state_kernel, a, count, bool(held)), f"states_{a}", ids, deps, args,
        in_specs,
        [far((4, 2, rows, BLK), BF)] * 2
        + [near(one, F32), near(one, F32), near(one, BF)] * 2
        + [near(two, BF)] * 2
        + [small, near((2, 8, 256), F32), small],
        10, cost(rows * 1024 * 60, rows * 1024 * 10, rows * 1024 * 2),
        scratch=[pltpu.VMEM((16, 256), F32)] * 4 + [pltpu.VMEM((2, 264, BLK), F32)],
        out_specs=[ANY] * 2 + [NEAR] * 11,
        aliases=aliases,
    )


def adjoint_kernel(count, ids, *refs):
    ins = (refs[0:5], refs[5:10])
    dzr, uu, vf, vr, lbs, got, du, dzc, dzf, acc, adj = refs[10:]
    tiles = du.shape[0]
    q = ids[0]
    for n in range(2):
        decay, bc, dstate, du0, plin = ins[n]
        lanes = slice(n * 256, n * 256 + 256)
        wf, wr = vf[:, lanes], vr[:, lanes]
        after = enter(got, n, False, q, count)
        for ks in range(4):
            cc = after[ks : ks + 1]
            for h in range(PARTS - 1, -1, -1):
                m = ks * PARTS + h
                adj[m : m + 1, :] = cc
                cc = lbs[n, m : m + 1, :] + plin[m : m + 1, :] * cc

        def tile(step, state):
            i = tiles - 1 - step
            cur, peep, bias = [state[0], state[1]], state[2], state[3]
            for k, r0, _ in reversed(list(pairs())):
                at = slice(r0, r0 + 16)
                dec = decay[i, k, at, :]
                ds = dstate[i, k, at, :]
                sr = dec * ds + wr * dzr[i, k, at, lanes].astype(F32)
                late = ds[8:] + cur[k]
                cur[k] = dec[8:] * cur[k] + sr[8:]
                early = ds[:8] + cur[k]
                cur[k] = dec[:8] * cur[k] + sr[:8]
                dcand = jnp.concatenate([early, late], axis=0) * (1.0 - dec)
                dfl = dcand * bc[i, k, at, :] * dec
                dzc[i, k, at, lanes] = dcand.astype(BF)
                dzf[i, k, at, lanes] = dfl.astype(BF)
                du[i, k, at, lanes] = (du0[i, k, at, :].astype(F32) + dfl * wf).astype(BF)
                w = dfl * uu[i, k, at, lanes].astype(F32)
                peep = peep + (w[:8] + w[8:])
                bias = bias + (dfl[:8] + dfl[8:])
            return cur[0], cur[1], peep, bias

        zero = jnp.zeros((8, 256), F32)
        end = lax.fori_loop(0, tiles, tile, (adj[0:8, :], adj[8:16, :], zero, zero))
        acc[n, 0:8, :] = end[2]
        acc[n, 8:16, :] = end[3]


def adjoints(a, count, ids, deps, fwd, mid, dzr, uu, vf, vr, lbs, got):
    tiles = uu.shape[0]
    rows = tiles * 128
    shape = (tiles, 2, 128, 512)
    args = []
    for f, m in zip(fwd, mid):
        args += near_in(f[1], *m) + [f[3]]
    chan = slice(a * 512, a * 512 + 512)
    args += near_in(dzr, uu) + [vf[:, chan], vr[:, chan], lbs, got]
    return call_flat(
        functools.partial(adjoint_kernel, count), f"adjoints_{a}", ids, deps, args,
        [NEAR] * len(args),
        [near(shape, BF)] * 3 + [near((2, 16, 256), F32)],
        6, cost(rows * 1024 * 20, rows * 1024 * 4), scratch=[pltpu.VMEM((16, 256), F32)],
    )


def wgrad_kernel(which, nz, n_kept, ids, ubt, dzc, dzf, dzr, *rest):
    kept, rest = rest[: max(n_kept - 3, 0)], rest[max(n_kept - 3, 0) :]
    own, xp, yp, da, db = rest[:5]
    scr, sems = rest[5 + n_kept :]
    copies = [
        pltpu.make_async_copy(src, dst, sems.at[n])
        for n, (src, dst) in enumerate(zip((dzc, dzf, dzr, *kept), rest[5 : 5 + n_kept]))
    ]
    for copy in copies:
        copy.start()
    q, c = ids[0], ids[2]
    rh = 1 - c if which == "other" else c
    half = scr.shape[0]
    rows = ubt.shape[1]

    def tile(lhs):
        i = pl.program_id(0)
        for g, dz in enumerate((dzc, dzf, dzr)):
            rhs = dz[...].reshape(rows, 512)
            scr[:, g * 512 : (g + 1) * 512] = jnp.dot(
                lhs[...], rhs, preferred_element_type=F32
            ).astype(BF)

        def block(r, j):
            return scr[:, pl.ds(pl.multiple_of(((q ^ r) * 3 + j) * BLK, BLK), BLK)]

        at = pl.ds(pl.multiple_of(i * half, half), half)
        for j in range(3):
            own[j, at, :] = block(0, j)
            xp[j, at, :] = block(1, j)
            yp[j, at, :] = block(2, j)

        @pl.when(i < nz // 2)
        def _():
            for j in range(3):
                da[j, at, :] = block(3, j)

        @pl.when(i >= nz // 2)
        def _():
            back = pl.ds(pl.multiple_of((i - nz // 2) * half, half), half)
            for j in range(3):
                db[j, back, :] = block(3, j)

    pltpu.emit_pipeline(
        tile, grid=(nz,), in_specs=[pl.BlockSpec((half, rows), lambda i: (2 * i + rh, 0))]
    )(ubt)
    for copy in copies:
        copy.wait()


def weight_grad_part(which, nz, ids, deps, ubt, dz, keep=()):
    width, rows = ubt.shape
    half = width // nz // 2
    kept = (*dz, *keep) if keep else ()
    return call_flat(
        functools.partial(wgrad_kernel, which, nz, len(kept)), "weight_grad_part", ids, deps,
        [*far_in(ubt), *near_in(*dz, *keep)], [ANY] + [NEAR] * (3 + len(keep)),
        [sds((3, nz * half, BLK), BF)] * 3
        + [sds((3, nz * half // 2, BLK), BF)] * 2
        + [far(v.shape, v.dtype) for v in kept],
        10, cost(2 * rows * nz * half * 1536, rows * width + width * 1536),
        scratch=[pltpu.VMEM((half, 1536), BF), pltpu.SemaphoreType.DMA((4,))],
        out_specs=[NEAR] * 5 + [ANY] * len(kept),
    )


def relay_kernel(ids, xp, yp, ra, rb, s1, s2):
    half = ra.shape[1]
    s1[:, :half, :] = xp[:, :half, :]
    s1[:, half:, :] = (xp[:, half:, :].astype(F32) + rb[...].astype(F32)).astype(BF)
    s2[:, :half, :] = (yp[:, :half, :].astype(F32) + ra[...].astype(F32)).astype(BF)
    s2[:, half:, :] = yp[:, half:, :]


def relay_sums(ids, deps, xp, yp, ra, rb):
    rows = xp.shape[1]
    return call_flat(
        relay_kernel, "relay_sums", ids, deps, [xp, yp, ra, rb], [NEAR] * 4,
        [sds(xp.shape, BF)] * 2, 16, cost(rows * 768, rows * 384 * 10),
    )


def plane_sum_kernel(nz, ids, own, r1, r2, *outs):
    rows = outs[0].shape[1]
    for k, out in enumerate(outs):
        start = lax.rem(ids[1] + k, nz) * rows
        at = pl.ds(pl.multiple_of(start, rows), rows)
        tot = own[:, at, :].astype(F32) + r1[:, at, :].astype(F32) + r2[:, at, :].astype(F32)
        out[...] = tot.astype(out.dtype)


def plane_sums(nz, ids, deps, own, r1, r2):
    rows = own.shape[1] // nz
    return call_flat(
        functools.partial(plane_sum_kernel, nz), "plane_sums", ids, deps, [own, r1, r2], [NEAR] * 3,
        [sds((3, rows, BLK), F32)] + [sds((3, rows, BLK), BF)] * (nz - 1), 16,
        cost(rows * 768 * nz, rows * 384 * 8 * nz),
    )


def fold_kernel(sets, d, ids, *refs):
    n = sum(len(g) for g in sets) if sets else 2
    srcs, outs = refs[:n], refs[n:]
    if sets:
        groups, at = [], 0
        for g in sets:
            groups.append(srcs[at : at + len(g)])
            at += len(g)
    else:
        groups = [[ref.at[g] for ref in srcs] for g in range(srcs[0].shape[0])]
    half = groups[0][0].shape[1] // 2
    bit = lax.rem(lax.div(ids[1], d), 2) if d else 0
    for g, parts in enumerate(groups):
        spots = ((outs[0], bit), (outs[1], 1 - bit)) if d else ((outs[g], None),)
        for out, where in spots:
            rows = slice(None) if where is None else pl.ds(pl.multiple_of(where * half, half), half)
            total = parts[0][:, rows, :].astype(F32)
            for part in parts[1:]:
                total = total + part[:, rows, :].astype(F32)
            if d:
                out[g] = total.astype(out.dtype)
            else:
                out[...] = total


def fold_z(d, ids, deps, sets):
    stacked = not isinstance(sets[0], (list, tuple))
    args = list(sets) if stacked else [v for g in sets for v in g]
    count = sets[0].shape[0] if stacked else len(sets)
    _, rows, _ = args[0].shape[-3:]
    if d:
        shape = (count, 3, rows // 2, BLK)
        out_shape = [sds(shape, F32), sds(shape, BF)]
    else:
        out_shape = [sds((3, rows, BLK), F32)] * count
    return call_flat(
        functools.partial(fold_kernel, None if stacked else [tuple(g) for g in sets], d), "fold_z",
        ids, deps, args, [NEAR] * len(args), out_shape, 8,
        cost(rows * 768 * count, rows * 384 * 10 * count),
    )


DIMS = (((1,), (1,)), ((), ()))
TILE_N = 512


def unit_kernel(k, ids, *refs):
    first, second, ws = refs[0:4], refs[4:8], refs[8:12]
    far_out, out, lhs, e0, wbuf, sems, wsems, osems = refs[13 if k == 0 else 12 :]
    c = ids[2]
    rows = out.shape[0]
    tiles = ws[0].shape[0] // TILE_N

    def fetch(m):
        slot, lane, copies = m % 2, 0, []
        for n, w in enumerate(ws):
            cols = w.shape[1]
            dst = wbuf.at[slot, :, lane : lane + cols]
            src = w.at[m * TILE_N : (m + 1) * TILE_N, :]
            copies.append(pltpu.make_async_copy(src, dst, wsems.at[slot, n]))
            lane += cols
        return copies

    copies = [(first[3].at[:, k], e0)]
    for mp in range(2):
        for g, ref in enumerate(first[:3]):
            dst = mp * 768 + g * 256
            src = ref.at[:, k, :, mp * 256 : (mp + 1) * 256]
            copies.append((src, lhs.at[:, :, dst : dst + 256]))
    copies = [pltpu.make_async_copy(a, b, sems.at[n]) for n, (a, b) in enumerate(copies)]
    for copy in copies + fetch(0):
        copy.start()
    for mp in range(2):
        for g, ref in enumerate(second[:3]):
            dst = 1536 + mp * 768 + g * 256
            lhs[:, :, dst : dst + 256] = ref[:, k, :, mp * 256 : (mp + 1) * 256]
    for copy in copies:
        copy.wait()
    moved = []
    for m in range(tiles):
        if m + 1 < tiles:
            for copy in fetch(m + 1):
                copy.start()
        for copy in fetch(m):
            copy.wait()
        lo = m * TILE_N
        left = lhs[...].reshape(rows, 3072)
        acc = lax.dot_general(left, wbuf[m % 2], DIMS, preferred_element_type=F32)
        out[:, lo : lo + TILE_N] = acc.astype(out.dtype)
        cols = slice(m * BLK, (m + 1) * BLK)
        for a, val in enumerate((e0[:, :, cols], second[3][:, k, :, cols])):
            lane = pl.ds(pl.multiple_of(lo + a * BLK + c * 256, BLK), BLK)
            total = out[:, lane].astype(F32) + val.reshape(rows, BLK).astype(F32)
            out[:, lane] = total.astype(out.dtype)
        slot = 1 - c if k else c
        done = pltpu.make_async_copy(
            out.at[:, lo : lo + TILE_N], far_out.at[slot, :, lo : lo + TILE_N], osems.at[m]
        )
        done.start()
        moved.append(done)
    for done in moved:
        done.wait()


def unit_grads(k, ids, deps, first, second, ws, held):
    tiles = first[0].shape[0]
    rows, width = tiles * 128, ws[0].shape[0]
    args = [*far_in(*first), *near_in(*second), *far_in(*ws)]
    return call_flat(
        functools.partial(unit_kernel, k), f"unit_grads_{k}", ids, deps, args + far_in(*held),
        [ANY] * 4 + [NEAR] * 4 + [ANY] * (4 + len(held)),
        far((2, rows, width), BF), 24, cost(2 * rows * width * 3072, width * 3072 * 2),
        scratch=[
            pltpu.VMEM((rows, width), BF),
            pltpu.VMEM((tiles, 128, 3072), BF),
            pltpu.VMEM((tiles, 128, 512), BF),
            pltpu.VMEM((2, TILE_N, 3072), BF),
            pltpu.SemaphoreType.DMA((7,)),
            pltpu.SemaphoreType.DMA((2, 4)),
            pltpu.SemaphoreType.DMA((width // TILE_N,)),
        ],
        out_specs=ANY, aliases={len(args): 0} if held else {},
    )


def norm_grad_kernel(ids, du2, tok, cot, lim, scl, gain, *rest):
    accb, accc = rest[:2], rest[2:4]
    out, sums, ga, ba, scr = rest[4:]
    c = ids[2]
    ga[...] = jnp.zeros_like(ga)
    ba[...] = jnp.zeros_like(ba)

    def tile(dur, tokr, cotr, outr):
        i = pl.program_id(0)
        for j in range(scr.shape[0]):
            lanes = slice(j * BLK, (j + 1) * BLK)
            scr[j, 0:128, :] = dur[0, :, lanes].astype(F32) + dur[1, :, lanes].astype(F32)
        step = lax.broadcasted_iota(jnp.int32, (STEPS, 1), 0) + i * STEPS
        gsum = jnp.zeros(ga.shape, F32)
        bsum = jnp.zeros(ba.shape, F32)
        for st in range(8):
            sq, h = divmod(st, PARTS)
            x16 = tokr[sq, h].astype(F32)
            c16 = cotr[sq, h].astype(F32)
            for part in range(2):
                cut = slice(part * 8, part * 8 + 8)
                du = jnp.concatenate(
                    [scr[j, pl.ds(st + part * 64, 8, stride=8), :] for j in range(scr.shape[0])],
                    axis=1,
                )
                normed, rstd = norm_of(x16[cut])
                dn = du * gain[...]
                m1 = jnp.mean(dn, axis=-1, keepdims=True)
                m2 = jnp.mean(dn * normed, axis=-1, keepdims=True)
                gy = jnp.where(step[cut] < lim[st], c16[cut] * scl[0], 0.0)
                outr[sq, h, cut, :] = rstd * (dn - m1 - normed * m2) + gy
                gsum = gsum + du * normed
                bsum = bsum + du
        ga[...] += gsum
        ba[...] += bsum

    seqs, parts, steps, width = tok.shape
    nat = pl.BlockSpec((seqs, parts, STEPS, width), lambda i: (0, 0, i, 0))
    pltpu.emit_pipeline(
        tile,
        grid=(steps // STEPS,),
        in_specs=[pl.BlockSpec((2, 128, width), lambda i: (0, i, 0)), nat, nat],
        out_specs=[nat],
    )(du2, tok, cot, out)
    sums[...] = jnp.zeros_like(sums)
    sums[4:5, :] = jnp.sum(ga[...], axis=0, keepdims=True)
    sums[5:6, :] = jnp.sum(ba[...], axis=0, keepdims=True)
    for s in range(4):
        a, mp = divmod(s, 2)
        rows = (
            accc[a][mp, 0:8, :],
            accb[a][mp, 0:8, :],
            accc[a][mp, 8:16, :],
            accb[a][mp, 8:16, :],
        )
        for j, val in enumerate(rows):
            val = jnp.sum(val, axis=0, keepdims=True)
            for mm in range(2):
                lane = pl.ds(core_lane(a, 2 * mp + mm, c), BLK)
                sums[j : j + 1, lane] = val[:, mm * BLK : (mm + 1) * BLK]


def norm_grads(ids, deps, du2, tok, cot, lim8, scale, gain, accb, accc):
    _, rows, width = du2.shape
    n = rows * width
    return call_flat(
        norm_grad_kernel, "norm_grads", ids, deps,
        [*far_in(du2, tok, cot), lim8, scale, gain, *accb, *accc],
        [ANY] * 3 + [SMEM] * 2 + [NEAR] * 5,
        [far(tok.shape, F32), sds((8, width), F32)], 14, cost(n * 20, n * 8),
        scratch=[
            pltpu.VMEM((8, width), F32),
            pltpu.VMEM((8, width), F32),
            pltpu.VMEM((width // BLK, 136, BLK), F32),
        ],
        out_specs=[ANY, NEAR],
    )


def activation_kernel(ids, tok, hown, hrcv, out, scr):
    c = ids[2]
    for s in range(4):
        a, mp = divmod(s, 2)
        for mm in range(2):
            for n, (ref, core) in enumerate(((hown, c), (hrcv, 1 - c))):
                scr[n, 0:128, :] = ref[s, mm].astype(F32)
                lane = pl.ds(core_lane(a, 2 * mp + mm, core), BLK)
                for st in range(8):
                    sq, h = divmod(st, PARTS)
                    val = scr[n, pl.ds(st, STEPS, stride=8), :]
                    out[sq, h, :, lane] = tok[sq, h, :, lane].astype(F32) + val


def activations_of(ids, deps, tok, hown, hrcv):
    seqs, parts, steps, width = tok.shape
    tiles = steps // STEPS
    nat = pl.BlockSpec((seqs, parts, STEPS, width), lambda i, ids: (0, 0, i, 0))
    hspec = pl.BlockSpec((4, 2, 128, BLK), lambda i, ids: (0, 0, i, 0))
    n = seqs * parts * steps * width
    return call(
        activation_kernel, "activations_of", (tiles,), ids, deps, far_in(tok, hown, hrcv),
        [nat, hspec, hspec], nat, far(tok.shape, F32), 16, cost(n, n * 8),
        scratch=[pltpu.VMEM((2, 136, BLK), F32)],
    )


def assemble_kernel(counts, ids, *refs):
    out = refs[-1]
    c = ids[2]
    start = 0
    for b, n in enumerate(counts):
        group = refs[start : start + n]
        start += n
        a, core = b % 2, c if b < 2 else 1 - c
        for j in range(3):
            total = group[0][j]
            for ref in group[1:]:
                total = total + ref[j].astype(F32)
            lane = pl.multiple_of(j * 512 + a * BLK + core * 256, BLK)
            out[:, pl.ds(lane, BLK)] = total


def assemble(ids, deps, groups):
    rows = groups[0][0].shape[1]
    counts = [len(g) for g in groups]
    args = [ref for group in groups for ref in group]
    return call_flat(
        functools.partial(assemble_kernel, counts), "assemble", ids, deps, args,
        [NEAR] * len(args), sds((rows, 1536), F32), 16, cost(0, rows * 1536 * 8),
    )


def local(
    nseq,
    ndp,
    tokens,
    cotangent,
    weight,
    forget_peep,
    reset_peep,
    forget_bias,
    reset_bias,
    norm_gain,
    norm_bias,
    lengths,
):
    axes = ("seq", "dp")
    nz = ndp // 2
    seqs, span, width = tokens.shape
    sub = span // PARTS
    q = lax.axis_index("seq").astype(jnp.int32)
    dp = lax.axis_index("dp").astype(jnp.int32)
    z, c = dp // 2, dp % 2
    ids = jnp.stack([q, z, c])

    def table(move):
        pairs = []
        for qq in range(nseq):
            for zz in range(nz):
                for cc in range(2):
                    to = move(qq, zz, cc)
                    if to is not None:
                        pairs.append((qq * ndp + zz * 2 + cc, to[0] * ndp + to[1] * 2 + to[2]))
        return pairs

    def send(value, move):
        return lax.ppermute(value, axes, table(move))

    def to_core(qq, zz, cc):
        return (qq, zz, 1 - cc)

    def to_x(qq, zz, cc):
        return (qq ^ 1, zz, cc)

    def to_y(qq, zz, cc):
        return (qq ^ 2, zz, cc)

    def shift_z(k):
        return lambda qq, zz, cc: (qq, (zz + k) % nz, cc)

    def shift_zc(k):
        return lambda qq, zz, cc: (qq, (zz + k) % nz, 1 - cc)

    def shift_q(k):
        return lambda qq, zz, cc: (qq + k, zz, cc) if 0 <= qq + k < nseq else None

    mine, theirs = split_weight(ids, weight)
    recv = send(theirs, to_core)
    nat = (seqs, PARTS, sub, width)
    tok4 = tokens.reshape(nat)
    cot4 = cotangent.reshape(nat)
    tok_oth = send(tokens, to_core).reshape(nat)
    len_oth = send(lengths, to_core)

    lens = jnp.stack([lengths, len_oth])
    counts = jnp.sum(lens, axis=1).astype(F32)
    scale = (seqs * span * nseq) / counts
    lim16 = (
        lens[:, :, None] - q * span - sub * jnp.arange(PARTS, dtype=jnp.int32)[None, None, :]
    ).reshape(2, 8)
    spread_rows = lambda v: jnp.broadcast_to(v, (2, STEPS, 8, BLK)).reshape(256, BLK)
    step_in_tile = jnp.arange(STEPS, dtype=jnp.int32)[None, :, None, None]
    lim = spread_rows(lim16[:, None, :, None] - step_in_tile)
    scl = spread_rows(scale[:, None, None, None])

    lim8, scale1 = lim16[0], scale[:1]

    def by_core(vec):
        v = lax.dynamic_slice_in_dim(vec.reshape(4, 4, BLK), 2 * c, 2, 1)
        return v.transpose(1, 0, 2).reshape(1, width // 2)

    vf, vr, bfor, brst = (by_core(v) for v in (forget_peep, reset_peep, forget_bias, reset_bias))
    gain, bias = norm_gain.reshape(1, width), norm_bias.reshape(1, width)

    tail = [mine]

    def run(kernel, *head, rest=(), token=-1, after=(), big=False):
        out = kernel(*head, ids, (tail[0], *after), *rest)
        tail[0] = out[token] if isinstance(out, (list, tuple)) else out
        if big:
            (tail[0],) = far_in(tail[0])
        return out

    groups = [[cc + 2 * zz for zz in range(nz)] for cc in range(2)]

    def along_z(piece):
        if nz <= 4:
            return [send(piece, shift_z(-k)) for k in range(1, nz)]
        got = lax.all_gather(piece, "dp", axis=0, tiled=True, axis_index_groups=groups)
        n = got.shape[0] // nz
        twice = jnp.concatenate([got, got], axis=0)
        return [lax.dynamic_slice_in_dim(twice, (z + 1) * n, n * (nz - 1), 0)]

    def gather_1(s, zs, after=()):
        rel = run(plane_pieces, s, rest=(zs,), after=after)
        return rel, send(rel, to_x), send(rel, to_y)

    def gather_2(s, got, after=()):
        rel, gx, gy = got
        tox, toy = run(cross_pieces, s, rest=(gx, gy), after=after)
        return rel, gx, gy, send(tox, to_x), send(toy, to_y)

    def spread(both):
        return lax.all_gather(both, "seq")

    def run_project(s, weights, before=None, after=()):
        rest = (ub, ulo, weights, lim, vf, bfor, before)
        return run(project, s, nz, rest=rest, token=4, after=after)

    def run_states(a, fwd, got, held, after=()):
        rest = (fwd, ub, ulo, cot4, cot_oth, lim, scl, vr, brst, got, held)
        out = run(states, a, nseq, rest=rest, after=after)
        return {
            "h": out[:2], "mid": (out[2:5], out[5:8]), "dzr": out[8], "u": out[9],
            "lbs": out[10], "summ": out[11], "acc": out[12],
        }

    def run_adjoints(a, fwd, m, got, after=()):
        rest = (fwd, m["mid"], m["dzr"], m["u"], vf, vr, m["lbs"], got)
        du, dzc, dzf, acc = run(adjoints, a, nseq, rest=rest, after=after)
        return {"du": du, "dz": (dzc, dzf, m["dzr"]), "acc": acc}

    def sum_1(which, dz, keep=(), after=(), hold=False):
        own, xp, yp, da, db, *kept = run(
            weight_grad_part, which, nz, rest=(ubt, dz, keep), token=3, after=after
        )
        if hold:
            da, db = run(gate, rest=((da, db),))
        return (own, xp, yp, send(da, to_x), send(db, to_y)), kept

    def sum_2(got, after=()):
        own, xp, yp, ra, rb = got
        s1, s2 = run(relay_sums, rest=(xp, yp, ra, rb), after=after)
        return own, send(s1, to_x), send(s2, to_y)

    def fold(sets, d):
        kept, out = run(fold_z, d, rest=(sets,))
        return kept, send(out, lambda qq, zz, cc: (qq, zz ^ d, cc))

    def sum_3_now(got):
        if nz > 4:
            got, d = [got], nz // 2
            while d:
                got, d = fold(got, d), d // 2
            return run(fold_z, 0, rest=(got,))
        parts = list(run(plane_sums, nz, rest=got))
        return parts[:1] + [send(parts[k], shift_z(k)) for k in range(1, nz)]

    def fold_rest(got):
        d = nz // 4
        while d:
            got, d = fold(got, d), d // 2
        return got

    high, p0, p1 = run(quarter_of, rest=(mine, recv), after=(tok_oth, len_oth))
    z0 = along_z(p0)
    cot_cols = run(other_columns, rest=(cotangent,), big=True)
    cot_oth = send(cot_cols, to_core).reshape(seqs, PARTS, sub, width // 2)
    z1 = along_z(p1)
    ub, ubt, ulo = run(
        norm_tokens, rest=(tok4, tok_oth, gain, bias), big=True, after=(lim8, scale1, lim, scl, cot_oth)
    )
    g0 = gather_1(0, z0)
    g0 = gather_2(0, g0)
    g1 = gather_1(1, z1)
    z23 = along_z(run(hand_on, rest=(high,)))
    f0 = run_project(0, (mine, recv, *g0))
    g1 = gather_2(1, g1)
    f1 = run_project(1, (mine, recv, *g1), f0[4])
    got = spread(f1[4])
    g2 = gather_1(2, z23, after=(got,))
    m0 = run_states(0, (f0, f1), got, ())
    got = spread(m0["summ"])
    g2 = gather_2(2, g2, after=(got,))
    d0 = run_adjoints(0, (f0, f1), m0, got)
    s0, _ = sum_1("other", d0["dz"])
    g3 = gather_1(3, z23, after=g2[3:])
    f2 = run_project(2, (mine, recv, *g2))
    g3 = gather_2(3, g3)
    s0 = sum_2(s0)
    s1, first = sum_1("own", d0["dz"], (d0["du"],))
    f3 = run_project(3, (mine, recv, *g3), f2[4])
    got = spread(f3[4])
    s1 = sum_2(s1, after=(got,))
    m1 = run_states(1, (f2, f3), got, m0["h"], after=s0[1:])
    s01 = fold([s0, s1], nz // 2)
    hrcv = send(run(gate, rest=(m1["h"][1:], "far"))[0], to_core)
    got = spread(run(hand_on, rest=(m1["summ"],)))
    d1 = run_adjoints(1, (f2, f3), m1, got)
    s2, _ = sum_1("other", d1["dz"])
    s3, _ = sum_1("own", d1["dz"], after=(hrcv,))
    s2 = sum_2(s2)
    s01 = fold_rest(s01)
    second = (*d1["dz"], d1["du"])
    ws = (f0[5], f1[5], f2[5], f3[5])
    du2 = run(unit_grads, 1, rest=(first, second, ws, ()), big=True)
    s3 = sum_2(s3)
    du2 = run(unit_grads, 0, rest=(first, second, ws, (du2,)), big=True)
    s2 = fold([s2], nz // 2)
    s0, s1 = run(fold_z, 0, rest=(s01,))
    s0 = send(s0, to_core)
    s3 = sum_3_now(s3)
    cores = [[2 * zz, 2 * zz + 1] for zz in range(nz)]
    du2 = lax.all_to_all(du2, "dp", 0, 0, axis_index_groups=cores, tiled=True)
    activations = run(activations_of, rest=(tok4, m1["h"][0], hrcv), big=True)
    input_grad, sums = run(
        norm_grads,
        rest=(
            du2, tok4, cot4, lim8, scale1, gain, (m0["acc"], m1["acc"]), (d0["acc"], d1["acc"])
        ),
        after=(s0,),
    )
    s2 = fold_rest(s2)
    s3 = run(fold_z, 0, rest=([s3],))
    if nz <= 4:
        sums = run(add_up, rest=(sums, *[send(sums, shift_z(k)) for k in range(1, nz)]))
    else:
        for b in range((nz - 1).bit_length()):
            hop = lambda qq, zz, cc, b=1 << b: (qq, zz ^ b, cc)
            sums = run(add_up, rest=(sums, send(sums, hop)))
    s2 = send(run(fold_z, 0, rest=(s2,))[0], to_core)
    moved = [send(sums, lambda qq, zz, cc, b=b: (qq ^ b, zz, cc)) for b in range(1, nseq)]
    sums = run(add_up, rest=(sums, *moved))
    moved = send(sums, to_core)
    sums = run(add_up, rest=(sums, moved))
    weight_grad = run(assemble, rest=(([s1], s3, [s0], [s2]),))
    shape = tokens.shape
    return (
        activations.reshape(shape),
        input_grad.reshape(shape),
        weight_grad,
        sums[0],
        sums[1],
        sums[2],
        sums[3],
        sums[4],
        sums[5],
    )


def solution(mesh):
    whole = P("dp", "seq", None)
    in_specs = (whole, whole, P("dp", None)) + (P(),) * 6 + (P("dp"),)
    out_specs = (whole, whole, P("dp", "seq")) + (P(),) * 6
    step = functools.partial(local, mesh.shape["seq"], mesh.shape["dp"])
    return jax.shard_map(step, mesh=mesh, in_specs=in_specs, out_specs=out_specs, check_vma=False)
```
